512 devices in a mesh: ctx: 64 (over z, x), ch: 8 (over y, core).
Axes of the slice: x: 4, y: 4, z: 16, core: 2. Of those that a mesh axis runs over, the one named last changes fastest.
Arguments:
- stream: bfloat16 [8192, 4096], P('ctx', 'ch'), may hold values from -1200 to 1200
- norm_gain: float32 [4096], P('ch'), may hold values from 0.5 to 1.5
- short_filter: float32 [3, 3, 4096], P(None, None, 'ch'), may hold values from -3 to 3
- decay_rate: float32 [4096, 16], P('ch'), may hold values from 0 to 1, as said below
- residue: float32 [4096, 16], P('ch'), may hold values from -1 to 1
Outputs:
- mixed: bfloat16 [8192, 4096], P('ctx', 'ch')
The draws below stay inside these ranges and needn't reach their ends.
Inputs may be any that keep to these rules, and one draw needn't show every extreme that they name: `decay_rate`: decay per position of each mode, positive.
All inputs are finite; a program needn't handle non-finite values.
Results may differ from the reference program's by a relative error of at most 0.01155.
Values may be sent and summed in bfloat16 or wider, within the bound.
No kernel may reach another device: no remote copies, remote signals or barrier semaphores. Data moves between devices by JAX's collectives and lax.ppermute only.
A program may use at most 64 MiB of HBM per device.

```python
import math
import jax
import jax.numpy as jnp
from jax import lax

C = 4096
R_MODES = 16
TAPS = 3
TOKENS = 8192


def rate_table(key, slow_share):
    key = jax.random.fold_in(key, 11)
    pick = jax.random.uniform(jax.random.fold_in(key, 1), (C, R_MODES))
    slow_low = 0.2 * math.log(10.0) / TOKENS
    slow_high = math.log(10.0) / TOKENS
    slow_draw = jax.random.uniform(jax.random.fold_in(key, 2), (C, R_MODES))
    fast_draw = jax.random.uniform(jax.random.fold_in(key, 3), (C, R_MODES))
    slow = jnp.exp(math.log(slow_low) + slow_draw * (math.log(slow_high) - math.log(slow_low)))
    fast = jnp.exp(math.log(1.0 / 50.0) + fast_draw * (math.log(1.0 / 30.0) - math.log(1.0 / 50.0)))
    return jnp.where(pick < slow_share, slow, fast).astype(jnp.float32)


def draw_decay_rate(key, part):
    share = 0.5
    return rate_table(key, share)


def draw_residue(key, part):
    share = 0.5
    rates = rate_table(key, share)
    key = jax.random.fold_in(key, 5)
    base = jnp.clip(jax.random.normal(key, (C, R_MODES), jnp.float32), -5.0, 5.0)
    return (base * jnp.sqrt(2.0 * rates / R_MODES)).astype(jnp.float32)


def draw_stream(key, part):
    key = jax.random.fold_in(key, 7)
    trend = 3.0
    widest = 4.0
    base = jnp.clip(jax.random.normal(jax.random.fold_in(key, 1), (TOKENS, C), jnp.float32), -4.0, 4.0)
    row_scale = jnp.exp(jax.random.uniform(jax.random.fold_in(key, 2), (TOKENS, 1)) * math.log(10.0))
    col_draw = jax.random.uniform(jax.random.fold_in(key, 3), (1, C))
    channel = jnp.arange(C, dtype=jnp.float32)[None, :] / C
    col_scale = jnp.exp(col_draw * math.log(widest)) * jnp.exp(0.5 * math.log(trend) * channel)
    return (base * row_scale * col_scale).astype(jnp.bfloat16)


def levels(stream_key, extent, pieces, low, largest):
    factor_of = 1.0
    for axis_at, blocks in pieces:
        draws = jax.random.uniform(jax.random.fold_in(jax.random.fold_in(stream_key, 6), axis_at), (blocks,), jnp.float32, low / len(pieces), largest / len(pieces))
        factor_of = factor_of * jnp.repeat(jnp.exp(draws), extent[axis_at] // blocks).reshape((-1,) + (1,) * (len(extent) - 1 - axis_at))
    return factor_of


def centred(rng, extent, spread, bound, cuts=(), kind=jnp.bfloat16):
    drawn = spread * jax.random.normal(rng, extent, jnp.float32)
    if cuts:
        drawn = drawn * levels(rng, extent, cuts, -0.22, 0.18)
    return jnp.clip(drawn, -bound, bound).astype(kind)


def setup_inputs(seed: int = 0) -> dict:
    splits = jax.random.split(jax.random.key(seed), 6)
    return {
        "stream": draw_stream(jax.random.fold_in(splits[5], 71), 0),
        "norm_gain": jnp.clip(1.0 + 0.1 * jax.random.normal(splits[1], (C,), jnp.float32), 0.5, 1.5),
        "short_filter": centred(splits[2], (TAPS, 3, C), 0.6, 3.0, ((2, 8),), jnp.float32),
        "decay_rate": draw_decay_rate(jax.random.fold_in(splits[5], 71), 0),
        "residue": draw_residue(jax.random.fold_in(splits[5], 71), 0),
    }


def reference(stream, norm_gain, short_filter, decay_rate, residue):
    values = stream.astype(jnp.float32)
    mean_square = lax.optimization_barrier(jnp.mean(values * values, axis=1))
    normed = (values * lax.rsqrt(mean_square + 1e-05)[:, None] * norm_gain[None, :]).astype(jnp.bfloat16)
    padded = jnp.concatenate([jnp.zeros((TAPS - 1, C), jnp.bfloat16), normed], axis=0).astype(jnp.float32)
    roles = []
    for role in range(3):
        total = jnp.zeros((TOKENS, C), jnp.float32)
        for tap in range(TAPS):
            total = total + short_filter[tap, role][None, :] * padded[TAPS - 1 - tap:TAPS - 1 - tap + TOKENS]
        roles.append(total)
    query_held = roles[0].astype(jnp.bfloat16)
    product = (roles[1] * roles[2]).astype(jnp.bfloat16)
    block = min(128, C)
    count = C // block
    columns = product.astype(jnp.float32).T.reshape(count, block, TOKENS)
    rate_blocks = decay_rate.reshape(count, block, R_MODES)
    weight_blocks = residue.reshape(count, block, R_MODES)

    def conv_block(parts):
        segment, rate, weight = parts
        times = jnp.arange(TOKENS, dtype=jnp.float32)
        filt = lax.optimization_barrier(jnp.sum(weight[:, :, None] * jnp.exp(-rate[:, :, None] * times[None, None, :]), axis=1))
        spectrum = jnp.fft.rfft(segment, 2 * TOKENS) * jnp.fft.rfft(filt, 2 * TOKENS)
        return jnp.fft.irfft(spectrum, 2 * TOKENS)[:, :TOKENS].astype(jnp.float32)
    convolved = lax.map(conv_block, (columns, rate_blocks, weight_blocks))
    conv = convolved.reshape(C, TOKENS).T.astype(jnp.bfloat16)
    return (query_held.astype(jnp.float32) * conv.astype(jnp.float32)).astype(jnp.bfloat16)
```

```python
import jax
import jax.numpy as jnp
from jax import lax
from jax.experimental import pallas as pl
from jax.experimental.pallas import tpu as pltpu
from jax.sharding import PartitionSpec as P

EXACT = lax.Precision.HIGHEST
EPSILON = 1e-05
SUB = 8
LANES = 128
RIM = 16
NEAR = 8

F32 = jnp.float32
BF16 = jnp.bfloat16


def call(body, outs, *args, scratch=(), flops=0):
    shapes = [jax.ShapeDtypeStruct(s, d) for s, d in outs]
    moved = sum(a.size * a.dtype.itemsize for a in args)
    return pl.pallas_call(
        body,
        out_shape=shapes,
        in_specs=[pl.BlockSpec(memory_space=pltpu.VMEM)] * len(args),
        out_specs=[pl.BlockSpec(memory_space=pltpu.VMEM)] * len(shapes),
        scratch_shapes=list(scratch),
        compiler_params=pltpu.CompilerParams(vmem_limit_bytes=16 * 2**20),
        cost_estimate=pl.CostEstimate(flops=flops, bytes_accessed=moved, transcendentals=0),
    )(*args)


def square_sums(stream_ref, rim_ref, rate_ref, residue_ref, sums_ref, rate_out, residue_out):
    peers = sums_ref.shape[0]
    ones = jnp.ones((peers, stream_ref.shape[1]), F32)
    contract = (((1,), (1,)), ((), ()))

    def rows(ref):
        values = ref[...].astype(F32)
        return lax.dot_general(ones, values * values, contract, precision=EXACT, preferred_element_type=F32)

    count = stream_ref.shape[0]
    sums_ref[...] = jnp.zeros_like(sums_ref)
    sums_ref[:, :count] = rows(stream_ref)
    sums_ref[:, count : count + RIM] = rows(rim_ref)
    rate_out[...] = rate_ref[...].T
    residue_out[...] = residue_ref[...].T


def block_states(chan_total, sums_ref, stream_ref, rim_ref, gain_ref, taps_ref, rate_ref, query_ref, product_ref, states_ref, normed_ref):
    count, chans = stream_ref.shape
    peers = states_ref.shape[0]
    modes = rate_ref.shape[0]
    ones = jnp.ones((sums_ref.shape[0], chans), F32)

    def normalize(ref, sums):
        mean_square = lax.dot_general(sums, ones, (((0,), (0,)), ((), ())), precision=EXACT, preferred_element_type=F32) / chan_total
        values = ref[...].astype(F32) * lax.rsqrt(mean_square + EPSILON) * gain_ref[...]
        return values.astype(BF16).astype(F32)

    normed_ref[:RIM] = normalize(rim_ref, sums_ref[:, count : count + RIM])
    normed_ref[RIM:] = normalize(stream_ref, sums_ref[:, :count])
    shifted = [normed_ref[RIM - j : RIM - j + count] for j in range(3)]

    def feature(role):
        total = taps_ref[pl.ds(role, 1)] * shifted[0]
        total = total + taps_ref[pl.ds(3 + role, 1)] * shifted[1]
        return total + taps_ref[pl.ds(6 + role, 1)] * shifted[2]

    query_ref[...] = feature(0).astype(BF16)
    product_ref[...] = (feature(1) * feature(2)).astype(BF16).astype(F32)

    lag = (SUB - 1 - lax.broadcasted_iota(jnp.int32, (SUB, LANES), 0)).astype(F32)

    def one_lane(lane, carry):
        at = pl.ds(pl.multiple_of(lane * LANES, LANES), LANES)
        blocks = [product_ref[pl.ds(i * SUB, SUB), at] for i in range(count // SUB)]
        for mode in range(modes):
            rate = rate_ref[pl.ds(mode, 1), at]
            step = jnp.broadcast_to(jnp.exp(-SUB * rate), (SUB, LANES))
            total = blocks[0]
            for block in blocks[1:]:
                total = total * step + block
            total = jnp.sum(total * jnp.exp(-rate * lag), axis=0, keepdims=True)
            for peer in range(peers):
                states_ref[peer, pl.ds(mode, 1), at] = total
        return carry

    lax.fori_loop(0, chans // LANES, one_lane, 0)


def add_mode(totals, term, rate):
    step = jnp.broadcast_to(jnp.exp(-SUB * rate), term.shape)
    out = []
    for total in totals:
        out.append(total + term)
        term = term * step
    return out


def inner_conv(rate_ref, residue_ref, product_ref, local_ref, filter_ref):
    count, chans = product_ref.shape
    modes = rate_ref.shape[0]
    blocks = count // SUB
    row = lax.broadcasted_iota(jnp.int32, (SUB, LANES), 0)
    lead = row.astype(F32)

    def one_lane(lane, carry):
        at = pl.ds(pl.multiple_of(lane * LANES, LANES), LANES)

        zero = jnp.zeros((SUB, LANES), F32)
        totals = [zero] * blocks
        for mode in range(modes):
            rate = rate_ref[pl.ds(mode, 1), at]
            term = residue_ref[pl.ds(mode, 1), at] * jnp.exp(-rate * lead)
            totals = add_mode(totals, term, rate)
        for i in range(blocks):
            filter_ref[pl.ds(i * SUB, SUB), :] = totals[i]

        shifted = [product_ref[pl.ds(i * SUB, SUB), at] for i in range(blocks)]
        totals = [zero] * blocks
        for b in range(SUB):
            for a in range(blocks):
                weight = filter_ref[pl.ds(a * SUB + b, 1), :]
                for j in range(blocks - a):
                    totals[j + a] = totals[j + a] + weight * shifted[j]
            if b < SUB - 1:
                rolled = [pltpu.roll(s, 1, 0) for s in shifted]
                shifted = [jnp.where(row == 0, before, now) for before, now in zip([zero] + rolled[:-1], rolled)]
        for i in range(blocks):
            local_ref[pl.ds(i * SUB, SUB), at] = totals[i]
        return carry

    lax.fori_loop(0, chans // LANES, one_lane, 0)


def near_scan(block, got_ref, rate_ref, before_ref, totals_ref):
    place = lax.axis_index("ctx") % NEAR
    step = jnp.exp(-block * rate_ref[...])
    total = jnp.zeros_like(step)
    before = total
    for j in range(NEAR):
        before = jnp.where(place == j, total, before)
        total = total * step + got_ref[j]
    before_ref[...] = before
    for peer in range(totals_ref.shape[0]):
        totals_ref[peer] = total


def outer_conv(block, far, got_ref, before_ref, rate_ref, residue_ref, local_ref, query_ref, mixed_ref, state_ref):
    count, chans = local_ref.shape
    modes = rate_ref.shape[0]
    blocks = count // SUB
    index = lax.axis_index("ctx")
    place, group = index % NEAR, index // NEAR
    rates = rate_ref[...]
    step = jnp.exp(-(block * NEAR) * rates)
    total = jnp.zeros_like(rates)
    state = total
    for j in range(far):
        state = jnp.where(group == j, total, state)
        total = total * step + got_ref[j]
    state = state * jnp.exp(-rates * (block * place).astype(F32)) + before_ref[...]
    state_ref[...] = state * residue_ref[...]
    lead = (1 + lax.broadcasted_iota(jnp.int32, (SUB, LANES), 0)).astype(F32)

    def one_lane(lane, carry):
        at = pl.ds(pl.multiple_of(lane * LANES, LANES), LANES)

        totals = [local_ref[pl.ds(i * SUB, SUB), at] for i in range(blocks)]
        for mode in range(modes):
            rate = rate_ref[pl.ds(mode, 1), at]
            term = state_ref[pl.ds(mode, 1), at] * jnp.exp(-rate * lead)
            totals = add_mode(totals, term, rate)
        for i in range(0, blocks, 2):
            rows = pl.ds(i * SUB, 2 * SUB)
            conv = jnp.concatenate(totals[i : i + 2], axis=0).astype(BF16).astype(F32)
            mixed_ref[rows, at] = (query_ref[rows, at].astype(F32) * conv).astype(BF16)
        return carry

    lax.fori_loop(0, chans // LANES, one_lane, 0)


def gather(copies, axis, groups=None):
    return lax.all_to_all(copies, axis, 0, 0, tiled=True, axis_index_groups=groups)


def per_device(stream, norm_gain, short_filter, decay_rate, residue):
    count, chans = stream.shape
    modes = decay_rate.shape[1]
    peers = lax.axis_size("ch")
    ctx = lax.axis_size("ctx")
    far = ctx // NEAR
    near_groups = [[g * NEAR + m for m in range(NEAR)] for g in range(far)]
    far_groups = [[g * NEAR + m for g in range(far)] for m in range(NEAR)]

    rim = lax.ppermute(stream[count - RIM :], "ctx", [(i, i + 1) for i in range(ctx - 1)])
    sums, rates, weights = call(
        square_sums,
        [((peers, 2 * LANES), F32), ((modes, chans), F32), ((modes, chans), F32)],
        stream, rim, decay_rate, residue,
    )
    sums = gather(sums, "ch")
    query, product, states = call(
        lambda *refs: block_states(chans * peers, *refs),
        [((count, chans), BF16), ((count, chans), F32), ((NEAR, modes, chans), F32)],
        sums, stream, rim, norm_gain[None, :], short_filter.reshape(9, chans), rates,
        scratch=[pltpu.VMEM((RIM + count, chans), F32)],
    )
    states = gather(states, "ctx", near_groups)
    (local,) = call(
        inner_conv, [((count, chans), F32)], rates, weights, product,
        scratch=[pltpu.VMEM((count, LANES), F32)], flops=10**7,
    )
    before, totals = call(
        lambda *refs: near_scan(count, *refs),
        [((modes, chans), F32), ((far, modes, chans), F32)],
        states, rates,
    )
    totals = gather(totals, "ctx", far_groups)
    (mixed,) = call(
        lambda *refs: outer_conv(count, far, *refs),
        [((count, chans), BF16)],
        totals, before, rates, weights, local, query,
        scratch=[pltpu.VMEM((modes, chans), F32)],
    )
    return mixed


def solution(mesh):
    in_specs = (P("ctx", "ch"), P("ch"), P(None, None, "ch"), P("ch", None), P("ch", None))
    out_specs = P("ctx", "ch")
    return jax.shard_map(
        per_device, mesh=mesh, in_specs=in_specs, out_specs=out_specs, check_vma=False
    )
```

```python
import jax
import jax.numpy as jnp
from jax import lax
from jax.experimental import pallas as pl
from jax.experimental.pallas import tpu as pltpu
from jax.sharding import PartitionSpec as P

EXACT = lax.Precision.HIGHEST
EPSILON = 1e-05
SUB = 8
LANES = 128
RIM = 16
NEAR = 8

F32 = jnp.float32
BF16 = jnp.bfloat16


def call(body, outs, *args, scratch=(), flops=0):
    shapes = [jax.ShapeDtypeStruct(s, d) for s, d in outs]
    moved = sum(a.size * a.dtype.itemsize for a in args)
    return pl.pallas_call(
        body,
        out_shape=shapes,
        in_specs=[pl.BlockSpec(memory_space=pltpu.VMEM)] * len(args),
        out_specs=[pl.BlockSpec(memory_space=pltpu.VMEM)] * len(shapes),
        scratch_shapes=list(scratch),
        compiler_params=pltpu.CompilerParams(vmem_limit_bytes=16 * 2**20),
        cost_estimate=pl.CostEstimate(flops=flops, bytes_accessed=moved, transcendentals=0),
    )(*args)


def square_sums(stream_ref, rim_ref, *refs):
    sums_ref, held = refs[len(refs) // 2], refs[: len(refs) // 2]
    for ref, out in zip(held, refs[len(refs) // 2 + 1 :]):
        out[...] = ref[...]
    peers = sums_ref.shape[0]
    ones = jnp.ones((SUB, stream_ref.shape[1]), F32)
    contract = (((1,), (1,)), ((), ()))

    def rows(ref):
        values = ref[...].astype(F32)
        return lax.dot_general(ones, values * values, contract, precision=EXACT, preferred_element_type=F32)

    count = stream_ref.shape[0]
    sums_ref[...] = jnp.zeros_like(sums_ref)
    own, before = rows(stream_ref), rows(rim_ref)
    for peer in range(peers):
        sums_ref[peer, :, :count] = own[:1]
        sums_ref[peer, :, count : count + RIM] = before[:1]


def block_states(chan_total, sums_ref, stream_ref, rim_ref, gain_ref, taps_ref, rate_ref, query_ref, product_ref, states_ref, normed_ref):
    count, chans = stream_ref.shape
    peers = states_ref.shape[0]
    modes = rate_ref.shape[0]
    ones = jnp.ones((SUB, chans), F32) / SUB
    sums_all = sums_ref[0]
    for peer in range(1, sums_ref.shape[0]):
        sums_all = sums_all + sums_ref[peer]
    sums_all = jnp.broadcast_to(sums_all, (SUB, sums_all.shape[1]))

    def normalize(ref, sums):
        mean_square = lax.dot_general(sums, ones, (((0,), (0,)), ((), ())), precision=EXACT, preferred_element_type=F32) / chan_total
        values = ref[...].astype(F32) * lax.rsqrt(mean_square + EPSILON) * gain_ref[...]
        return values.astype(BF16).astype(F32)

    normed_ref[:RIM] = normalize(rim_ref, sums_all[:, count : count + RIM])
    normed_ref[RIM:] = normalize(stream_ref, sums_all[:, :count])
    shifted = [normed_ref[RIM - j : RIM - j + count] for j in range(3)]

    def feature(role):
        total = taps_ref[pl.ds(role, 1)] * shifted[0]
        total = total + taps_ref[pl.ds(3 + role, 1)] * shifted[1]
        return total + taps_ref[pl.ds(6 + role, 1)] * shifted[2]

    query_ref[...] = feature(0).astype(BF16)
    product_ref[...] = (feature(1) * feature(2)).astype(BF16).astype(F32)

    lag = (SUB - 1 - lax.broadcasted_iota(jnp.int32, (SUB, LANES), 0)).astype(F32)

    def one_lane(lane, carry):
        at = pl.ds(pl.multiple_of(lane * LANES, LANES), LANES)
        blocks = [product_ref[pl.ds(i * SUB, SUB), at] for i in range(count // SUB)]
        for mode in range(modes):
            rate = rate_ref[pl.ds(mode, 1), at]
            step = jnp.broadcast_to(jnp.exp(-SUB * rate), (SUB, LANES))
            total = blocks[0]
            for block in blocks[1:]:
                total = total * step + block
            total = jnp.sum(total * jnp.exp(-rate * lag), axis=0, keepdims=True)
            for peer in range(peers):
                states_ref[peer, pl.ds(mode, 1), at] = total
        return carry

    lax.fori_loop(0, chans // LANES, one_lane, 0)


def add_mode(totals, term, rate):
    step = jnp.broadcast_to(jnp.exp(-SUB * rate), term.shape)
    out = []
    for total in totals:
        out.append(total + term)
        term = term * step
    return out


def inner_conv(rate_ref, residue_ref, product_ref, local_ref, filter_ref):
    count, chans = product_ref.shape
    modes = rate_ref.shape[0]
    blocks = count // SUB
    row = lax.broadcasted_iota(jnp.int32, (SUB, LANES), 0)
    lead = row.astype(F32)

    def one_lane(lane, carry):
        at = pl.ds(pl.multiple_of(lane * LANES, LANES), LANES)

        zero = jnp.zeros((SUB, LANES), F32)
        totals = [zero] * blocks
        for mode in range(modes):
            rate = rate_ref[pl.ds(mode, 1), at]
            term = residue_ref[pl.ds(mode, 1), at] * jnp.exp(-rate * lead)
            totals = add_mode(totals, term, rate)
        for i in range(blocks):
            filter_ref[pl.ds(i * SUB, SUB), :] = totals[i]

        shifted = [product_ref[pl.ds(i * SUB, SUB), at] for i in range(blocks)]
        totals = [zero] * blocks
        for b in range(SUB):
            for a in range(blocks):
                weight = filter_ref[pl.ds(a * SUB + b, 1), :]
                for j in range(blocks - a):
                    totals[j + a] = totals[j + a] + weight * shifted[j]
            if b < SUB - 1:
                rolled = [pltpu.roll(s, 1, 0) for s in shifted]
                shifted = [jnp.where(row == 0, before, now) for before, now in zip([zero] + rolled[:-1], rolled)]
        for i in range(blocks):
            local_ref[pl.ds(i * SUB, SUB), at] = totals[i]
        return carry

    lax.fori_loop(0, chans // LANES, one_lane, 0)


def near_scan(block, got_ref, rate_ref, residue_ref, product_ref, before_ref, totals_ref, local_ref, filter_ref):
    place = lax.axis_index("ctx") % NEAR
    step = jnp.exp(-block * rate_ref[...])
    total = jnp.zeros_like(step)
    before = total
    for j in range(NEAR):
        before = jnp.where(place == j, total, before)
        total = total * step + got_ref[j]
    before_ref[...] = before
    for peer in range(totals_ref.shape[0]):
        totals_ref[peer] = total
    inner_conv(rate_ref, residue_ref, product_ref, local_ref, filter_ref)


def outer_conv(block, far, got_ref, before_ref, rate_ref, residue_ref, local_ref, query_ref, mixed_ref, state_ref):
    count, chans = local_ref.shape
    modes = rate_ref.shape[0]
    blocks = count // SUB
    index = lax.axis_index("ctx")
    place, group = index % NEAR, index // NEAR
    rates = rate_ref[...]
    step = jnp.exp(-(block * NEAR) * rates)
    total = jnp.zeros_like(rates)
    state = total
    for j in range(far):
        state = jnp.where(group == j, total, state)
        total = total * step + got_ref[j]
    state = state * jnp.exp(-rates * (block * place).astype(F32)) + before_ref[...]
    state_ref[...] = state * residue_ref[...]
    lead = (1 + lax.broadcasted_iota(jnp.int32, (SUB, LANES), 0)).astype(F32)

    def one_lane(lane, carry):
        at = pl.ds(pl.multiple_of(lane * LANES, LANES), LANES)

        totals = [local_ref[pl.ds(i * SUB, SUB), at] for i in range(blocks)]
        for mode in range(modes):
            rate = rate_ref[pl.ds(mode, 1), at]
            term = state_ref[pl.ds(mode, 1), at] * jnp.exp(-rate * lead)
            totals = add_mode(totals, term, rate)
        for i in range(0, blocks, 2):
            rows = pl.ds(i * SUB, 2 * SUB)
            conv = jnp.concatenate(totals[i : i + 2], axis=0).astype(BF16).astype(F32)
            mixed_ref[rows, at] = (query_ref[rows, at].astype(F32) * conv).astype(BF16)
        return carry

    lax.fori_loop(0, chans // LANES, one_lane, 0)


def gather(copies, axis, groups=None):
    return lax.all_to_all(copies, axis, 0, 0, tiled=True, axis_index_groups=groups)


def per_device(stream, norm_gain, short_filter, decay_rate, residue):
    count, chans = stream.shape
    modes = decay_rate.shape[1]
    peers = lax.axis_size("ch")
    ctx = lax.axis_size("ctx")
    far = ctx // NEAR
    near_groups = [[g * NEAR + m for m in range(NEAR)] for g in range(far)]
    far_groups = [[g * NEAR + m for g in range(far)] for m in range(NEAR)]

    rim = lax.ppermute(stream[count - RIM :], "ctx", [(i, i + 1) for i in range(ctx - 1)])
    params = [norm_gain[None, :], short_filter.reshape(9, chans), decay_rate.T, residue.T]
    sums, gain, taps, rates, weights = call(
        square_sums, [((peers, 1, 2 * LANES), F32)] + [(p.shape, F32) for p in params], stream, rim, *params
    )
    sums = gather(sums, "ch")
    query, product, states = call(
        lambda *refs: block_states(chans * peers, *refs),
        [((count, chans), BF16), ((count, chans), F32), ((NEAR, modes, chans), F32)],
        sums, stream, rim, gain, taps, rates,
        scratch=[pltpu.VMEM((RIM + count, chans), F32)],
    )
    states = gather(states, "ctx", near_groups)
    before, totals, local = call(
        lambda *refs: near_scan(count, *refs),
        [((modes, chans), F32), ((far, modes, chans), F32), ((count, chans), F32)],
        states, rates, weights, product,
        scratch=[pltpu.VMEM((count, LANES), F32)], flops=10**7,
    )
    totals = gather(totals, "ctx", far_groups)
    (mixed,) = call(
        lambda *refs: outer_conv(count, far, *refs),
        [((count, chans), BF16)],
        totals, before, rates, weights, local, query,
        scratch=[pltpu.VMEM((modes, chans), F32)],
    )
    return mixed


def solution(mesh):
    in_specs = (P("ctx", "ch"), P("ch"), P(None, None, "ch"), P("ch", None), P("ch", None))
    out_specs = P("ctx", "ch")
    return jax.shard_map(
        per_device, mesh=mesh, in_specs=in_specs, out_specs=out_specs, check_vma=False
    )
```

```python
import jax
import jax.numpy as jnp
from jax import lax
from jax.experimental import pallas as pl
from jax.experimental.pallas import tpu as pltpu
from jax.sharding import PartitionSpec as P

EXACT = lax.Precision.HIGHEST
EPSILON = 1e-05
SUB = 8
LANES = 128
NEAR = 16

F32 = jnp.float32
BF16 = jnp.bfloat16


def call(body, outs, *args, scratch=(), flops=0):
    shapes = [jax.ShapeDtypeStruct(s, d) for s, d in outs]
    moved = sum(a.size * a.dtype.itemsize for a in args)
    return pl.pallas_call(
        body,
        out_shape=shapes,
        in_specs=[pl.BlockSpec(memory_space=pltpu.VMEM)] * len(args),
        out_specs=[pl.BlockSpec(memory_space=pltpu.VMEM)] * len(shapes),
        scratch_shapes=list(scratch),
        compiler_params=pltpu.CompilerParams(vmem_limit_bytes=16 * 2**20),
        cost_estimate=pl.CostEstimate(flops=flops, bytes_accessed=moved, transcendentals=0),
    )(*args)


def pack(ref):
    return jnp.concatenate([ref[:, l * LANES : (l + 1) * LANES] for l in range(ref.shape[1] // LANES)], axis=0)


def square_sums(stream_ref, gain_ref, taps_ref, rate_ref, residue_ref, sums_ref, gain_out, taps_out, rate_out, residue_out, taps_pack, rate_pack, residue_pack):
    chans = stream_ref.shape[1]
    values = stream_ref[...].astype(F32)
    sums = lax.dot_general(
        jnp.ones((SUB, chans), F32), values * values, (((1,), (1,)), ((), ())), precision=EXACT, preferred_element_type=F32
    )
    for peer in range(sums_ref.shape[0]):
        sums_ref[peer] = sums[:1]
    gain_out[...] = gain_ref[...]
    taps_out[...] = taps_ref[...]
    rate_out[...] = rate_ref[...]
    residue_out[...] = residue_ref[...]
    rate_pack[...] = pack(rate_ref)
    residue_pack[...] = pack(residue_ref)
    lanes = chans // LANES
    for k in range(taps_ref.shape[0]):
        for l in range(lanes):
            taps_pack[pl.ds(k * lanes + l, 1), :] = taps_ref[pl.ds(k, 1), pl.ds(l * LANES, LANES)]


def block_states(chan_total, sums_ref, stream_ref, gain_ref, taps_ref, rate_ref, query_ref, product_ref, message_ref, normed_ref, end_ref):
    count, chans = stream_ref.shape
    lanes = chans // LANES
    modes = rate_ref.shape[0]
    sums = sums_ref[0]
    for peer in range(1, sums_ref.shape[0]):
        sums = sums + sums_ref[peer]
    sums = jnp.broadcast_to(sums, (SUB, count))
    mean_square = lax.dot_general(
        sums, jnp.ones((SUB, chans), F32) / SUB, (((0,), (0,)), ((), ())), precision=EXACT, preferred_element_type=F32
    ) / chan_total
    values = stream_ref[...].astype(F32) * lax.rsqrt(mean_square + EPSILON) * gain_ref[...]
    normed_ref[:SUB] = jnp.zeros((SUB, chans), F32)
    normed_ref[SUB:] = values.astype(BF16).astype(F32)
    shifted = [normed_ref[SUB - j : SUB - j + count] for j in range(3)]

    def feature(role):
        total = taps_ref[pl.ds(role, 1)] * shifted[0]
        total = total + taps_ref[pl.ds(3 + role, 1)] * shifted[1]
        return total + taps_ref[pl.ds(6 + role, 1)] * shifted[2]

    query_ref[...] = feature(0).astype(BF16)
    product_ref[...] = (feature(1) * feature(2)).astype(BF16).astype(F32)
    row = lax.broadcasted_iota(jnp.int32, (SUB, chans), 0)
    product_ref[:SUB] = jnp.where(row < 2, 0.0, product_ref[:SUB])

    lag = (SUB - 1 - lax.broadcasted_iota(jnp.int32, (SUB, LANES), 0)).astype(F32)

    def one_lane(lane, carry):
        at = pl.ds(pl.multiple_of(lane * LANES, LANES), LANES)
        blocks = [product_ref[pl.ds(i * SUB, SUB), at] for i in range(count // SUB)]
        for mode in range(modes):
            rate = rate_ref[pl.ds(mode, 1), at]
            step = jnp.broadcast_to(jnp.exp(-SUB * rate), (SUB, LANES))
            total = blocks[0]
            for block in blocks[1:]:
                total = total * step + block
            end_ref[pl.ds(mode, 1), at] = jnp.sum(total * jnp.exp(-rate * lag), axis=0, keepdims=True)
        return carry

    lax.fori_loop(0, lanes, one_lane, 0)
    message_ref[0, : lanes * modes] = pack(end_ref)
    for e, place in enumerate((0, 1, count - 2, count - 1)):
        for l in range(lanes):
            message_ref[0, pl.ds(lanes * (modes + e) + l, 1), :] = normed_ref[pl.ds(SUB + place, 1), pl.ds(l * LANES, LANES)]
    message = message_ref[0]
    for peer in range(1, message_ref.shape[0]):
        message_ref[peer] = message


def first_rows(taps_ref, role, last, head):
    lanes = taps_ref.shape[0] // 9
    taps = [taps_ref[pl.ds((3 * j + role) * lanes, lanes)] for j in range(3)]
    first = taps[0] * head[0] + taps[1] * last[1] + taps[2] * last[0]
    second = taps[0] * head[1] + taps[1] * head[0] + taps[2] * last[1]
    return first, second


def first_products(taps_ref, last, head):
    keys, values = first_rows(taps_ref, 1, last, head), first_rows(taps_ref, 2, last, head)
    return [(k * v).astype(BF16).astype(F32) for k, v in zip(keys, values)]


def spread(rows, modes):
    return jnp.concatenate([jnp.broadcast_to(rows[l : l + 1], (modes, LANES)) for l in range(rows.shape[0])], axis=0)


def pairs(ref, start, lanes):
    return ref[pl.ds(start, lanes), :], ref[pl.ds(start + lanes, lanes), :]


def near_scan(block, lanes, got_ref, rate_ref, taps_ref, before_ref, total_ref, message_ref):
    place = lax.axis_index("ctx") % NEAR
    states = rate_ref.shape[0]
    modes = states // lanes
    rates = rate_ref[...]
    step, late, later = jnp.exp(-block * rates), jnp.exp(-(block - 1) * rates), jnp.exp(-(block - 2) * rates)
    total = got_ref[0, :states]
    before = jnp.where(place == 1, total, jnp.zeros_like(total))
    for j in range(1, NEAR):
        last = pairs(got_ref.at[j - 1], states + 2 * lanes, lanes)
        head = pairs(got_ref.at[j], states, lanes)
        first, second = first_products(taps_ref, last, head)
        total = total * step + got_ref[j, :states] + late * spread(first, modes) + later * spread(second, modes)
        if j < NEAR - 1:
            before = jnp.where(place == j + 1, total, before)
    before_ref[...] = before
    total_ref[...] = total
    send(block, lanes, None, total, got_ref, rates, taps_ref, message_ref)


def send(block, lanes, came_ref, total, got_ref, rates, taps_ref, message_ref):
    states = rates.shape[0]
    modes = states // lanes
    head = pairs(got_ref.at[0], states, lanes)
    if came_ref is None:
        last = [jnp.zeros((lanes, LANES), F32)] * 2
    else:
        last = pairs(came_ref, states, lanes)
        total = total + came_ref[:states] * jnp.exp(-(block * NEAR) * rates)
    first, second = first_products(taps_ref, last, head)
    total = total + jnp.exp(-(block * NEAR - 1) * rates) * spread(first, modes)
    total = total + jnp.exp(-(block * NEAR - 2) * rates) * spread(second, modes)
    message_ref[:states] = total
    message_ref[states:] = got_ref[NEAR - 1, states + 2 * lanes :]


def chain_step(block, lanes, came_ref, total_ref, got_ref, rate_ref, taps_ref, message_ref):
    send(block, lanes, came_ref, total_ref[...], got_ref, rate_ref[...], taps_ref, message_ref)


def add_mode(totals, term, rate):
    step = jnp.broadcast_to(jnp.exp(-SUB * rate), term.shape)
    out = []
    for total in totals:
        out.append(total + term)
        term = term * step
    return out


def inner_conv(rate_ref, residue_ref, product_ref, after_ref, local_ref, filter_ref):
    count, chans = product_ref.shape
    modes = rate_ref.shape[0]
    blocks = count // SUB
    row = lax.broadcasted_iota(jnp.int32, (SUB, LANES), 0)
    lead = row.astype(F32)

    def one_lane(lane, carry):
        at = pl.ds(pl.multiple_of(lane * LANES, LANES), LANES)
        zero = jnp.zeros((SUB, LANES), F32)
        totals = [zero] * blocks
        for mode in range(modes):
            rate = rate_ref[pl.ds(mode, 1), at]
            term = residue_ref[pl.ds(mode, 1), at] * jnp.exp(-rate * lead)
            totals = add_mode(totals, term, rate)
        for i in range(blocks):
            filter_ref[pl.ds(i * SUB, SUB), :] = totals[i]

        shifted = [product_ref[pl.ds(i * SUB, SUB), at] for i in range(blocks)]
        totals = [zero] * blocks
        for b in range(SUB):
            for a in range(blocks):
                weight = filter_ref[pl.ds(a * SUB + b, 1), :]
                for j in range(blocks - a):
                    totals[j + a] = totals[j + a] + weight * shifted[j]
            if b < SUB - 1:
                rolled = [pltpu.roll(s, 1, 0) for s in shifted]
                shifted = [jnp.where(row == 0, before, now) for before, now in zip([zero] + rolled[:-1], rolled)]
        for i in range(blocks):
            local_ref[pl.ds(i * SUB, SUB), at] = totals[i]
        return carry

    lax.fori_loop(0, chans // LANES, one_lane, 0)


def outer_conv(steps, got_ref, *refs):
    came_refs, refs = refs[:steps], refs[steps:]
    before_ref, rate_pack, residue_pack, taps_ref, rate_ref, local_ref, query_ref, mixed_ref, state_ref = refs
    count, chans = local_ref.shape
    lanes = chans // LANES
    modes = rate_ref.shape[0]
    states = lanes * modes
    blocks = count // SUB
    place = lax.axis_index("ctx") % NEAR
    rates = rate_pack[...]
    came = came_refs[0][...]
    for ref in came_refs[1:]:
        came = came + ref[...]
    group_last = (came[states : states + lanes], came[states + lanes :])
    first, second = first_products(taps_ref, group_last, pairs(got_ref.at[0], states, lanes))
    lag = (count * place).astype(F32)
    lead = jnp.exp(-rates * lag)
    state = before_ref[...] + came[:states] * lead
    held = jnp.exp(-rates * jnp.maximum(lag - 1.0, 0.0)) * spread(first, modes)
    held = held + jnp.exp(-rates * jnp.maximum(lag - 2.0, 0.0)) * spread(second, modes)
    state = state + jnp.where(place > 0, held, 0.0)

    own_last = pairs(got_ref.at[jnp.maximum(place - 1, 0)], states + 2 * lanes, lanes)
    own_last = [jnp.where(place > 0, own, group) for own, group in zip(own_last, group_last)]
    own_head = pairs(got_ref.at[place], states, lanes)
    own_query = [q.astype(BF16).astype(F32) for q in first_rows(taps_ref, 0, own_last, own_head)]
    first, second = first_products(taps_ref, own_last, own_head)
    ahead = jnp.exp(rates) * spread(second, modes)
    state = state * jnp.exp(-rates) + spread(first, modes) + ahead
    state = state * residue_pack[...]
    ahead = ahead * residue_pack[...]
    extra = [jnp.sum(ahead[l * modes : (l + 1) * modes], axis=0, keepdims=True) for l in range(lanes)]
    row = lax.broadcasted_iota(jnp.int32, (SUB, LANES), 0)
    lead = row.astype(F32)
    for l in range(lanes):
        state_ref[:modes, pl.ds(l * LANES, LANES)] = state[l * modes : (l + 1) * modes]
        take = jnp.where(row == 0, jnp.broadcast_to(extra[l], row.shape), 0.0)
        query = jnp.where(row == 0, own_query[0][l : l + 1], jnp.where(row == 1, own_query[1][l : l + 1], 0.0))
        state_ref[modes : modes + SUB, pl.ds(l * LANES, LANES)] = take
        state_ref[modes + SUB :, pl.ds(l * LANES, LANES)] = query
    rows = lax.broadcasted_iota(jnp.int32, (2 * SUB, LANES), 0)

    def one_lane(lane, carry):
        at = pl.ds(pl.multiple_of(lane * LANES, LANES), LANES)
        totals = [local_ref[pl.ds(i * SUB, SUB), at] for i in range(blocks)]
        for mode in range(modes):
            rate = rate_ref[pl.ds(mode, 1), at]
            term = state_ref[pl.ds(mode, 1), at] * jnp.exp(-rate * lead)
            totals = add_mode(totals, term, rate)
        totals[0] = totals[0] - state_ref[pl.ds(modes, SUB), at]
        for i in range(0, blocks, 2):
            where = pl.ds(i * SUB, 2 * SUB)
            conv = jnp.concatenate(totals[i : i + 2], axis=0).astype(BF16).astype(F32)
            query = query_ref[where, at].astype(F32)
            if i == 0:
                fixed = state_ref[pl.ds(modes + SUB, SUB), at]
                query = jnp.where(rows < 2, jnp.concatenate([fixed, fixed], axis=0), query)
            mixed_ref[where, at] = (query * conv).astype(BF16)
        return carry

    lax.fori_loop(0, lanes, one_lane, 0)


def gather(copies, axis, groups=None):
    return lax.all_to_all(copies, axis, 0, 0, tiled=True, axis_index_groups=groups)


def per_device(stream, norm_gain, short_filter, decay_rate, residue):
    count, chans = stream.shape
    modes = decay_rate.shape[1]
    lanes = chans // LANES
    states = lanes * modes
    peers = lax.axis_size("ch")
    groups = lax.axis_size("ctx") // NEAR
    members = [[g * NEAR + m for m in range(NEAR)] for g in range(groups)]

    params = [norm_gain[None, :], short_filter.reshape(9, chans), decay_rate.T, residue.T]
    packed = [((9 * lanes, LANES), F32), ((states, LANES), F32), ((states, LANES), F32)]
    sums, gain, taps, rates, weights, taps_pack, rate_pack, residue_pack = call(
        square_sums, [((peers, 1, count), F32)] + [(p.shape, F32) for p in params] + packed, stream, *params
    )
    sums = gather(sums, "ch")
    query, product, message = call(
        lambda *refs: block_states(chans * peers, *refs),
        [((count, chans), BF16), ((count, chans), F32), ((NEAR, states + 4 * lanes, LANES), F32)],
        sums, stream, gain, taps, rates,
        scratch=[pltpu.VMEM((SUB + count, chans), F32), pltpu.VMEM((modes, chans), F32)],
    )
    got = gather(message, "ctx", members)
    carried = ((states + 2 * lanes, LANES), F32)
    before, total, message = call(
        lambda *refs: near_scan(count, lanes, *refs),
        [((states, LANES), F32), ((states, LANES), F32), carried],
        got, rate_pack, taps_pack,
    )
    came = []
    for g in range(1, groups):
        if g > 1:
            (message,) = call(
                lambda *refs: chain_step(count, lanes, *refs), [carried], came[-1], total, got, rate_pack, taps_pack
            )
        came.append(lax.ppermute(message, "ctx", [(a, b) for a, b in zip(members[g - 1], members[g])]))
        if g == 1:
            (local,) = call(
                inner_conv, [((count, chans), F32)], rates, weights, product, before,
                scratch=[pltpu.VMEM((count, LANES), F32)], flops=10**7,
            )
    (mixed,) = call(
        lambda *refs: outer_conv(len(came), *refs),
        [((count, chans), BF16)],
        got, *came, before, rate_pack, residue_pack, taps_pack, rates, local, query,
        scratch=[pltpu.VMEM((modes + 2 * SUB, chans), F32)],
    )
    return mixed


def solution(mesh):
    in_specs = (P("ctx", "ch"), P("ch"), P(None, None, "ch"), P("ch", None), P("ch", None))
    out_specs = P("ctx", "ch")
    return jax.shard_map(
        per_device, mesh=mesh, in_specs=in_specs, out_specs=out_specs, check_vma=False
    )
```

```python
import jax
import jax.numpy as jnp
from jax import lax
from jax.experimental import pallas as pl
from jax.experimental.pallas import tpu as pltpu
from jax.sharding import PartitionSpec as P

EXACT = lax.Precision.HIGHEST
EPSILON = 1e-05
SUB = 8
LANES = 128
NEAR = 4

F32 = jnp.float32
BF16 = jnp.bfloat16


def call(body, outs, *args, scratch=(), flops=0):
    shapes = [jax.ShapeDtypeStruct(s, d) for s, d in outs]
    moved = sum(a.size * a.dtype.itemsize for a in args)
    return pl.pallas_call(
        body,
        out_shape=shapes,
        in_specs=[pl.BlockSpec(memory_space=pltpu.VMEM)] * len(args),
        out_specs=[pl.BlockSpec(memory_space=pltpu.VMEM)] * len(shapes),
        scratch_shapes=list(scratch),
        compiler_params=pltpu.CompilerParams(vmem_limit_bytes=16 * 2**20),
        cost_estimate=pl.CostEstimate(flops=flops, bytes_accessed=moved, transcendentals=0),
    )(*args)


def pack(ref):
    return jnp.concatenate([ref[:, l * LANES : (l + 1) * LANES] for l in range(ref.shape[1] // LANES)], axis=0)


def square_sums(stream_ref, gain_ref, taps_ref, rate_ref, residue_ref, sums_ref, gain_out, taps_out, rate_out, residue_out, taps_pack, rate_pack, residue_pack):
    chans = stream_ref.shape[1]
    values = stream_ref[...].astype(F32)
    sums = lax.dot_general(
        jnp.ones((SUB, chans), F32), values * values, (((1,), (1,)), ((), ())), precision=EXACT, preferred_element_type=F32
    )
    for peer in range(sums_ref.shape[0]):
        sums_ref[peer] = sums[:1]
    gain_out[...] = gain_ref[...]
    taps_out[...] = taps_ref[...]
    rate_out[...] = rate_ref[...]
    residue_out[...] = residue_ref[...]
    rate_pack[...] = pack(rate_ref)
    residue_pack[...] = pack(residue_ref)
    lanes = chans // LANES
    for k in range(taps_ref.shape[0]):
        for l in range(lanes):
            taps_pack[pl.ds(k * lanes + l, 1), :] = taps_ref[pl.ds(k, 1), pl.ds(l * LANES, LANES)]


def block_states(chan_total, sums_ref, stream_ref, gain_ref, taps_ref, rate_ref, query_ref, product_ref, message_ref, normed_ref, end_ref):
    count, chans = stream_ref.shape
    lanes = chans // LANES
    modes = rate_ref.shape[0]
    sums = sums_ref[0]
    for peer in range(1, sums_ref.shape[0]):
        sums = sums + sums_ref[peer]
    sums = jnp.broadcast_to(sums, (SUB, count))
    mean_square = lax.dot_general(
        sums, jnp.ones((SUB, chans), F32) / SUB, (((0,), (0,)), ((), ())), precision=EXACT, preferred_element_type=F32
    ) / chan_total
    values = stream_ref[...].astype(F32) * lax.rsqrt(mean_square + EPSILON) * gain_ref[...]
    normed_ref[:SUB] = jnp.zeros((SUB, chans), F32)
    normed_ref[SUB:] = values.astype(BF16).astype(F32)
    shifted = [normed_ref[SUB - j : SUB - j + count] for j in range(3)]

    def feature(role):
        total = taps_ref[pl.ds(role, 1)] * shifted[0]
        total = total + taps_ref[pl.ds(3 + role, 1)] * shifted[1]
        return total + taps_ref[pl.ds(6 + role, 1)] * shifted[2]

    query_ref[...] = feature(0).astype(BF16)
    product_ref[...] = (feature(1) * feature(2)).astype(BF16).astype(F32)
    row = lax.broadcasted_iota(jnp.int32, (SUB, chans), 0)
    product_ref[:SUB] = jnp.where(row < 2, 0.0, product_ref[:SUB])

    lag = (SUB - 1 - lax.broadcasted_iota(jnp.int32, (SUB, LANES), 0)).astype(F32)

    def one_lane(lane, carry):
        at = pl.ds(pl.multiple_of(lane * LANES, LANES), LANES)
        blocks = [product_ref[pl.ds(i * SUB, SUB), at] for i in range(count // SUB)]
        for mode in range(modes):
            rate = rate_ref[pl.ds(mode, 1), at]
            step = jnp.broadcast_to(jnp.exp(-SUB * rate), (SUB, LANES))
            total = blocks[0]
            for block in blocks[1:]:
                total = total * step + block
            end_ref[pl.ds(mode, 1), at] = jnp.sum(total * jnp.exp(-rate * lag), axis=0, keepdims=True)
        return carry

    lax.fori_loop(0, lanes, one_lane, 0)
    message_ref[0, : lanes * modes] = pack(end_ref)
    for e, place in enumerate((0, 1, count - 2, count - 1)):
        for l in range(lanes):
            message_ref[0, pl.ds(lanes * (modes + e) + l, 1), :] = normed_ref[pl.ds(SUB + place, 1), pl.ds(l * LANES, LANES)]
    message = message_ref[0]
    for peer in range(1, message_ref.shape[0]):
        message_ref[peer] = message


def first_rows(taps_ref, role, last, head):
    lanes = taps_ref.shape[0] // 9
    taps = [taps_ref[pl.ds((3 * j + role) * lanes, lanes)] for j in range(3)]
    first = taps[0] * head[0] + taps[1] * last[1] + taps[2] * last[0]
    second = taps[0] * head[1] + taps[1] * head[0] + taps[2] * last[1]
    return first, second


def first_products(taps_ref, last, head):
    keys, values = first_rows(taps_ref, 1, last, head), first_rows(taps_ref, 2, last, head)
    return [(k * v).astype(BF16).astype(F32) for k, v in zip(keys, values)]


def spread(rows, modes):
    return jnp.concatenate([jnp.broadcast_to(rows[l : l + 1], (modes, LANES)) for l in range(rows.shape[0])], axis=0)


def pairs(ref, start, lanes):
    return ref[pl.ds(start, lanes), :], ref[pl.ds(start + lanes, lanes), :]


def step_over(block, lanes, rates, taps_ref, state, last, run_ref):
    states = rates.shape[0]
    modes = states // lanes
    first, second = first_products(taps_ref, last, pairs(run_ref, states, lanes))
    end = run_ref[:states] + state * jnp.exp(-block * rates)
    end = end + jnp.exp(-(block - 1) * rates) * spread(first, modes) + jnp.exp(-(block - 2) * rates) * spread(second, modes)
    return end, pairs(run_ref, states + 2 * lanes, lanes)


def step_into(block, lanes, place, rates, taps_ref, state, last, got_ref, before_ref):
    states = rates.shape[0]
    modes = states // lanes
    first, second = first_products(taps_ref, last, pairs(got_ref.at[0], states, lanes))
    lag = (block * place).astype(F32)
    held = jnp.exp(-rates * jnp.maximum(lag - 1.0, 0.0)) * spread(first, modes)
    held = held + jnp.exp(-rates * jnp.maximum(lag - 2.0, 0.0)) * spread(second, modes)
    state = before_ref[...] + state * jnp.exp(-rates * lag) + jnp.where(place > 0, held, 0.0)
    inside = pairs(got_ref.at[jnp.maximum(place - 1, 0)], states + 2 * lanes, lanes)
    return state, [jnp.where(place > 0, a, b) for a, b in zip(inside, last)]


def near_scan(block, lanes, place, got_ref, rate_ref, taps_ref, before_ref, message_ref):
    states = rate_ref.shape[0]
    rates = rate_ref[...]
    total, last = got_ref[0, :states], pairs(got_ref.at[0], states + 2 * lanes, lanes)
    before = jnp.where(place() == 1, total, jnp.zeros_like(total))
    for j in range(1, NEAR):
        total, last = step_over(block, lanes, rates, taps_ref, total, last, got_ref.at[j])
        if j < NEAR - 1:
            before = jnp.where(place() == j + 1, total, before)
    before_ref[...] = before
    head = got_ref[0, states : states + 2 * lanes]
    tail = got_ref[NEAR - 1, states + 2 * lanes :]
    for peer in range(message_ref.shape[0]):
        message_ref[peer, :states] = total
        message_ref[peer, states : states + 2 * lanes] = head
        message_ref[peer, states + 2 * lanes :] = tail


def relay(block, lanes, came_ref, own_ref, rate_ref, taps_ref, out_ref):
    rates = rate_ref[...]
    states = rates.shape[0]
    state, last = jnp.zeros_like(rates), [jnp.zeros((lanes, LANES), F32)] * 2
    for ref in (came_ref, own_ref.at[0]):
        state, last = step_over(block, lanes, rates, taps_ref, state, last, ref)
    out_ref[:states] = state
    out_ref[pl.ds(states, lanes)] = last[0]
    out_ref[pl.ds(states + lanes, lanes)] = last[1]


def add_mode(totals, term, rate):
    step = jnp.broadcast_to(jnp.exp(-SUB * rate), term.shape)
    out = []
    for total in totals:
        out.append(total + term)
        term = term * step
    return out


def inner_conv(rate_ref, residue_ref, product_ref, after_ref, local_ref, filter_ref):
    count, chans = product_ref.shape
    modes = rate_ref.shape[0]
    blocks = count // SUB
    row = lax.broadcasted_iota(jnp.int32, (SUB, LANES), 0)
    lead = row.astype(F32)

    def one_lane(lane, carry):
        at = pl.ds(pl.multiple_of(lane * LANES, LANES), LANES)
        zero = jnp.zeros((SUB, LANES), F32)
        totals = [zero] * blocks
        for mode in range(modes):
            rate = rate_ref[pl.ds(mode, 1), at]
            term = residue_ref[pl.ds(mode, 1), at] * jnp.exp(-rate * lead)
            totals = add_mode(totals, term, rate)
        for i in range(blocks):
            filter_ref[pl.ds(i * SUB, SUB), :] = totals[i]

        shifted = [product_ref[pl.ds(i * SUB, SUB), at] for i in range(blocks)]
        totals = [zero] * blocks
        for b in range(SUB):
            for a in range(blocks):
                weight = filter_ref[pl.ds(a * SUB + b, 1), :]
                for j in range(blocks - a):
                    totals[j + a] = totals[j + a] + weight * shifted[j]
            if b < SUB - 1:
                rolled = [pltpu.roll(s, 1, 0) for s in shifted]
                shifted = [jnp.where(row == 0, before, now) for before, now in zip([zero] + rolled[:-1], rolled)]
        for i in range(blocks):
            local_ref[pl.ds(i * SUB, SUB), at] = totals[i]
        return carry

    lax.fori_loop(0, chans // LANES, one_lane, 0)


def outer_conv(near_ref, near_before, far_ref, far_before, odd_ref, third_ref, fourth_ref, rate_pack, residue_pack, taps_ref, rate_ref, local_ref, query_ref, mixed_ref, state_ref):
    count, chans = local_ref.shape
    lanes = chans // LANES
    modes = rate_ref.shape[0]
    states = lanes * modes
    blocks = count // SUB
    place, level, group = places()
    rates = rate_pack[...]
    came = third_ref[...] + fourth_ref[...]
    state, last = came[:states], (came[states : states + lanes], came[states + lanes :])
    after, after_last = step_over(count * NEAR * NEAR, lanes, rates, taps_ref, state, last, odd_ref)
    odd = group % 2 == 1
    state, last = jnp.where(odd, after, state), [jnp.where(odd, a, b) for a, b in zip(after_last, last)]
    state, last = step_into(count * NEAR, lanes, level, rates, taps_ref, state, last, far_ref, far_before)
    state, own_last = step_into(count, lanes, place, rates, taps_ref, state, last, near_ref, near_before)
    own_head = pairs(near_ref.at[place], states, lanes)
    own_query = [q.astype(BF16).astype(F32) for q in first_rows(taps_ref, 0, own_last, own_head)]
    first, second = first_products(taps_ref, own_last, own_head)
    ahead = jnp.exp(rates) * spread(second, modes)
    state = state * jnp.exp(-rates) + spread(first, modes) + ahead
    state = state * residue_pack[...]
    ahead = ahead * residue_pack[...]
    extra = [jnp.sum(ahead[l * modes : (l + 1) * modes], axis=0, keepdims=True) for l in range(lanes)]
    row = lax.broadcasted_iota(jnp.int32, (SUB, LANES), 0)
    lead = row.astype(F32)
    for l in range(lanes):
        state_ref[:modes, pl.ds(l * LANES, LANES)] = state[l * modes : (l + 1) * modes]
        take = jnp.where(row == 0, jnp.broadcast_to(extra[l], row.shape), 0.0)
        query = jnp.where(row == 0, own_query[0][l : l + 1], jnp.where(row == 1, own_query[1][l : l + 1], 0.0))
        state_ref[modes : modes + SUB, pl.ds(l * LANES, LANES)] = take
        state_ref[modes + SUB :, pl.ds(l * LANES, LANES)] = query
    rows = lax.broadcasted_iota(jnp.int32, (2 * SUB, LANES), 0)

    def one_lane(lane, carry):
        at = pl.ds(pl.multiple_of(lane * LANES, LANES), LANES)
        totals = [local_ref[pl.ds(i * SUB, SUB), at] for i in range(blocks)]
        for mode in range(modes):
            rate = rate_ref[pl.ds(mode, 1), at]
            term = state_ref[pl.ds(mode, 1), at] * jnp.exp(-rate * lead)
            totals = add_mode(totals, term, rate)
        totals[0] = totals[0] - state_ref[pl.ds(modes, SUB), at]
        for i in range(0, blocks, 2):
            where = pl.ds(i * SUB, 2 * SUB)
            conv = jnp.concatenate(totals[i : i + 2], axis=0).astype(BF16).astype(F32)
            query = query_ref[where, at].astype(F32)
            if i == 0:
                fixed = state_ref[pl.ds(modes + SUB, SUB), at]
                query = jnp.where(rows < 2, jnp.concatenate([fixed, fixed], axis=0), query)
            mixed_ref[where, at] = (query * conv).astype(BF16)
        return carry

    lax.fori_loop(0, lanes, one_lane, 0)


def places():
    index = lax.axis_index("ctx")
    return index % NEAR, index // NEAR % NEAR, index // NEAR**2


def gather(copies, axis, groups=None):
    return lax.all_to_all(copies, axis, 0, 0, tiled=True, axis_index_groups=groups)


def per_device(stream, norm_gain, short_filter, decay_rate, residue):
    count, chans = stream.shape
    modes = decay_rate.shape[1]
    lanes = chans // LANES
    states = lanes * modes
    peers = lax.axis_size("ch")
    ctx = lax.axis_size("ctx")
    runs = [[r + m for m in range(NEAR)] for r in range(0, ctx, NEAR)]
    columns = [[g + m + NEAR * r for r in range(NEAR)] for g in range(0, ctx, NEAR**2) for m in range(NEAR)]
    groups = [[g + m for m in range(NEAR**2)] for g in range(0, ctx, NEAR**2)]

    params = [norm_gain[None, :], short_filter.reshape(9, chans), decay_rate.T, residue.T]
    packed = [((9 * lanes, LANES), F32), ((states, LANES), F32), ((states, LANES), F32)]
    sums, gain, taps, rates, weights, taps_pack, rate_pack, residue_pack = call(
        square_sums, [((peers, 1, count), F32)] + [(p.shape, F32) for p in params] + packed, stream, *params
    )
    sums = gather(sums, "ch")
    query, product, message = call(
        lambda *refs: block_states(chans * peers, *refs),
        [((count, chans), BF16), ((count, chans), F32), ((NEAR, states + 4 * lanes, LANES), F32)],
        sums, stream, gain, taps, rates,
        scratch=[pltpu.VMEM((SUB + count, chans), F32), pltpu.VMEM((modes, chans), F32)],
    )
    shapes = [((states, LANES), F32), ((NEAR, states + 4 * lanes, LANES), F32)]
    near = gather(message, "ctx", runs)
    near_before, message = call(
        lambda *refs: near_scan(count, lanes, lambda: places()[0], *refs), shapes, near, rate_pack, taps_pack
    )
    far = gather(message, "ctx", columns)
    far_before, message = call(
        lambda *refs: near_scan(count * NEAR, lanes, lambda: places()[1], *refs),
        [shapes[0], ((1,) + shapes[1][0][1:], F32)],
        far, rate_pack, taps_pack,
    )
    hops = [list(zip(groups[a], groups[b])) for a, b in ((0, 1), (2, 3), (1, 2), (1, 3))]
    odd = lax.ppermute(message[0], "ctx", hops[0] + hops[1])
    (local,) = call(
        inner_conv, [((count, chans), F32)], rates, weights, product, far_before,
        scratch=[pltpu.VMEM((count, LANES), F32)], flops=10**7,
    )
    (relayed,) = call(
        lambda *refs: relay(count * NEAR**2, lanes, *refs),
        [((states + 2 * lanes, LANES), F32)],
        odd, message, rate_pack, taps_pack,
    )
    fourth = lax.ppermute(relayed, "ctx", hops[3])
    third = lax.ppermute(relayed, "ctx", hops[2])
    (mixed,) = call(
        outer_conv,
        [((count, chans), BF16)],
        near, near_before, far, far_before, odd, third, fourth, rate_pack, residue_pack, taps_pack, rates, local, query,
        scratch=[pltpu.VMEM((modes + 2 * SUB, chans), F32)],
    )
    return mixed


def solution(mesh):
    in_specs = (P("ctx", "ch"), P("ch"), P(None, None, "ch"), P("ch", None), P("ch", None))
    out_specs = P("ctx", "ch")
    return jax.shard_map(
        per_device, mesh=mesh, in_specs=in_specs, out_specs=out_specs, check_vma=False
    )
```

```python
import jax
import jax.numpy as jnp
from jax import lax
from jax.experimental import pallas as pl
from jax.experimental.pallas import tpu as pltpu
from jax.sharding import PartitionSpec as P

EXACT = lax.Precision.HIGHEST
EPSILON = 1e-05
SUB = 8
LANES = 128
NEAR = 4

F32 = jnp.float32
BF16 = jnp.bfloat16


def call(body, outs, *args, scratch=(), flops=0, space=pltpu.VMEM, grant=16):
    shapes = [jax.ShapeDtypeStruct(s, d) for s, d in outs]
    moved = sum(a.size * a.dtype.itemsize for a in args)
    return pl.pallas_call(
        body,
        out_shape=shapes,
        in_specs=[pl.BlockSpec(memory_space=space)] * len(args),
        out_specs=[pl.BlockSpec(memory_space=pltpu.VMEM)] * len(shapes),
        scratch_shapes=list(scratch),
        compiler_params=pltpu.CompilerParams(vmem_limit_bytes=grant * 2**20),
        cost_estimate=pl.CostEstimate(flops=flops, bytes_accessed=moved, transcendentals=0),
    )(*args)


def pack(ref):
    return jnp.concatenate([ref[:, l * LANES : (l + 1) * LANES] for l in range(ref.shape[1] // LANES)], axis=0)


def square_sums(*refs):
    count = 5
    held, refs = refs[:count], refs[count:]
    (stream_ref, gain_ref, taps_ref, rate_ref, residue_ref), refs = refs[:count], refs[count:]
    sums_ref, taps_pack, rate_pack, residue_pack, sem = refs
    copies = [pltpu.make_async_copy(held[i], out, sem.at[i]) for i, out in enumerate((stream_ref, gain_ref, taps_ref, rate_ref, residue_ref))]
    for copy in copies:
        copy.start()
    for copy in copies:
        copy.wait()
    chans = stream_ref.shape[1]
    values = stream_ref[...].astype(F32)
    sums = lax.dot_general(
        jnp.ones((SUB, chans), F32), values * values, (((1,), (1,)), ((), ())), precision=EXACT, preferred_element_type=F32
    )
    for peer in range(sums_ref.shape[0]):
        sums_ref[peer] = sums[:1]
    rate_pack[...] = pack(rate_ref)
    residue_pack[...] = pack(residue_ref)
    lanes = chans // LANES
    for tap in range(3):
        for role in range(3):
            for l in range(lanes):
                taps_pack[pl.ds((tap * 3 + role) * lanes + l, 1), :] = taps_ref[tap, pl.ds(role, 1), pl.ds(l * LANES, LANES)]


def block_states(chan_total, sums_ref, stream_ref, gain_ref, taps_ref, rate_ref, query_ref, product_ref, message_ref, normed_ref, end_ref):
    count, chans = stream_ref.shape
    lanes = chans // LANES
    modes = rate_ref.shape[0]
    sums = sums_ref[0]
    for peer in range(1, sums_ref.shape[0]):
        sums = sums + sums_ref[peer]
    sums = jnp.broadcast_to(sums, (SUB, count))
    mean_square = lax.dot_general(
        sums, jnp.ones((SUB, chans), F32) / SUB, (((0,), (0,)), ((), ())), precision=EXACT, preferred_element_type=F32
    ) / chan_total
    values = stream_ref[...].astype(F32) * lax.rsqrt(mean_square + EPSILON) * gain_ref[...]
    normed_ref[:SUB] = jnp.zeros((SUB, chans), F32)
    normed_ref[SUB:] = values.astype(BF16).astype(F32)
    shifted = [normed_ref[SUB - j : SUB - j + count] for j in range(3)]

    def feature(role):
        total = taps_ref[0, pl.ds(role, 1)] * shifted[0]
        total = total + taps_ref[1, pl.ds(role, 1)] * shifted[1]
        return total + taps_ref[2, pl.ds(role, 1)] * shifted[2]

    query_ref[...] = feature(0).astype(BF16)
    product_ref[...] = (feature(1) * feature(2)).astype(BF16).astype(F32)
    row = lax.broadcasted_iota(jnp.int32, (SUB, chans), 0)
    product_ref[:SUB] = jnp.where(row < 2, 0.0, product_ref[:SUB])

    lag = (SUB - 1 - lax.broadcasted_iota(jnp.int32, (SUB, LANES), 0)).astype(F32)

    def one_lane(lane, carry):
        at = pl.ds(pl.multiple_of(lane * LANES, LANES), LANES)
        blocks = [product_ref[pl.ds(i * SUB, SUB), at] for i in range(count // SUB)]
        for mode in range(modes):
            rate = rate_ref[pl.ds(mode, 1), at]
            step = jnp.broadcast_to(jnp.exp(-SUB * rate), (SUB, LANES))
            total = blocks[0]
            for block in blocks[1:]:
                total = total * step + block
            end_ref[pl.ds(mode, 1), at] = jnp.sum(total * jnp.exp(-rate * lag), axis=0, keepdims=True)
        return carry

    lax.fori_loop(0, lanes, one_lane, 0)
    message_ref[0, : lanes * modes] = pack(end_ref)
    for e, place in enumerate((0, 1, count - 2, count - 1)):
        for l in range(lanes):
            message_ref[0, pl.ds(lanes * (modes + e) + l, 1), :] = normed_ref[pl.ds(SUB + place, 1), pl.ds(l * LANES, LANES)]
    message = message_ref[0]
    for peer in range(1, message_ref.shape[0]):
        message_ref[peer] = message


def first_rows(taps_ref, role, last, head):
    lanes = taps_ref.shape[0] // 9
    taps = [taps_ref[pl.ds((3 * j + role) * lanes, lanes)] for j in range(3)]
    first = taps[0] * head[0] + taps[1] * last[1] + taps[2] * last[0]
    second = taps[0] * head[1] + taps[1] * head[0] + taps[2] * last[1]
    return first, second


def first_products(taps_ref, last, head):
    keys, values = first_rows(taps_ref, 1, last, head), first_rows(taps_ref, 2, last, head)
    return [(k * v).astype(BF16).astype(F32) for k, v in zip(keys, values)]


def spread(rows, modes):
    return jnp.concatenate([jnp.broadcast_to(rows[l : l + 1], (modes, LANES)) for l in range(rows.shape[0])], axis=0)


def pairs(ref, start, lanes):
    return ref[start : start + lanes], ref[start + lanes : start + 2 * lanes]


def step_over(block, lanes, rates, taps_ref, state, last, run_ref):
    states = rates.shape[0]
    modes = states // lanes
    first, second = first_products(taps_ref, last, pairs(run_ref, states, lanes))
    end = run_ref[:states] + state * jnp.exp(-block * rates)
    end = end + jnp.exp(-(block - 1) * rates) * spread(first, modes) + jnp.exp(-(block - 2) * rates) * spread(second, modes)
    return end, pairs(run_ref, states + 2 * lanes, lanes)


def step_into(block, lanes, place, rates, taps_ref, state, last, got_ref, before_ref):
    states = rates.shape[0]
    modes = states // lanes
    first, second = first_products(taps_ref, last, pairs(got_ref.at[0], states, lanes))
    lag = (block * place).astype(F32)
    held = jnp.exp(-rates * jnp.maximum(lag - 1.0, 0.0)) * spread(first, modes)
    held = held + jnp.exp(-rates * jnp.maximum(lag - 2.0, 0.0)) * spread(second, modes)
    state = before_ref[...] + state * jnp.exp(-rates * lag) + jnp.where(place > 0, held, 0.0)
    inside = pairs(got_ref.at[jnp.maximum(place - 1, 0)], states + 2 * lanes, lanes)
    return state, [jnp.where(place > 0, a, b) for a, b in zip(inside, last)]


def near_scan(block, lanes, place, got_ref, rate_ref, taps_ref, before_ref, message_ref):
    states = rate_ref.shape[0]
    rates = rate_ref[...]
    total, last = got_ref[0, :states], pairs(got_ref.at[0], states + 2 * lanes, lanes)
    before = jnp.where(place() == 1, total, jnp.zeros_like(total))
    for j in range(1, NEAR):
        total, last = step_over(block, lanes, rates, taps_ref, total, last, got_ref.at[j])
        if j < NEAR - 1:
            before = jnp.where(place() == j + 1, total, before)
    before_ref[...] = before
    head = got_ref[0, states : states + 2 * lanes]
    tail = got_ref[NEAR - 1, states + 2 * lanes :]
    for peer in range(message_ref.shape[0]):
        message_ref[peer, :states] = total
        message_ref[peer, states : states + 2 * lanes] = head
        message_ref[peer, states + 2 * lanes :] = tail


def relay(block, lanes, came_ref, own_ref, rate_ref, taps_ref, out_ref):
    rates = rate_ref[...]
    states = rates.shape[0]
    low = places()[2] == 0
    own, came = own_ref[0], came_ref[...]
    state, last = jnp.zeros_like(rates), [jnp.zeros((lanes, LANES), F32)] * 2
    for run in (jnp.where(low, own, came), jnp.where(low, came, own)):
        state, last = step_over(block, lanes, rates, taps_ref, state, last, run)
    out_ref[:states] = state
    out_ref[pl.ds(states, lanes)] = last[0]
    out_ref[pl.ds(states + lanes, lanes)] = last[1]
    rest = states + 2 * lanes
    out_ref[rest:] = jnp.zeros((out_ref.shape[0] - rest, LANES), F32)


def add_mode(totals, term, rate):
    step = jnp.broadcast_to(jnp.exp(-SUB * rate), term.shape)
    out = []
    for total in totals:
        out.append(total + term)
        term = term * step
    return out


def inner_conv(rate_ref, residue_ref, product_ref, after_ref, local_ref, filter_ref):
    count, chans = product_ref.shape
    modes = rate_ref.shape[0]
    blocks = count // SUB
    row = lax.broadcasted_iota(jnp.int32, (SUB, LANES), 0)
    lead = row.astype(F32)

    def one_lane(lane, carry):
        at = pl.ds(pl.multiple_of(lane * LANES, LANES), LANES)
        zero = jnp.zeros((SUB, LANES), F32)
        totals = [zero] * blocks
        for mode in range(modes):
            rate = rate_ref[pl.ds(mode, 1), at]
            term = residue_ref[pl.ds(mode, 1), at] * jnp.exp(-rate * lead)
            totals = add_mode(totals, term, rate)
        for i in range(blocks):
            filter_ref[pl.ds(i * SUB, SUB), :] = totals[i]

        shifted = [product_ref[pl.ds(i * SUB, SUB), at] for i in range(blocks)]
        totals = [zero] * blocks
        for b in range(SUB):
            for a in range(blocks):
                weight = filter_ref[pl.ds(a * SUB + b, 1), :]
                for j in range(blocks - a):
                    totals[j + a] = totals[j + a] + weight * shifted[j]
            if b < SUB - 1:
                rolled = [pltpu.roll(s, 1, 0) for s in shifted]
                shifted = [jnp.where(row == 0, before, now) for before, now in zip([zero] + rolled[:-1], rolled)]
        for i in range(blocks):
            local_ref[pl.ds(i * SUB, SUB), at] = totals[i]
        return carry

    lax.fori_loop(0, chans // LANES, one_lane, 0)


def outer_conv(near_ref, near_before, far_ref, far_before, swap_ref, two_ref, third_ref, rate_pack, residue_pack, taps_ref, rate_ref, local_ref, query_ref, mixed_ref, state_ref):
    count, chans = local_ref.shape
    lanes = chans // LANES
    modes = rate_ref.shape[0]
    states = lanes * modes
    blocks = count // SUB
    place, level, group = places()
    rates = rate_pack[...]
    came = two_ref[...]
    state, last = came[:states], (came[states : states + lanes], came[states + lanes : states + 2 * lanes])
    run = jnp.where(group == 1, swap_ref[...], third_ref[...])
    after, after_last = step_over(count * NEAR * NEAR, lanes, rates, taps_ref, state, last, run)
    odd = group % 2 == 1
    state, last = jnp.where(odd, after, state), [jnp.where(odd, a, b) for a, b in zip(after_last, last)]
    state, last = step_into(count * NEAR, lanes, level, rates, taps_ref, state, last, far_ref, far_before)
    state, own_last = step_into(count, lanes, place, rates, taps_ref, state, last, near_ref, near_before)
    own_head = pairs(near_ref.at[place], states, lanes)
    own_query = [q.astype(BF16).astype(F32) for q in first_rows(taps_ref, 0, own_last, own_head)]
    first, second = first_products(taps_ref, own_last, own_head)
    ahead = jnp.exp(rates) * spread(second, modes)
    state = state * jnp.exp(-rates) + spread(first, modes) + ahead
    state = state * residue_pack[...]
    ahead = ahead * residue_pack[...]
    extra = [jnp.sum(ahead[l * modes : (l + 1) * modes], axis=0, keepdims=True) for l in range(lanes)]
    row = lax.broadcasted_iota(jnp.int32, (SUB, LANES), 0)
    lead = row.astype(F32)
    for l in range(lanes):
        state_ref[:modes, pl.ds(l * LANES, LANES)] = state[l * modes : (l + 1) * modes]
        take = jnp.where(row == 0, jnp.broadcast_to(extra[l], row.shape), 0.0)
        query = jnp.where(row == 0, own_query[0][l : l + 1], jnp.where(row == 1, own_query[1][l : l + 1], 0.0))
        state_ref[modes : modes + SUB, pl.ds(l * LANES, LANES)] = take
        state_ref[modes + SUB :, pl.ds(l * LANES, LANES)] = query
    rows = lax.broadcasted_iota(jnp.int32, (2 * SUB, LANES), 0)

    def one_lane(lane, carry):
        at = pl.ds(pl.multiple_of(lane * LANES, LANES), LANES)
        totals = [local_ref[pl.ds(i * SUB, SUB), at] for i in range(blocks)]
        for mode in range(modes):
            rate = rate_ref[pl.ds(mode, 1), at]
            term = state_ref[pl.ds(mode, 1), at] * jnp.exp(-rate * lead)
            totals = add_mode(totals, term, rate)
        totals[0] = totals[0] - state_ref[pl.ds(modes, SUB), at]
        for i in range(0, blocks, 2):
            where = pl.ds(i * SUB, 2 * SUB)
            conv = jnp.concatenate(totals[i : i + 2], axis=0).astype(BF16).astype(F32)
            query = query_ref[where, at].astype(F32)
            if i == 0:
                fixed = state_ref[pl.ds(modes + SUB, SUB), at]
                query = jnp.where(rows < 2, jnp.concatenate([fixed, fixed], axis=0), query)
            mixed_ref[where, at] = (query * conv).astype(BF16)
        return carry

    lax.fori_loop(0, lanes, one_lane, 0)


def places():
    index = lax.axis_index("ctx")
    return index % NEAR, index // NEAR % NEAR, index // NEAR**2


def gather(copies, axis, groups=None):
    return lax.all_to_all(copies, axis, 0, 0, tiled=True, axis_index_groups=groups)


def per_device(stream, norm_gain, short_filter, decay_rate, residue):
    count, chans = stream.shape
    modes = decay_rate.shape[1]
    lanes = chans // LANES
    states = lanes * modes
    peers = lax.axis_size("ch")
    ctx = lax.axis_size("ctx")
    runs = [[r + m for m in range(NEAR)] for r in range(0, ctx, NEAR)]
    columns = [[g + m + NEAR * r for r in range(NEAR)] for g in range(0, ctx, NEAR**2) for m in range(NEAR)]
    groups = [[g + m for m in range(NEAR**2)] for g in range(0, ctx, NEAR**2)]

    held = [stream, norm_gain[None, :], short_filter, decay_rate.T, residue.T]
    held = [pltpu.with_memory_space_constraint(h, pltpu.HBM) for h in held]
    stream, gain, taps, rates, weights, sums, taps_pack, rate_pack, residue_pack = call(
        square_sums,
        [(h.shape, h.dtype) for h in held]
        + [((peers, 1, count), F32), ((9 * lanes, LANES), F32), ((states, LANES), F32), ((states, LANES), F32)],
        *held,
        scratch=[pltpu.SemaphoreType.DMA((len(held),))],
        space=pltpu.HBM,
    )
    sums = gather(sums, "ch")
    query, product, message = call(
        lambda *refs: block_states(chans * peers, *refs),
        [((count, chans), BF16), ((count, chans), F32), ((NEAR, states + 4 * lanes, LANES), F32)],
        sums, stream, gain, taps, rates,
        scratch=[pltpu.VMEM((SUB + count, chans), F32), pltpu.VMEM((modes, chans), F32)],
    )
    shapes = [((states, LANES), F32), ((NEAR, states + 4 * lanes, LANES), F32)]
    near = gather(message, "ctx", runs)
    near_before, message = call(
        lambda *refs: near_scan(count, lanes, lambda: places()[0], *refs), shapes, near, rate_pack, taps_pack
    )
    far = gather(message, "ctx", columns)
    far_before, message = call(
        lambda *refs: near_scan(count * NEAR, lanes, lambda: places()[1], *refs),
        [shapes[0], ((1,) + shapes[1][0][1:], F32)],
        far, rate_pack, taps_pack,
    )
    hops = lambda *ends: [pair for a, b in ends for pair in zip(groups[a], groups[b])]
    swap = lax.ppermute(message[0], "ctx", hops((0, 1), (1, 0)))
    (two,) = call(
        lambda *refs: relay(count * NEAR**2, lanes, *refs),
        [((states + 6 * lanes, LANES), F32)],
        swap, message, rate_pack, taps_pack,
    )
    third, two = lax.optimization_barrier((message[0], two))
    third = lax.ppermute(third, "ctx", hops((2, 3)))
    two = lax.ppermute(two, "ctx", hops((0, 3), (1, 2)))
    (local,) = call(
        inner_conv, [((count, chans), F32)], rates, weights, product, far_before,
        scratch=[pltpu.VMEM((count, LANES), F32)], flops=10**7,
    )
    (mixed,) = call(
        outer_conv,
        [((count, chans), BF16)],
        near, near_before, far, far_before, swap, two, third, rate_pack, residue_pack, taps_pack, rates, local, query,
        scratch=[pltpu.VMEM((modes + 2 * SUB, chans), F32)],
    )
    return mixed


def solution(mesh):
    in_specs = (P("ctx", "ch"), P("ch"), P(None, None, "ch"), P("ch", None), P("ch", None))
    out_specs = P("ctx", "ch")
    return jax.shard_map(
        per_device, mesh=mesh, in_specs=in_specs, out_specs=out_specs, check_vma=False
    )
```

```python
import jax
import jax.numpy as jnp
from jax import lax
from jax.experimental import pallas as pl
from jax.experimental.pallas import tpu as pltpu
from jax.sharding import PartitionSpec as P

EXACT = lax.Precision.HIGHEST
EPSILON = 1e-05
SUB = 8
LANES = 128
NEAR = 16

F32 = jnp.float32
BF16 = jnp.bfloat16


def call(body, outs, *args, scratch=(), flops=0, space=pltpu.VMEM, in_hbm=(), out_hbm=(), aliases=None):
    shapes = [jax.ShapeDtypeStruct(s, d) for s, d in outs]
    spaces = [pltpu.HBM if i in in_hbm else space for i in range(len(args))]
    out_spaces = [pltpu.HBM if i in out_hbm else pltpu.VMEM for i in range(len(outs))]
    moved = sum(a.size * a.dtype.itemsize for a in args)
    return pl.pallas_call(
        body,
        out_shape=shapes,
        in_specs=[pl.BlockSpec(memory_space=m) for m in spaces],
        out_specs=[pl.BlockSpec(memory_space=m) for m in out_spaces],
        scratch_shapes=list(scratch),
        input_output_aliases=aliases or {},
        compiler_params=pltpu.CompilerParams(vmem_limit_bytes=16 * 2**20),
        cost_estimate=pl.CostEstimate(flops=flops, bytes_accessed=moved, transcendentals=0),
    )(*args)


def pack(ref):
    return jnp.concatenate([ref[:, l * LANES : (l + 1) * LANES] for l in range(ref.shape[1] // LANES)], axis=0)


def square_sums(*refs):
    count = 5
    held, refs = refs[:count], refs[count:]
    (stream_ref, gain_ref, taps_ref, rate_ref, residue_ref), refs = refs[:count], refs[count:]
    sums_ref, taps_pack, rate_pack, residue_pack, sem = refs
    copies = [pltpu.make_async_copy(held[i], out, sem.at[i]) for i, out in enumerate((stream_ref, gain_ref, taps_ref, rate_ref, residue_ref))]
    for copy in copies:
        copy.start()
    for copy in copies:
        copy.wait()
    chans = stream_ref.shape[1]
    values = stream_ref[...].astype(F32)
    sums = lax.dot_general(
        jnp.ones((SUB, chans), F32), values * values, (((1,), (1,)), ((), ())), precision=EXACT, preferred_element_type=F32
    )
    for peer in range(sums_ref.shape[0]):
        sums_ref[peer] = sums[:1]
    rate_pack[...] = pack(rate_ref)
    residue_pack[...] = pack(residue_ref)
    lanes = chans // LANES
    for tap in range(3):
        for role in range(3):
            for l in range(lanes):
                taps_pack[pl.ds((tap * 3 + role) * lanes + l, 1), :] = taps_ref[tap, pl.ds(role, 1), pl.ds(l * LANES, LANES)]


def block_states(chan_total, sums_ref, stream_ref, gain_ref, taps_ref, rate_ref, query_ref, product_ref, message_ref, normed_ref, end_ref, whole_ref):
    count, chans = stream_ref.shape
    lanes = chans // LANES
    modes = rate_ref.shape[0]
    sums = sums_ref[0]
    for peer in range(1, sums_ref.shape[0]):
        sums = sums + sums_ref[peer]
    sums = jnp.broadcast_to(sums, (SUB, count))
    mean_square = lax.dot_general(
        sums, jnp.ones((SUB, chans), F32) / SUB, (((0,), (0,)), ((), ())), precision=EXACT, preferred_element_type=F32
    ) / chan_total
    values = stream_ref[...].astype(F32) * lax.rsqrt(mean_square + EPSILON) * gain_ref[...]
    normed_ref[:SUB] = jnp.zeros((SUB, chans), F32)
    normed_ref[SUB:] = values.astype(BF16).astype(F32)
    shifted = [normed_ref[SUB - j : SUB - j + count] for j in range(3)]

    def feature(role):
        total = taps_ref[0, pl.ds(role, 1)] * shifted[0]
        total = total + taps_ref[1, pl.ds(role, 1)] * shifted[1]
        return total + taps_ref[2, pl.ds(role, 1)] * shifted[2]

    query_ref[...] = feature(0).astype(BF16)
    product_ref[...] = (feature(1) * feature(2)).astype(BF16).astype(F32)
    row = lax.broadcasted_iota(jnp.int32, (SUB, chans), 0)
    product_ref[:SUB] = jnp.where(row < 2, 0.0, product_ref[:SUB])

    lag = (SUB - 1 - lax.broadcasted_iota(jnp.int32, (SUB, LANES), 0)).astype(F32)

    def one_lane(lane, carry):
        at = pl.ds(pl.multiple_of(lane * LANES, LANES), LANES)
        blocks = [product_ref[pl.ds(i * SUB, SUB), at] for i in range(count // SUB)]
        for mode in range(modes):
            rate = rate_ref[pl.ds(mode, 1), at]
            step = jnp.broadcast_to(jnp.exp(-SUB * rate), (SUB, LANES))
            total = blocks[0]
            for block in blocks[1:]:
                total = total * step + block
            end_ref[pl.ds(mode, 1), at] = jnp.sum(total * jnp.exp(-rate * lag), axis=0, keepdims=True)
        return carry

    lax.fori_loop(0, lanes, one_lane, 0)
    whole_ref[: lanes * modes] = pack(end_ref)
    for e, place in enumerate((0, 1, count - 2, count - 1)):
        for l in range(lanes):
            whole_ref[pl.ds(lanes * (modes + e) + l, 1), :] = normed_ref[pl.ds(SUB + place, 1), pl.ds(l * LANES, LANES)]
    message = whole_ref[...].astype(BF16)
    for peer in range(message_ref.shape[0]):
        message_ref[peer] = message


def first_rows(taps_ref, role, last, head):
    lanes = taps_ref.shape[0] // 9
    taps = [taps_ref[pl.ds((3 * j + role) * lanes, lanes)] for j in range(3)]
    first = taps[0] * head[0] + taps[1] * last[1] + taps[2] * last[0]
    second = taps[0] * head[1] + taps[1] * head[0] + taps[2] * last[1]
    return first, second


def first_products(taps_ref, last, head):
    keys, values = first_rows(taps_ref, 1, last, head), first_rows(taps_ref, 2, last, head)
    return [(k * v).astype(BF16).astype(F32) for k, v in zip(keys, values)]


def spread(rows, modes):
    return jnp.concatenate([jnp.broadcast_to(rows[l : l + 1], (modes, LANES)) for l in range(rows.shape[0])], axis=0)


def pairs(ref, start, lanes):
    return ref[start : start + lanes], ref[start + lanes : start + 2 * lanes]


def step_over(block, lanes, rates, taps_ref, state, last, run):
    states = rates.shape[0]
    modes = states // lanes
    first, second = first_products(taps_ref, last, pairs(run, states, lanes))
    end = run[:states] + state * jnp.exp(-block * rates)
    end = end + jnp.exp(-(block - 1) * rates) * spread(first, modes) + jnp.exp(-(block - 2) * rates) * spread(second, modes)
    return end, pairs(run, states + 2 * lanes, lanes)


def step_into(block, lanes, place, rates, taps_ref, state, last, got_ref, before_ref):
    states = rates.shape[0]
    modes = states // lanes
    first, second = first_products(taps_ref, last, pairs(got_ref[0].astype(F32), states, lanes))
    lag = (block * place).astype(F32)
    held = jnp.exp(-rates * jnp.maximum(lag - 1.0, 0.0)) * spread(first, modes)
    held = held + jnp.exp(-rates * jnp.maximum(lag - 2.0, 0.0)) * spread(second, modes)
    state = before_ref[...] + state * jnp.exp(-rates * lag) + jnp.where(place > 0, held, 0.0)
    inside = pairs(got_ref[jnp.maximum(place - 1, 0)].astype(F32), states + 2 * lanes, lanes)
    return state, [jnp.where(place > 0, a, b) for a, b in zip(inside, last)]


def near_scan(block, lanes, got_ref, rate_ref, taps_ref, before_ref, message_ref):
    place, _ = places()
    states = rate_ref.shape[0]
    rates = rate_ref[...]
    run = got_ref[0].astype(F32)
    head = run[states : states + 2 * lanes]
    total, last = run[:states], pairs(run, states + 2 * lanes, lanes)
    before = jnp.where(place == 1, total, jnp.zeros_like(total))
    for j in range(1, NEAR):
        total, last = step_over(block, lanes, rates, taps_ref, total, last, got_ref[j].astype(F32))
        if j < NEAR - 1:
            before = jnp.where(place == j + 1, total, before)
    before_ref[...] = before
    message_ref[:states] = total
    message_ref[states : states + 2 * lanes] = head
    message_ref[states + 2 * lanes : states + 3 * lanes] = last[0]
    message_ref[states + 3 * lanes :] = last[1]


def relay(block, lanes, came_ref, own_ref, rate_ref, taps_ref, after_ref, out_ref):
    rates = rate_ref[...]
    states = rates.shape[0]
    low = places()[1] == 0
    own, came = own_ref[...], came_ref[...]
    state, last = jnp.zeros_like(rates), [jnp.zeros((lanes, LANES), F32)] * 2
    for run in (jnp.where(low, own, came), jnp.where(low, came, own)):
        state, last = step_over(block, lanes, rates, taps_ref, state, last, run)
    out_ref[:states] = state
    out_ref[pl.ds(states, lanes)] = last[0]
    out_ref[pl.ds(states + lanes, lanes)] = last[1]
    rest = states + 2 * lanes
    out_ref[rest:] = jnp.zeros((out_ref.shape[0] - rest, LANES), F32)


def add_mode(totals, term, rate):
    step = jnp.broadcast_to(jnp.exp(-SUB * rate), term.shape)
    out = []
    for total in totals:
        out.append(total + term)
        term = term * step
    return out


def inner_conv(rate_ref, residue_ref, product_ref, local_ref, filter_ref):
    count, chans = product_ref.shape
    modes = rate_ref.shape[0]
    blocks = count // SUB
    row = lax.broadcasted_iota(jnp.int32, (SUB, LANES), 0)
    lead = row.astype(F32)

    def one_lane(lane, carry):
        at = pl.ds(pl.multiple_of(lane * LANES, LANES), LANES)
        zero = jnp.zeros((SUB, LANES), F32)
        totals = [zero] * blocks
        for mode in range(modes):
            rate = rate_ref[pl.ds(mode, 1), at]
            term = residue_ref[pl.ds(mode, 1), at] * jnp.exp(-rate * lead)
            totals = add_mode(totals, term, rate)
        for i in range(blocks):
            filter_ref[pl.ds(i * SUB, SUB), :] = totals[i]

        shifted = [product_ref[pl.ds(i * SUB, SUB), at] for i in range(blocks)]
        totals = [zero] * blocks
        for b in range(SUB):
            for a in range(blocks):
                weight = filter_ref[pl.ds(a * SUB + b, 1), :]
                for j in range(blocks - a):
                    totals[j + a] = totals[j + a] + weight * shifted[j]
            if b < SUB - 1:
                rolled = [pltpu.roll(s, 1, 0) for s in shifted]
                shifted = [jnp.where(row == 0, before, now) for before, now in zip([zero] + rolled[:-1], rolled)]
        for i in range(blocks):
            local_ref[pl.ds(i * SUB, SUB), at] = totals[i]
        return carry

    lax.fori_loop(0, chans // LANES, one_lane, 0)


def finish(state, last, got_ref, before_ref, rate_pack, residue_pack, taps_ref, rate_ref, query_ref, local_ref, mixed_ref, state_ref):
    count, chans = local_ref.shape
    lanes = chans // LANES
    modes = rate_ref.shape[0]
    states = lanes * modes
    blocks = count // SUB
    place, _ = places()
    rates = rate_pack[...]
    state, own_last = step_into(count, lanes, place, rates, taps_ref, state, last, got_ref, before_ref)
    own_head = pairs(got_ref[place].astype(F32), states, lanes)
    own_query = [q.astype(BF16).astype(F32) for q in first_rows(taps_ref, 0, own_last, own_head)]
    first, second = first_products(taps_ref, own_last, own_head)
    ahead = jnp.exp(rates) * spread(second, modes)
    state = state * jnp.exp(-rates) + spread(first, modes) + ahead
    state = state * residue_pack[...]
    ahead = ahead * residue_pack[...]
    extra = [jnp.sum(ahead[l * modes : (l + 1) * modes], axis=0, keepdims=True) for l in range(lanes)]
    row = lax.broadcasted_iota(jnp.int32, (SUB, LANES), 0)
    lead = row.astype(F32)
    for l in range(lanes):
        state_ref[:modes, pl.ds(l * LANES, LANES)] = state[l * modes : (l + 1) * modes]
        take = jnp.where(row == 0, jnp.broadcast_to(extra[l], row.shape), 0.0)
        query = jnp.where(row == 0, own_query[0][l : l + 1], jnp.where(row == 1, own_query[1][l : l + 1], 0.0))
        state_ref[modes : modes + SUB, pl.ds(l * LANES, LANES)] = take
        state_ref[modes + SUB :, pl.ds(l * LANES, LANES)] = query
    rows = lax.broadcasted_iota(jnp.int32, (2 * SUB, LANES), 0)

    def one_lane(lane, carry):
        at = pl.ds(pl.multiple_of(lane * LANES, LANES), LANES)
        totals = [local_ref[pl.ds(i * SUB, SUB), at] for i in range(blocks)]
        for mode in range(modes):
            rate = rate_ref[pl.ds(mode, 1), at]
            term = state_ref[pl.ds(mode, 1), at] * jnp.exp(-rate * lead)
            totals = add_mode(totals, term, rate)
        totals[0] = totals[0] - state_ref[pl.ds(modes, SUB), at]
        for i in range(0, blocks, 2):
            where = pl.ds(i * SUB, 2 * SUB)
            conv = jnp.concatenate(totals[i : i + 2], axis=0).astype(BF16).astype(F32)
            query = query_ref[where, at].astype(F32)
            if i == 0:
                fixed = state_ref[pl.ds(modes + SUB, SUB), at]
                query = jnp.where(rows < 2, jnp.concatenate([fixed, fixed], axis=0), query)
            mixed_ref[where, at] = (query * conv).astype(BF16)
        return carry

    lax.fori_loop(0, lanes, one_lane, 0)


def early(got_ref, before_ref, rate_pack, residue_pack, taps_ref, rate_ref, query_ref, residue_ref, product_ref, local_ref, out_ref, filter_ref, state_ref, mixed_ref, sem):
    _, group = places()

    @pl.when(group < 2)
    def _():
        inner_conv(rate_ref, residue_ref, product_ref, local_ref, filter_ref)

    @pl.when(group == 0)
    def _():
        nothing = jnp.zeros(rate_pack.shape, F32)
        last = [jnp.zeros((taps_ref.shape[0] // 9, LANES), F32)] * 2
        finish(nothing, last, got_ref, before_ref, rate_pack, residue_pack, taps_ref, rate_ref, query_ref, local_ref, mixed_ref, state_ref)
        copy = pltpu.make_async_copy(mixed_ref, out_ref, sem)
        copy.start()
        copy.wait()


def later(rate_ref, residue_ref, product_ref, after_ref, held_ref, local_ref, filter_ref):
    @pl.when(places()[1] >= 2)
    def _():
        inner_conv(rate_ref, residue_ref, product_ref, local_ref, filter_ref)


def final(got_ref, before_ref, rate_pack, residue_pack, taps_ref, rate_ref, query_ref, local_ref, swap_ref, two_ref, third_ref, held_ref, out_ref, state_ref, mixed_ref, sem):
    _, group = places()
    block = local_ref.shape[0] * NEAR
    states = rate_pack.shape[0]
    lanes = taps_ref.shape[0] // 9

    @pl.when(group > 0)
    def _():
        came = two_ref[...]
        state, last = came[:states], (came[states : states + lanes], came[states + lanes : states + 2 * lanes])
        run = jnp.where(group == 1, swap_ref[...], third_ref[...])
        after, after_last = step_over(block, lanes, rate_pack[...], taps_ref, state, last, run)
        odd = group % 2 == 1
        state, last = jnp.where(odd, after, state), [jnp.where(odd, a, b) for a, b in zip(after_last, last)]
        finish(state, last, got_ref, before_ref, rate_pack, residue_pack, taps_ref, rate_ref, query_ref, local_ref, mixed_ref, state_ref)
        copy = pltpu.make_async_copy(mixed_ref, out_ref, sem)
        copy.start()
        copy.wait()


def places():
    index = lax.axis_index("ctx")
    return index % NEAR, index // NEAR


def gather(copies, axis, groups=None):
    return lax.all_to_all(copies, axis, 0, 0, tiled=True, axis_index_groups=groups)


def per_device(stream, norm_gain, short_filter, decay_rate, residue):
    count, chans = stream.shape
    modes = decay_rate.shape[1]
    lanes = chans // LANES
    states = lanes * modes
    peers = lax.axis_size("ch")
    ctx = lax.axis_size("ctx")
    groups = [[g + m for m in range(NEAR)] for g in range(0, ctx, NEAR)]

    held = [stream, norm_gain[None, :], short_filter, decay_rate.T, residue.T]
    held = [pltpu.with_memory_space_constraint(h, pltpu.HBM) for h in held]
    stream, gain, taps, rates, weights, sums, taps_pack, rate_pack, residue_pack = call(
        square_sums,
        [(h.shape, h.dtype) for h in held]
        + [((peers, 1, count), F32), ((9 * lanes, LANES), F32), ((states, LANES), F32), ((states, LANES), F32)],
        *held,
        scratch=[pltpu.SemaphoreType.DMA((len(held),))],
        space=pltpu.HBM,
    )
    sums = gather(sums, "ch")
    query, product, message = call(
        lambda *refs: block_states(chans * peers, *refs),
        [((count, chans), BF16), ((count, chans), F32), ((NEAR, states + 4 * lanes, LANES), BF16)],
        sums, stream, gain, taps, rates,
        scratch=[pltpu.VMEM((SUB + count, chans), F32), pltpu.VMEM((modes, chans), F32), pltpu.VMEM((states + 4 * lanes, LANES), F32)],
    )
    near = gather(message, "ctx", groups)
    near_before, message = call(
        lambda *refs: near_scan(count, lanes, *refs),
        [((states, LANES), F32), ((states + 4 * lanes, LANES), F32)],
        near, rate_pack, taps_pack,
    )
    hops = lambda *ends: [pair for a, b in ends for pair in zip(groups[a], groups[b])]
    swap = lax.ppermute(message, "ctx", hops((0, 1), (1, 0)))
    common = [near, near_before, rate_pack, residue_pack, taps_pack, rates, query]
    work = [pltpu.VMEM((modes + 2 * SUB, chans), F32), pltpu.VMEM((count, chans), BF16), pltpu.SemaphoreType.DMA]
    local, mixed = call(
        early,
        [((count, chans), F32), ((count, chans), BF16)],
        *common, weights, product,
        scratch=[pltpu.VMEM((count, LANES), F32)] + work, flops=10**7, out_hbm=(1,),
    )
    (two,) = call(
        lambda *refs: relay(count * NEAR, lanes, *refs),
        [((states + 6 * lanes, LANES), F32)],
        swap, message, rate_pack, taps_pack, local,
    )
    third, relayed = lax.optimization_barrier((message, two))
    third = lax.ppermute(third, "ctx", hops((2, 3)))
    two = lax.ppermute(relayed, "ctx", hops((0, 3), (1, 2)))
    (local,) = call(
        later, [((count, chans), F32)], rates, weights, product, relayed, local,
        scratch=[pltpu.VMEM((count, LANES), F32)], flops=10**7, aliases={4: 0},
    )
    (mixed,) = call(
        final,
        [((count, chans), BF16)],
        *common, local, swap, two, third, mixed,
        scratch=work, in_hbm=(11,), out_hbm=(0,), aliases={11: 0},
    )
    return mixed


def solution(mesh):
    in_specs = (P("ctx", "ch"), P("ch"), P(None, None, "ch"), P("ch", None), P("ch", None))
    out_specs = P("ctx", "ch")
    return jax.shard_map(
        per_device, mesh=mesh, in_specs=in_specs, out_specs=out_specs, check_vma=False
    )
```

```python
import jax
import jax.numpy as jnp
from jax import lax
from jax.experimental import pallas as pl
from jax.experimental.pallas import tpu as pltpu
from jax.sharding import PartitionSpec as P

EXACT = lax.Precision.HIGHEST
EPSILON = 1e-05
SUB = 8
LANES = 128
NEAR = 16

F32 = jnp.float32
BF16 = jnp.bfloat16


def call(body, outs, *args, scratch=(), flops=0, space=pltpu.VMEM, in_hbm=(), out_hbm=(), aliases=None):
    shapes = [jax.ShapeDtypeStruct(s, d) for s, d in outs]
    spaces = [pltpu.HBM if i in in_hbm else space for i in range(len(args))]
    out_spaces = [pltpu.HBM if i in out_hbm else pltpu.VMEM for i in range(len(outs))]
    moved = sum(a.size * a.dtype.itemsize for a in args)
    return pl.pallas_call(
        body,
        out_shape=shapes,
        in_specs=[pl.BlockSpec(memory_space=m) for m in spaces],
        out_specs=[pl.BlockSpec(memory_space=m) for m in out_spaces],
        scratch_shapes=list(scratch),
        input_output_aliases=aliases or {},
        compiler_params=pltpu.CompilerParams(vmem_limit_bytes=16 * 2**20),
        cost_estimate=pl.CostEstimate(flops=flops, bytes_accessed=moved, transcendentals=0),
    )(*args)


def pack(ref):
    return jnp.concatenate([ref[:, l * LANES : (l + 1) * LANES] for l in range(ref.shape[1] // LANES)], axis=0)


def exact_parts(values, count):
    parts = []
    for _ in range(count):
        parts.append(values.astype(BF16))
        values = values - parts[-1].astype(F32)
    return parts


def square_sums(*refs):
    count = 5
    held, refs = refs[:count], refs[count:]
    (stream_ref, gain_ref, taps_ref, rate_ref, residue_ref), refs = refs[:count], refs[count:]
    sums_ref, taps_pack, rate_pack, residue_pack, sem = refs
    copies = [pltpu.make_async_copy(held[i], out, sem.at[i]) for i, out in enumerate((stream_ref, gain_ref, taps_ref, rate_ref, residue_ref))]
    for copy in copies:
        copy.start()
    for copy in copies:
        copy.wait()
    chans = stream_ref.shape[1]
    values = stream_ref[...].astype(F32)
    sums = jnp.zeros((SUB, values.shape[0]), F32)
    for part in exact_parts(values * values, 2):
        sums = sums + lax.dot_general(jnp.ones((SUB, chans), BF16), part, (((1,), (1,)), ((), ())), preferred_element_type=F32)
    for peer in range(sums_ref.shape[0]):
        sums_ref[peer] = sums[:1]
    rate_pack[...] = pack(rate_ref)
    residue_pack[...] = pack(residue_ref)
    lanes = chans // LANES
    for tap in range(3):
        for role in range(3):
            for l in range(lanes):
                taps_pack[pl.ds((tap * 3 + role) * lanes + l, 1), :] = taps_ref[tap, pl.ds(role, 1), pl.ds(l * LANES, LANES)]


def block_states(chan_total, sums_ref, stream_ref, gain_ref, taps_ref, rate_ref, query_ref, product_ref, message_ref, normed_ref, end_ref, whole_ref):
    count, chans = stream_ref.shape
    lanes = chans // LANES
    modes = rate_ref.shape[0]
    sums = sums_ref[0]
    for peer in range(1, sums_ref.shape[0]):
        sums = sums + sums_ref[peer]
    scale = lax.rsqrt(sums / chan_total + EPSILON)
    parts = exact_parts(jnp.broadcast_to(scale, (2 * SUB, count)), 3)
    ones = jnp.full((2 * SUB, chans), 1.0 / (2 * SUB), BF16)
    scale = jnp.zeros((count, chans), F32)
    for part in parts:
        scale = scale + lax.dot_general(part, ones, (((0,), (0,)), ((), ())), preferred_element_type=F32)
    values = stream_ref[...].astype(F32) * scale * gain_ref[...]
    normed_ref[:SUB] = jnp.zeros((SUB, chans), F32)
    normed_ref[SUB:] = values.astype(BF16).astype(F32)
    shifted = [normed_ref[SUB - j : SUB - j + count] for j in range(3)]

    def feature(role):
        total = taps_ref[0, pl.ds(role, 1)] * shifted[0]
        total = total + taps_ref[1, pl.ds(role, 1)] * shifted[1]
        return total + taps_ref[2, pl.ds(role, 1)] * shifted[2]

    query_ref[...] = feature(0).astype(BF16)
    product_ref[...] = (feature(1) * feature(2)).astype(BF16).astype(F32)
    row = lax.broadcasted_iota(jnp.int32, (SUB, chans), 0)
    product_ref[:SUB] = jnp.where(row < 2, 0.0, product_ref[:SUB])

    lag = (SUB - 1 - lax.broadcasted_iota(jnp.int32, (SUB, LANES), 0)).astype(F32)

    def one_lane(lane, carry):
        at = pl.ds(pl.multiple_of(lane * LANES, LANES), LANES)
        blocks = [product_ref[pl.ds(i * SUB, SUB), at] for i in range(count // SUB)]
        for mode in range(modes):
            rate = rate_ref[pl.ds(mode, 1), at]
            step = jnp.broadcast_to(jnp.exp(-SUB * rate), (SUB, LANES))
            total = blocks[0]
            for block in blocks[1:]:
                total = total * step + block
            end_ref[pl.ds(mode, 1), at] = jnp.sum(total * jnp.exp(-rate * lag), axis=0, keepdims=True)
        return carry

    lax.fori_loop(0, lanes, one_lane, 0)
    whole_ref[: lanes * modes] = pack(end_ref)
    for e, place in enumerate((0, 1, count - 2, count - 1)):
        for l in range(lanes):
            whole_ref[pl.ds(lanes * (modes + e) + l, 1), :] = normed_ref[pl.ds(SUB + place, 1), pl.ds(l * LANES, LANES)]
    message = whole_ref[...].astype(BF16)
    for peer in range(message_ref.shape[0]):
        message_ref[peer] = message


def first_rows(taps_ref, role, last, head):
    lanes = taps_ref.shape[0] // 9
    taps = [taps_ref[pl.ds((3 * j + role) * lanes, lanes)] for j in range(3)]
    first = taps[0] * head[0] + taps[1] * last[1] + taps[2] * last[0]
    second = taps[0] * head[1] + taps[1] * head[0] + taps[2] * last[1]
    return first, second


def first_products(taps_ref, last, head):
    keys, values = first_rows(taps_ref, 1, last, head), first_rows(taps_ref, 2, last, head)
    return [(k * v).astype(BF16).astype(F32) for k, v in zip(keys, values)]


def spread(rows, modes):
    return jnp.concatenate([jnp.broadcast_to(rows[l : l + 1], (modes, LANES)) for l in range(rows.shape[0])], axis=0)


def pairs(ref, start, lanes):
    return ref[start : start + lanes], ref[start + lanes : start + 2 * lanes]


def step_over(block, lanes, rates, taps_ref, state, last, run):
    states = rates.shape[0]
    modes = states // lanes
    first, second = first_products(taps_ref, last, pairs(run, states, lanes))
    end = run[:states] + state * jnp.exp(-block * rates)
    end = end + jnp.exp(-(block - 1) * rates) * spread(first, modes) + jnp.exp(-(block - 2) * rates) * spread(second, modes)
    return end, pairs(run, states + 2 * lanes, lanes)


def step_into(block, lanes, place, rates, taps_ref, state, last, got_ref, before_ref):
    states = rates.shape[0]
    modes = states // lanes
    first, second = first_products(taps_ref, last, pairs(got_ref[0].astype(F32), states, lanes))
    lag = (block * place).astype(F32)
    held = jnp.exp(-rates * jnp.maximum(lag - 1.0, 0.0)) * spread(first, modes)
    held = held + jnp.exp(-rates * jnp.maximum(lag - 2.0, 0.0)) * spread(second, modes)
    state = before_ref[...] + state * jnp.exp(-rates * lag) + jnp.where(place > 0, held, 0.0)
    inside = pairs(got_ref[jnp.maximum(place - 1, 0)].astype(F32), states + 2 * lanes, lanes)
    return state, [jnp.where(place > 0, a, b) for a, b in zip(inside, last)]


def near_scan(block, lanes, got_ref, rate_ref, taps_ref, before_ref, message_ref):
    place, _ = places()
    states = rate_ref.shape[0]
    rates = rate_ref[...]
    run = got_ref[0].astype(F32)
    head = run[states : states + 2 * lanes]
    total, last = run[:states], pairs(run, states + 2 * lanes, lanes)
    before = jnp.where(place == 1, total, jnp.zeros_like(total))
    for j in range(1, NEAR):
        total, last = step_over(block, lanes, rates, taps_ref, total, last, got_ref[j].astype(F32))
        if j < NEAR - 1:
            before = jnp.where(place == j + 1, total, before)
    before_ref[...] = before
    message_ref[...] = jnp.concatenate([total, head, *last], axis=0).astype(BF16)


def relay(block, lanes, came_ref, own_ref, rate_ref, taps_ref, after_ref, out_ref):
    rates = rate_ref[...]
    states = rates.shape[0]
    low = places()[1] == 0
    own, came = own_ref[...].astype(F32), came_ref[...].astype(F32)
    state, last = jnp.zeros_like(rates), [jnp.zeros((lanes, LANES), F32)] * 2
    for run in (jnp.where(low, own, came), jnp.where(low, came, own)):
        state, last = step_over(block, lanes, rates, taps_ref, state, last, run)
    rest = jnp.zeros((out_ref.shape[0] - states - 2 * lanes, LANES), F32)
    out_ref[...] = jnp.concatenate([state, *last, rest], axis=0).astype(BF16)


def add_mode(totals, term, rate):
    step = jnp.broadcast_to(jnp.exp(-SUB * rate), term.shape)
    out = []
    for total in totals:
        out.append(total + term)
        term = term * step
    return out


def inner_conv(rate_ref, residue_ref, product_ref, local_ref, filter_ref):
    count, chans = product_ref.shape
    modes = rate_ref.shape[0]
    blocks = count // SUB
    row = lax.broadcasted_iota(jnp.int32, (SUB, LANES), 0)
    lead = row.astype(F32)

    def one_lane(lane, carry):
        at = pl.ds(pl.multiple_of(lane * LANES, LANES), LANES)
        zero = jnp.zeros((SUB, LANES), F32)
        totals = [zero] * blocks
        for mode in range(modes):
            rate = rate_ref[pl.ds(mode, 1), at]
            term = residue_ref[pl.ds(mode, 1), at] * jnp.exp(-rate * lead)
            totals = add_mode(totals, term, rate)
        for i in range(blocks):
            filter_ref[pl.ds(i * SUB, SUB), :] = totals[i]

        shifted = [product_ref[pl.ds(i * SUB, SUB), at] for i in range(blocks)]
        totals = [zero] * blocks
        for b in range(SUB):
            for a in range(blocks):
                weight = filter_ref[pl.ds(a * SUB + b, 1), :]
                for j in range(blocks - a):
                    totals[j + a] = totals[j + a] + weight * shifted[j]
            if b < SUB - 1:
                rolled = [pltpu.roll(s, 1, 0) for s in shifted]
                shifted = [jnp.where(row == 0, before, now) for before, now in zip([zero] + rolled[:-1], rolled)]
        for i in range(blocks):
            local_ref[pl.ds(i * SUB, SUB), at] = totals[i]
        return carry

    lax.fori_loop(0, chans // LANES, one_lane, 0)


def finish(state, last, got_ref, before_ref, rate_pack, residue_pack, taps_ref, rate_ref, query_ref, local_ref, mixed_ref, state_ref):
    count, chans = local_ref.shape
    lanes = chans // LANES
    modes = rate_ref.shape[0]
    states = lanes * modes
    blocks = count // SUB
    place, _ = places()
    rates = rate_pack[...]
    state, own_last = step_into(count, lanes, place, rates, taps_ref, state, last, got_ref, before_ref)
    own_head = pairs(got_ref[place].astype(F32), states, lanes)
    own_query = [q.astype(BF16).astype(F32) for q in first_rows(taps_ref, 0, own_last, own_head)]
    first, second = first_products(taps_ref, own_last, own_head)
    ahead = jnp.exp(rates) * spread(second, modes)
    state = state * jnp.exp(-rates) + spread(first, modes) + ahead
    state = state * residue_pack[...]
    ahead = ahead * residue_pack[...]
    extra = [jnp.sum(ahead[l * modes : (l + 1) * modes], axis=0, keepdims=True) for l in range(lanes)]
    row = lax.broadcasted_iota(jnp.int32, (SUB, LANES), 0)
    lead = row.astype(F32)
    for l in range(lanes):
        state_ref[:modes, pl.ds(l * LANES, LANES)] = state[l * modes : (l + 1) * modes]
        take = jnp.where(row == 0, jnp.broadcast_to(extra[l], row.shape), 0.0)
        query = jnp.where(row == 0, own_query[0][l : l + 1], jnp.where(row == 1, own_query[1][l : l + 1], 0.0))
        state_ref[modes : modes + SUB, pl.ds(l * LANES, LANES)] = take
        state_ref[modes + SUB :, pl.ds(l * LANES, LANES)] = query
    rows = lax.broadcasted_iota(jnp.int32, (2 * SUB, LANES), 0)

    def one_lane(lane, carry):
        at = pl.ds(pl.multiple_of(lane * LANES, LANES), LANES)
        totals = [local_ref[pl.ds(i * SUB, SUB), at] for i in range(blocks)]
        for mode in range(modes):
            rate = rate_ref[pl.ds(mode, 1), at]
            term = state_ref[pl.ds(mode, 1), at] * jnp.exp(-rate * lead)
            totals = add_mode(totals, term, rate)
        totals[0] = totals[0] - state_ref[pl.ds(modes, SUB), at]
        for i in range(0, blocks, 2):
            where = pl.ds(i * SUB, 2 * SUB)
            conv = jnp.concatenate(totals[i : i + 2], axis=0).astype(BF16).astype(F32)
            query = query_ref[where, at].astype(F32)
            if i == 0:
                fixed = state_ref[pl.ds(modes + SUB, SUB), at]
                query = jnp.where(rows < 2, jnp.concatenate([fixed, fixed], axis=0), query)
            mixed_ref[where, at] = (query * conv).astype(BF16)
        return carry

    lax.fori_loop(0, lanes, one_lane, 0)


def early(got_ref, before_ref, rate_pack, residue_pack, taps_ref, rate_ref, query_ref, residue_ref, product_ref, local_ref, out_ref, filter_ref, state_ref, mixed_ref, sem):
    _, group = places()

    @pl.when(group < 2)
    def _():
        inner_conv(rate_ref, residue_ref, product_ref, local_ref, filter_ref)

    @pl.when(group == 0)
    def _():
        nothing = jnp.zeros(rate_pack.shape, F32)
        last = [jnp.zeros((taps_ref.shape[0] // 9, LANES), F32)] * 2
        finish(nothing, last, got_ref, before_ref, rate_pack, residue_pack, taps_ref, rate_ref, query_ref, local_ref, mixed_ref, state_ref)
        copy = pltpu.make_async_copy(mixed_ref, out_ref, sem)
        copy.start()
        copy.wait()


def later(rate_ref, residue_ref, product_ref, after_ref, held_ref, local_ref, filter_ref):
    @pl.when(places()[1] >= 2)
    def _():
        inner_conv(rate_ref, residue_ref, product_ref, local_ref, filter_ref)


def final(got_ref, before_ref, rate_pack, residue_pack, taps_ref, rate_ref, query_ref, local_ref, swap_ref, two_ref, third_ref, held_ref, out_ref, state_ref, mixed_ref, sem):
    _, group = places()
    block = local_ref.shape[0] * NEAR
    states = rate_pack.shape[0]
    lanes = taps_ref.shape[0] // 9

    @pl.when(group > 0)
    def _():
        came = two_ref[...].astype(F32)
        state, last = came[:states], (came[states : states + lanes], came[states + lanes : states + 2 * lanes])
        run = jnp.where(group == 1, swap_ref[...].astype(F32), third_ref[...].astype(F32))
        after, after_last = step_over(block, lanes, rate_pack[...], taps_ref, state, last, run)
        odd = group % 2 == 1
        state, last = jnp.where(odd, after, state), [jnp.where(odd, a, b) for a, b in zip(after_last, last)]
        finish(state, last, got_ref, before_ref, rate_pack, residue_pack, taps_ref, rate_ref, query_ref, local_ref, mixed_ref, state_ref)
        copy = pltpu.make_async_copy(mixed_ref, out_ref, sem)
        copy.start()
        copy.wait()


def places():
    index = lax.axis_index("ctx")
    return index % NEAR, index // NEAR


def gather(copies, axis, groups=None):
    return lax.all_to_all(copies, axis, 0, 0, tiled=True, axis_index_groups=groups)


def per_device(stream, norm_gain, short_filter, decay_rate, residue):
    count, chans = stream.shape
    modes = decay_rate.shape[1]
    lanes = chans // LANES
    states = lanes * modes
    peers = lax.axis_size("ch")
    ctx = lax.axis_size("ctx")
    groups = [[g + m for m in range(NEAR)] for g in range(0, ctx, NEAR)]

    held = [stream, norm_gain[None, :], short_filter, decay_rate.T, residue.T]
    held = [pltpu.with_memory_space_constraint(h, pltpu.HBM) for h in held]
    stream, gain, taps, rates, weights, sums, taps_pack, rate_pack, residue_pack = call(
        square_sums,
        [(h.shape, h.dtype) for h in held]
        + [((peers, 1, count), F32), ((9 * lanes, LANES), F32), ((states, LANES), F32), ((states, LANES), F32)],
        *held,
        scratch=[pltpu.SemaphoreType.DMA((len(held),))],
        space=pltpu.HBM,
    )
    sums = gather(sums, "ch")
    query, product, message = call(
        lambda *refs: block_states(chans * peers, *refs),
        [((count, chans), BF16), ((count, chans), F32), ((NEAR, states + 4 * lanes, LANES), BF16)],
        sums, stream, gain, taps, rates,
        scratch=[pltpu.VMEM((SUB + count, chans), F32), pltpu.VMEM((modes, chans), F32), pltpu.VMEM((states + 4 * lanes, LANES), F32)],
    )
    near = gather(message, "ctx", groups)
    near_before, message = call(
        lambda *refs: near_scan(count, lanes, *refs),
        [((states, LANES), F32), ((states + 4 * lanes, LANES), BF16)],
        near, rate_pack, taps_pack,
    )
    hops = lambda *ends: [pair for a, b in ends for pair in zip(groups[a], groups[b])]
    swap = lax.ppermute(message, "ctx", hops((0, 1), (1, 0)))
    common = [near, near_before, rate_pack, residue_pack, taps_pack, rates, query]
    work = [pltpu.VMEM((modes + 2 * SUB, chans), F32), pltpu.VMEM((count, chans), BF16), pltpu.SemaphoreType.DMA]
    local, mixed = call(
        early,
        [((count, chans), F32), ((count, chans), BF16)],
        *common, weights, product,
        scratch=[pltpu.VMEM((count, LANES), F32)] + work, flops=10**7, out_hbm=(1,),
    )
    (two,) = call(
        lambda *refs: relay(count * NEAR, lanes, *refs),
        [((states + 8 * lanes, LANES), BF16)],
        swap, message, rate_pack, taps_pack, local,
    )
    third, relayed = lax.optimization_barrier((message, two))
    third = lax.ppermute(third, "ctx", hops((2, 3)))
    two = lax.ppermute(relayed, "ctx", hops((0, 3), (1, 2)))
    (local,) = call(
        later, [((count, chans), F32)], rates, weights, product, relayed, local,
        scratch=[pltpu.VMEM((count, LANES), F32)], flops=10**7, aliases={4: 0},
    )
    (mixed,) = call(
        final,
        [((count, chans), BF16)],
        *common, local, swap, two, third, mixed,
        scratch=work, in_hbm=(11,), out_hbm=(0,), aliases={11: 0},
    )
    return mixed


def solution(mesh):
    in_specs = (P("ctx", "ch"), P("ch"), P(None, None, "ch"), P("ch", None), P("ch", None))
    out_specs = P("ctx", "ch")
    return jax.shard_map(
        per_device, mesh=mesh, in_specs=in_specs, out_specs=out_specs, check_vma=False
    )
```

```python
import jax
import jax.numpy as jnp
from jax import lax
from jax.experimental import pallas as pl
from jax.experimental.pallas import tpu as pltpu
from jax.sharding import PartitionSpec as P

EXACT = lax.Precision.HIGHEST
EPSILON = 1e-05
SUB = 8
LANES = 128
NEAR = 16

F32 = jnp.float32
BF16 = jnp.bfloat16


def call(body, outs, *args, scratch=(), flops=0, space=pltpu.VMEM, in_hbm=(), out_hbm=(), aliases=None):
    shapes = [jax.ShapeDtypeStruct(s, d) for s, d in outs]
    spaces = [pltpu.HBM if i in in_hbm else space for i in range(len(args))]
    out_spaces = [pltpu.HBM if i in out_hbm else pltpu.VMEM for i in range(len(outs))]
    moved = sum(a.size * a.dtype.itemsize for a in args)
    return pl.pallas_call(
        body,
        out_shape=shapes,
        in_specs=[pl.BlockSpec(memory_space=m) for m in spaces],
        out_specs=[pl.BlockSpec(memory_space=m) for m in out_spaces],
        scratch_shapes=list(scratch),
        input_output_aliases=aliases or {},
        compiler_params=pltpu.CompilerParams(vmem_limit_bytes=16 * 2**20),
        cost_estimate=pl.CostEstimate(flops=flops, bytes_accessed=moved, transcendentals=0),
    )(*args)


def pack(ref):
    return jnp.concatenate([ref[:, l * LANES : (l + 1) * LANES] for l in range(ref.shape[1] // LANES)], axis=0)


def square_sums(*refs):
    count = 5
    held, outs, refs = refs[:count], refs[count : 2 * count], refs[2 * count :]
    sums_ref, taps_pack, rate_pack, residue_pack, sem = refs
    copies = [pltpu.make_async_copy(source, target, sem.at[i]) for i, (source, target) in enumerate(zip(held, outs))]
    for copy in copies:
        copy.start()
    copies[0].wait()
    stream_ref, _, taps_ref, rate_ref, residue_ref = outs
    lanes = stream_ref.shape[1] // LANES
    total = 0.0
    for l in range(lanes):
        values = stream_ref[:, l * LANES : (l + 1) * LANES].astype(F32)
        total = total + values * values
    sums = jnp.sum(total.T, axis=0, keepdims=True)
    for peer in range(sums_ref.shape[0]):
        sums_ref[peer] = sums
    for copy in copies[1:]:
        copy.wait()
    rate_pack[...] = pack(rate_ref)
    residue_pack[...] = pack(residue_ref)
    for tap in range(3):
        for role in range(3):
            for l in range(lanes):
                taps_pack[pl.ds((tap * 3 + role) * lanes + l, 1), :] = taps_ref[tap, pl.ds(role, 1), pl.ds(l * LANES, LANES)]


def block_states(chan_total, sums_ref, stream_ref, gain_ref, taps_ref, rate_ref, query_ref, product_ref, message_ref, edge_ref, end_ref, whole_ref):
    count, chans = stream_ref.shape
    lanes = chans // LANES
    modes = rate_ref.shape[0]
    blocks = count // SUB
    sums = sums_ref[0]
    for peer in range(1, sums_ref.shape[0]):
        sums = sums + sums_ref[peer]
    rest = lax.rsqrt(sums / chan_total + EPSILON)
    rows = lax.broadcasted_iota(jnp.int32, (2 * SUB, count), 0)
    parts = jnp.zeros((2 * SUB, count), F32)
    for i in range(3):
        part = rest.astype(BF16).astype(F32)
        parts = jnp.where(rows == i, part, parts)
        rest = rest - part
    scale = lax.dot_general(
        parts.astype(BF16), jnp.ones((2 * SUB, LANES), BF16), (((0,), (0,)), ((), ())), preferred_element_type=F32
    )
    row = lax.broadcasted_iota(jnp.int32, (SUB, LANES), 0)
    lag = (SUB - 1 - row).astype(F32)

    def one_lane(lane, carry):
        at = pl.ds(pl.multiple_of(lane * LANES, LANES), LANES)
        gain = jnp.broadcast_to(gain_ref[:, at], (SUB, LANES))
        taps = [[jnp.broadcast_to(taps_ref[j, pl.ds(role, 1), at], (SUB, LANES)) for j in range(3)] for role in range(3)]
        before = [jnp.zeros((SUB, LANES), F32)] * 2
        products, queries = [], []
        for i in range(blocks):
            if i % 2 == 0:
                pair = stream_ref[pl.ds(i * SUB, 2 * SUB), at].astype(F32)
            normed = pair[i % 2 * SUB : (i % 2 + 1) * SUB] * scale[i * SUB : (i + 1) * SUB] * gain
            normed = normed.astype(BF16).astype(F32)
            if i == 0:
                edge_ref[:2, at] = normed[:2]
            if i == blocks - 1:
                edge_ref[2:4, at] = normed[SUB - 2 :]
            rolled = [pltpu.roll(normed, j, 0) for j in (1, 2)]
            shifted = [normed] + [jnp.where(row < j, b, r) for j, b, r in zip((1, 2), before, rolled)]
            before = rolled
            query, key, value = [sum(t * n for t, n in zip(taps[role], shifted)) for role in range(3)]
            product = (key * value).astype(BF16).astype(F32)
            if i == 0:
                product = jnp.where(row < 2, 0.0, product)
            product_ref[pl.ds(i * SUB, SUB), at] = product
            products.append(product)
            queries.append(query)
            if i % 2 == 1:
                query_ref[pl.ds((i - 1) * SUB, 2 * SUB), at] = jnp.concatenate(queries[-2:], axis=0).astype(BF16)
        for mode in range(modes):
            rate = rate_ref[pl.ds(mode, 1), at]
            step = jnp.broadcast_to(jnp.exp(-SUB * rate), (SUB, LANES))
            total = products[0]
            for product in products[1:]:
                total = total * step + product
            end_ref[pl.ds(mode, 1), at] = jnp.sum(total * jnp.exp(-rate * lag), axis=0, keepdims=True)
        return carry

    lax.fori_loop(0, lanes, one_lane, 0)
    whole_ref[: lanes * modes] = pack(end_ref)
    for e in range(4):
        for l in range(lanes):
            whole_ref[pl.ds(lanes * (modes + e) + l, 1), :] = edge_ref[pl.ds(e, 1), pl.ds(l * LANES, LANES)]
    message = whole_ref[...].astype(BF16)
    for peer in range(message_ref.shape[0]):
        message_ref[peer] = message


def first_rows(taps_ref, role, last, head):
    lanes = taps_ref.shape[0] // 9
    taps = [taps_ref[pl.ds((3 * j + role) * lanes, lanes)] for j in range(3)]
    first = taps[0] * head[0] + taps[1] * last[1] + taps[2] * last[0]
    second = taps[0] * head[1] + taps[1] * head[0] + taps[2] * last[1]
    return first, second


def first_products(taps_ref, last, head):
    keys, values = first_rows(taps_ref, 1, last, head), first_rows(taps_ref, 2, last, head)
    return [(k * v).astype(BF16).astype(F32) for k, v in zip(keys, values)]


def spread(rows, modes):
    return jnp.concatenate([jnp.broadcast_to(rows[l : l + 1], (modes, LANES)) for l in range(rows.shape[0])], axis=0)


def pairs(ref, start, lanes):
    return ref[start : start + lanes], ref[start + lanes : start + 2 * lanes]


def step_over(block, lanes, rates, taps_ref, state, last, run):
    states = rates.shape[0]
    modes = states // lanes
    first, second = first_products(taps_ref, last, pairs(run, states, lanes))
    end = run[:states] + state * jnp.exp(-block * rates)
    end = end + jnp.exp(-(block - 1) * rates) * spread(first, modes) + jnp.exp(-(block - 2) * rates) * spread(second, modes)
    return end, pairs(run, states + 2 * lanes, lanes)


def step_into(block, lanes, place, rates, taps_ref, state, last, got_ref, before_ref):
    states = rates.shape[0]
    modes = states // lanes
    first, second = first_products(taps_ref, last, pairs(got_ref[0].astype(F32), states, lanes))
    lag = (block * place).astype(F32)
    held = jnp.exp(-rates * jnp.maximum(lag - 1.0, 0.0)) * spread(first, modes)
    held = held + jnp.exp(-rates * jnp.maximum(lag - 2.0, 0.0)) * spread(second, modes)
    state = before_ref[...] + state * jnp.exp(-rates * lag) + jnp.where(place > 0, held, 0.0)
    inside = pairs(got_ref[jnp.maximum(place - 1, 0)].astype(F32), states + 2 * lanes, lanes)
    return state, [jnp.where(place > 0, a, b) for a, b in zip(inside, last)]


def near_scan(block, lanes, got_ref, rate_ref, taps_ref, before_ref, message_ref):
    place, _ = places()
    states = rate_ref.shape[0]
    rates = rate_ref[...]
    run = got_ref[0].astype(F32)
    head = run[states : states + 2 * lanes]
    total, last = run[:states], pairs(run, states + 2 * lanes, lanes)
    before = jnp.where(place == 1, total, jnp.zeros_like(total))
    for j in range(1, NEAR):
        total, last = step_over(block, lanes, rates, taps_ref, total, last, got_ref[j].astype(F32))
        if j < NEAR - 1:
            before = jnp.where(place == j + 1, total, before)
    before_ref[...] = before
    message_ref[...] = jnp.concatenate([total, head, *last], axis=0).astype(BF16)


def relay(block, lanes, came_ref, own_ref, rate_ref, taps_ref, after_ref, out_ref):
    rates = rate_ref[...]
    states = rates.shape[0]
    low = places()[1] == 0
    own, came = own_ref[...].astype(F32), came_ref[...].astype(F32)
    state, last = jnp.zeros_like(rates), [jnp.zeros((lanes, LANES), F32)] * 2
    for run in (jnp.where(low, own, came), jnp.where(low, came, own)):
        state, last = step_over(block, lanes, rates, taps_ref, state, last, run)
    rest = jnp.zeros((out_ref.shape[0] - states - 2 * lanes, LANES), F32)
    out_ref[...] = jnp.concatenate([state, *last, rest], axis=0).astype(BF16)


def add_mode(totals, term, rate):
    step = jnp.broadcast_to(jnp.exp(-SUB * rate), term.shape)
    out = []
    for total in totals:
        out.append(total + term)
        term = term * step
    return out


def inner_conv(rate_ref, residue_ref, product_ref, local_ref, filter_ref):
    count, chans = product_ref.shape
    modes = rate_ref.shape[0]
    blocks = count // SUB
    row = lax.broadcasted_iota(jnp.int32, (SUB, LANES), 0)
    lead = row.astype(F32)

    def one_lane(lane, carry):
        at = pl.ds(pl.multiple_of(lane * LANES, LANES), LANES)
        zero = jnp.zeros((SUB, LANES), F32)
        totals = [zero] * blocks
        for mode in range(modes):
            rate = rate_ref[pl.ds(mode, 1), at]
            term = residue_ref[pl.ds(mode, 1), at] * jnp.exp(-rate * lead)
            totals = add_mode(totals, term, rate)
        for i in range(blocks):
            filter_ref[pl.ds(i * SUB, SUB), :] = totals[i]

        shifted = [product_ref[pl.ds(i * SUB, SUB), at] for i in range(blocks)]
        totals = [zero] * blocks
        for b in range(SUB):
            for a in range(blocks):
                weight = filter_ref[pl.ds(a * SUB + b, 1), :]
                for j in range(blocks - a):
                    totals[j + a] = totals[j + a] + weight * shifted[j]
            if b < SUB - 1:
                rolled = [pltpu.roll(s, 1, 0) for s in shifted]
                shifted = [jnp.where(row == 0, before, now) for before, now in zip([zero] + rolled[:-1], rolled)]
        for i in range(blocks):
            local_ref[pl.ds(i * SUB, SUB), at] = totals[i]
        return carry

    lax.fori_loop(0, chans // LANES, one_lane, 0)


def finish(state, last, got_ref, before_ref, rate_pack, residue_pack, taps_ref, rate_ref, query_ref, local_ref, mixed_ref, state_ref):
    count, chans = local_ref.shape
    lanes = chans // LANES
    modes = rate_ref.shape[0]
    states = lanes * modes
    blocks = count // SUB
    place, _ = places()
    rates = rate_pack[...]
    state, own_last = step_into(count, lanes, place, rates, taps_ref, state, last, got_ref, before_ref)
    own_head = pairs(got_ref[place].astype(F32), states, lanes)
    own_query = [q.astype(BF16).astype(F32) for q in first_rows(taps_ref, 0, own_last, own_head)]
    first, second = first_products(taps_ref, own_last, own_head)
    ahead = jnp.exp(rates) * spread(second, modes)
    state = state * jnp.exp(-rates) + spread(first, modes) + ahead
    state = state * residue_pack[...]
    ahead = ahead * residue_pack[...]
    extra = [jnp.sum(ahead[l * modes : (l + 1) * modes], axis=0, keepdims=True) for l in range(lanes)]
    row = lax.broadcasted_iota(jnp.int32, (SUB, LANES), 0)
    lead = row.astype(F32)
    for l in range(lanes):
        state_ref[:modes, pl.ds(l * LANES, LANES)] = state[l * modes : (l + 1) * modes]
        take = jnp.where(row == 0, jnp.broadcast_to(extra[l], row.shape), 0.0)
        query = jnp.where(row == 0, own_query[0][l : l + 1], jnp.where(row == 1, own_query[1][l : l + 1], 0.0))
        state_ref[modes : modes + SUB, pl.ds(l * LANES, LANES)] = take
        state_ref[modes + SUB :, pl.ds(l * LANES, LANES)] = query
    rows = lax.broadcasted_iota(jnp.int32, (2 * SUB, LANES), 0)

    def one_lane(lane, carry):
        at = pl.ds(pl.multiple_of(lane * LANES, LANES), LANES)
        totals = [local_ref[pl.ds(i * SUB, SUB), at] for i in range(blocks)]
        for mode in range(modes):
            rate = rate_ref[pl.ds(mode, 1), at]
            term = state_ref[pl.ds(mode, 1), at] * jnp.exp(-rate * lead)
            totals = add_mode(totals, term, rate)
        totals[0] = totals[0] - state_ref[pl.ds(modes, SUB), at]
        for i in range(0, blocks, 2):
            where = pl.ds(i * SUB, 2 * SUB)
            conv = jnp.concatenate(totals[i : i + 2], axis=0).astype(BF16).astype(F32)
            query = query_ref[where, at].astype(F32)
            if i == 0:
                fixed = state_ref[pl.ds(modes + SUB, SUB), at]
                query = jnp.where(rows < 2, jnp.concatenate([fixed, fixed], axis=0), query)
            mixed_ref[where, at] = (query * conv).astype(BF16)
        return carry

    lax.fori_loop(0, lanes, one_lane, 0)


def leave(mixed_ref, out_ref, sem):
    copy = pltpu.make_async_copy(mixed_ref, out_ref, sem)
    copy.start()
    copy.wait()


def early_inner(rate_ref, residue_ref, product_ref, after_ref, local_ref, filter_ref):
    @pl.when(places()[1] < 2)
    def _():
        inner_conv(rate_ref, residue_ref, product_ref, local_ref, filter_ref)


def early_output(got_ref, before_ref, rate_pack, residue_pack, taps_ref, rate_ref, query_ref, residue_ref, product_ref, swap_ref, after_ref, held_ref, local_ref, out_ref, filter_ref, state_ref, mixed_ref, sem):
    group = places()[1]

    @pl.when(group >= 2)
    def _():
        inner_conv(rate_ref, residue_ref, product_ref, local_ref, filter_ref)

    @pl.when(group < 2)
    def _():
        rates = rate_pack[...]
        state, last = jnp.zeros_like(rates), [jnp.zeros((taps_ref.shape[0] // 9, LANES), F32)] * 2
        after, after_last = step_over(local_ref.shape[0] * NEAR, len(last[0]), rates, taps_ref, state, last, swap_ref[...].astype(F32))
        state, last = jnp.where(group == 1, after, state), [jnp.where(group == 1, a, b) for a, b in zip(after_last, last)]
        finish(state, last, got_ref, before_ref, rate_pack, residue_pack, taps_ref, rate_ref, query_ref, local_ref, mixed_ref, state_ref)
        leave(mixed_ref, out_ref, sem)


def last_output(got_ref, before_ref, rate_pack, residue_pack, taps_ref, rate_ref, query_ref, local_ref, two_ref, third_ref, held_ref, out_ref, state_ref, mixed_ref, sem):
    group = places()[1]
    states = rate_pack.shape[0]
    lanes = taps_ref.shape[0] // 9

    @pl.when(group >= 2)
    def _():
        came = two_ref[...].astype(F32)
        state, last = came[:states], (came[states : states + lanes], came[states + lanes : states + 2 * lanes])
        after, after_last = step_over(local_ref.shape[0] * NEAR, lanes, rate_pack[...], taps_ref, state, last, third_ref[...].astype(F32))
        odd = group == 3
        state, last = jnp.where(odd, after, state), [jnp.where(odd, a, b) for a, b in zip(after_last, last)]
        finish(state, last, got_ref, before_ref, rate_pack, residue_pack, taps_ref, rate_ref, query_ref, local_ref, mixed_ref, state_ref)
        leave(mixed_ref, out_ref, sem)


def places():
    index = lax.axis_index("ctx")
    return index % NEAR, index // NEAR


def gather(copies, axis, groups=None):
    return lax.all_to_all(copies, axis, 0, 0, tiled=True, axis_index_groups=groups)


def per_device(stream, norm_gain, short_filter, decay_rate, residue):
    count, chans = stream.shape
    modes = decay_rate.shape[1]
    lanes = chans // LANES
    states = lanes * modes
    peers = lax.axis_size("ch")
    ctx = lax.axis_size("ctx")
    groups = [[g + m for m in range(NEAR)] for g in range(0, ctx, NEAR)]

    held = [stream, norm_gain[None, :], short_filter, decay_rate.T, residue.T]
    held = [pltpu.with_memory_space_constraint(h, pltpu.HBM) for h in held]
    stream, gain, taps, rates, weights, sums, taps_pack, rate_pack, residue_pack = call(
        square_sums,
        [(h.shape, h.dtype) for h in held]
        + [((peers, 1, count), F32), ((9 * lanes, LANES), F32), ((states, LANES), F32), ((states, LANES), F32)],
        *held,
        scratch=[pltpu.SemaphoreType.DMA((len(held),))],
        space=pltpu.HBM,
    )
    sums = gather(sums, "ch")
    query, product, message = call(
        lambda *refs: block_states(chans * peers, *refs),
        [((count, chans), BF16), ((count, chans), F32), ((NEAR, states + 4 * lanes, LANES), BF16)],
        sums, stream, gain, taps, rates,
        scratch=[pltpu.VMEM((SUB, chans), F32), pltpu.VMEM((modes, chans), F32), pltpu.VMEM((states + 4 * lanes, LANES), F32)],
    )
    near = gather(message, "ctx", groups)
    near_before, message = call(
        lambda *refs: near_scan(count, lanes, *refs),
        [((states, LANES), F32), ((states + 4 * lanes, LANES), BF16)],
        near, rate_pack, taps_pack,
    )
    outs = [((count, chans), F32), ((count, chans), BF16)]
    common = [near, near_before, rate_pack, residue_pack, taps_pack, rates, query]
    room = [pltpu.VMEM((count, LANES), F32)]
    work = [pltpu.VMEM((modes + 2 * SUB, chans), F32), pltpu.VMEM((count, chans), BF16), pltpu.SemaphoreType.DMA]
    hops = lambda *ends: [pair for a, b in ends for pair in zip(a, b)]
    first, second, third, fourth = groups
    width = NEAR // 4
    turned = [fourth[NEAR - width * (i // width + 1) + i % width] for i in range(NEAR)]
    swap = lax.ppermute(message, "ctx", hops((first, second), (second, first)))
    (local,) = call(early_inner, outs[:1], rates, weights, product, near_before, scratch=room, flops=10**7)
    (two,) = call(
        lambda *refs: relay(count * NEAR, lanes, *refs),
        [((states + 8 * lanes, LANES), BF16)],
        swap, message, rate_pack, taps_pack, local,
    )
    message, relayed = lax.optimization_barrier((message, two))
    three = lax.ppermute(message, "ctx", hops((third, fourth)))
    two = lax.ppermute(relayed, "ctx", hops((first, turned), (second, third)))
    local, mixed = call(
        early_output, outs, *common, weights, product, swap, relayed, local,
        scratch=room + work, flops=10**7, out_hbm=(1,), aliases={11: 0},
    )
    (mixed,) = call(
        last_output, outs[1:], *common, local, two, three, mixed,
        scratch=work, in_hbm=(10,), out_hbm=(0,), aliases={10: 0},
    )
    return mixed


def solution(mesh):
    in_specs = (P("ctx", "ch"), P("ch"), P(None, None, "ch"), P("ch", None), P("ch", None))
    out_specs = P("ctx", "ch")
    return jax.shard_map(
        per_device, mesh=mesh, in_specs=in_specs, out_specs=out_specs, check_vma=False
    )
```

```python
import jax
import jax.numpy as jnp
from jax import lax
from jax.experimental import pallas as pl
from jax.experimental.pallas import tpu as pltpu
from jax.sharding import PartitionSpec as P

EXACT = lax.Precision.HIGHEST
EPSILON = 1e-05
SUB = 8
LANES = 128
WIDE = 16
NEAR = 8

F32 = jnp.float32
BF16 = jnp.bfloat16


def call(body, outs, *args, scratch=(), flops=0, space=pltpu.VMEM, in_hbm=(), out_hbm=(), aliases=None):
    shapes = [jax.ShapeDtypeStruct(s, d) for s, d in outs]
    spaces = [pltpu.HBM if i in in_hbm else space for i in range(len(args))]
    out_spaces = [pl.ANY if i in out_hbm else pltpu.VMEM for i in range(len(outs))]
    moved = sum(a.size * a.dtype.itemsize for a in args)
    return pl.pallas_call(
        body,
        out_shape=shapes,
        in_specs=[pl.BlockSpec(memory_space=m) for m in spaces],
        out_specs=[pl.BlockSpec(memory_space=m) for m in out_spaces],
        scratch_shapes=list(scratch),
        input_output_aliases=aliases or {},
        compiler_params=pltpu.CompilerParams(vmem_limit_bytes=16 * 2**20),
        cost_estimate=pl.CostEstimate(flops=flops, bytes_accessed=moved, transcendentals=0),
    )(*args)


def pack(ref):
    return jnp.concatenate([ref[:, l * LANES : (l + 1) * LANES] for l in range(ref.shape[1] // LANES)], axis=0)


def square_sums(*refs):
    count = 5
    held, outs, refs = refs[:count], refs[count : 2 * count], refs[2 * count :]
    sums_ref, taps_pack, rate_pack, residue_pack, sem = refs
    copies = [pltpu.make_async_copy(source, target, sem.at[i]) for i, (source, target) in enumerate(zip(held, outs))]
    for copy in copies:
        copy.start()
    copies[0].wait()
    stream_ref, _, taps_ref, rate_ref, residue_ref = outs
    lanes = stream_ref.shape[1] // LANES
    total = 0.0
    for l in range(lanes):
        values = stream_ref[:, l * LANES : (l + 1) * LANES].astype(F32)
        total = total + values * values
    sums = jnp.sum(total.T, axis=0, keepdims=True)
    for peer in range(sums_ref.shape[0]):
        sums_ref[peer] = sums
    for copy in copies[1:]:
        copy.wait()
    rate_pack[...] = pack(rate_ref)
    residue_pack[...] = pack(residue_ref)
    for tap in range(3):
        for role in range(3):
            for l in range(lanes):
                taps_pack[pl.ds((tap * 3 + role) * lanes + l, 1), :] = taps_ref[tap, pl.ds(role, 1), pl.ds(l * LANES, LANES)]


def block_states(chan_total, sums_ref, stream_ref, gain_ref, taps_ref, rate_ref, query_ref, product_ref, wide_ref, near_ref, edge_ref, end_ref, whole_ref):
    count, chans = stream_ref.shape
    lanes = chans // LANES
    modes = rate_ref.shape[0]
    blocks = count // SUB
    sums = sums_ref[0]
    for peer in range(1, sums_ref.shape[0]):
        sums = sums + sums_ref[peer]
    rest = lax.rsqrt(sums / chan_total + EPSILON)
    rows = lax.broadcasted_iota(jnp.int32, (2 * SUB, count), 0)
    parts = jnp.zeros((2 * SUB, count), F32)
    for i in range(3):
        part = rest.astype(BF16).astype(F32)
        parts = jnp.where(rows == i, part, parts)
        rest = rest - part
    scale = lax.dot_general(
        parts.astype(BF16), jnp.ones((2 * SUB, LANES), BF16), (((0,), (0,)), ((), ())), preferred_element_type=F32
    )
    row = lax.broadcasted_iota(jnp.int32, (SUB, LANES), 0)
    lag = (SUB - 1 - row).astype(F32)

    def one_lane(lane, carry):
        at = pl.ds(pl.multiple_of(lane * LANES, LANES), LANES)
        gain = jnp.broadcast_to(gain_ref[:, at], (SUB, LANES))
        taps = [[jnp.broadcast_to(taps_ref[j, pl.ds(role, 1), at], (SUB, LANES)) for j in range(3)] for role in range(3)]
        before = [jnp.zeros((SUB, LANES), F32)] * 2
        products, queries = [], []
        for i in range(blocks):
            if i % 2 == 0:
                pair = stream_ref[pl.ds(i * SUB, 2 * SUB), at].astype(F32)
            normed = pair[i % 2 * SUB : (i % 2 + 1) * SUB] * scale[i * SUB : (i + 1) * SUB] * gain
            normed = normed.astype(BF16).astype(F32)
            if i == 0:
                edge_ref[:2, at] = normed[:2]
            if i == blocks - 1:
                edge_ref[2:4, at] = normed[SUB - 2 :]
            rolled = [pltpu.roll(normed, j, 0) for j in (1, 2)]
            shifted = [normed] + [jnp.where(row < j, b, r) for j, b, r in zip((1, 2), before, rolled)]
            before = rolled
            query, key, value = [sum(t * n for t, n in zip(taps[role], shifted)) for role in range(3)]
            product = (key * value).astype(BF16).astype(F32)
            if i == 0:
                product = jnp.where(row < 2, 0.0, product)
            product_ref[pl.ds(i * SUB, SUB), at] = product
            products.append(product)
            queries.append(query)
            if i % 2 == 1:
                query_ref[pl.ds((i - 1) * SUB, 2 * SUB), at] = jnp.concatenate(queries[-2:], axis=0).astype(BF16)
        for mode in range(modes):
            rate = rate_ref[pl.ds(mode, 1), at]
            step = jnp.broadcast_to(jnp.exp(-SUB * rate), (SUB, LANES))
            total = products[0]
            for product in products[1:]:
                total = total * step + product
            end_ref[pl.ds(mode, 1), at] = jnp.sum(total * jnp.exp(-rate * lag), axis=0, keepdims=True)
        return carry

    lax.fori_loop(0, lanes, one_lane, 0)
    whole_ref[: lanes * modes] = pack(end_ref)
    for e in range(4):
        for l in range(lanes):
            whole_ref[pl.ds(lanes * (modes + e) + l, 1), :] = edge_ref[pl.ds(e, 1), pl.ds(l * LANES, LANES)]
    message = whole_ref[...].astype(BF16)
    for ref in (wide_ref, near_ref):
        for peer in range(ref.shape[0]):
            ref[peer] = message


def first_rows(taps_ref, role, last, head):
    lanes = taps_ref.shape[0] // 9
    taps = [taps_ref[pl.ds((3 * j + role) * lanes, lanes)] for j in range(3)]
    first = taps[0] * head[0] + taps[1] * last[1] + taps[2] * last[0]
    second = taps[0] * head[1] + taps[1] * head[0] + taps[2] * last[1]
    return first, second


def first_products(taps_ref, last, head):
    keys, values = first_rows(taps_ref, 1, last, head), first_rows(taps_ref, 2, last, head)
    return [(k * v).astype(BF16).astype(F32) for k, v in zip(keys, values)]


def spread(rows, modes):
    return jnp.concatenate([jnp.broadcast_to(rows[l : l + 1], (modes, LANES)) for l in range(rows.shape[0])], axis=0)


def pairs(ref, start, lanes):
    return ref[start : start + lanes], ref[start + lanes : start + 2 * lanes]


def step_over(block, lanes, rates, taps_ref, state, last, run):
    states = rates.shape[0]
    modes = states // lanes
    first, second = first_products(taps_ref, last, pairs(run, states, lanes))
    end = run[:states] + state * jnp.exp(-block * rates)
    end = end + jnp.exp(-(block - 1) * rates) * spread(first, modes) + jnp.exp(-(block - 2) * rates) * spread(second, modes)
    return end, pairs(run, states + 2 * lanes, lanes)


def step_into(block, lanes, place, rates, taps_ref, state, last, edge_ref, before_ref):
    states = rates.shape[0]
    modes = states // lanes
    first, second = first_products(taps_ref, last, pairs(edge_ref, 0, lanes))
    lag = (block * place).astype(F32)
    held = jnp.exp(-rates * jnp.maximum(lag - 1.0, 0.0)) * spread(first, modes)
    held = held + jnp.exp(-rates * jnp.maximum(lag - 2.0, 0.0)) * spread(second, modes)
    state = before_ref[...] + state * jnp.exp(-rates * lag) + jnp.where(place > 0, held, 0.0)
    inside = pairs(edge_ref, 2 * lanes, lanes)
    return state, [jnp.where(place > 0, a, b) for a, b in zip(inside, last)]


def near_scan(block, lanes, got_ref, rate_ref, taps_ref, before_ref, edge_ref):
    size = got_ref.shape[0]
    place = lax.axis_index("ctx") % size
    states = rate_ref.shape[0]
    rates = rate_ref[...]
    run = got_ref[0].astype(F32)
    head = run[states : states + 2 * lanes]
    total, last = run[:states], pairs(run, states + 2 * lanes, lanes)
    before = jnp.where(place == 1, total, jnp.zeros_like(total))
    for j in range(1, size):
        total, last = step_over(block, lanes, rates, taps_ref, total, last, got_ref[j].astype(F32))
        if j < size - 1:
            before = jnp.where(place == j + 1, total, before)
    before_ref[...] = before
    edge_ref[: 2 * lanes] = head
    edge_ref[2 * lanes : 4 * lanes] = got_ref[jnp.maximum(place - 1, 0)].astype(F32)[states + 2 * lanes :]
    edge_ref[4 * lanes :] = got_ref[place].astype(F32)[states : states + 2 * lanes]
    return jnp.concatenate([total, head, *last], axis=0)


def write(message, *refs):
    for ref in refs:
        rest = ref.shape[0] - message.shape[0]
        whole = jnp.concatenate([message, jnp.zeros((rest, LANES), F32)], axis=0) if rest else message
        ref[...] = whole.astype(BF16)


def first_scan(block, lanes, got_ref, rate_ref, taps_ref, before_ref, edge_ref, message_ref):
    @pl.when(lax.axis_index("ctx") // WIDE == 0)
    def _():
        write(near_scan(block, lanes, got_ref, rate_ref, taps_ref, before_ref, edge_ref), message_ref)


def second_scan(block, lanes, got_ref, came_ref, rate_ref, taps_ref, before_ref, edge_ref, *message_refs):
    @pl.when(lax.axis_index("ctx") // WIDE == 1)
    def _():
        rates = rate_ref[...]
        own = near_scan(block, lanes, got_ref, rate_ref, taps_ref, before_ref, edge_ref)
        state, last = jnp.zeros_like(rates), [jnp.zeros((lanes, LANES), F32)] * 2
        for run in (came_ref[...].astype(F32), own):
            state, last = step_over(block * WIDE, lanes, rates, taps_ref, state, last, run)
        write(jnp.concatenate([state, *last], axis=0), *message_refs)


def third_scan(block, lanes, got_ref, rate_ref, taps_ref, before_ref, edge_ref, *message_refs):
    @pl.when(lax.axis_index("ctx") // WIDE == 2)
    def _():
        write(near_scan(block, lanes, got_ref, rate_ref, taps_ref, before_ref, edge_ref), *message_refs)


def fourth_scan(block, lanes, got_ref, third_before, third_edge, third_message, rate_ref, taps_ref, before_ref, edge_ref, message_ref):
    group = lax.axis_index("ctx") // WIDE

    @pl.when(group == 2)
    def _():
        before_ref[...] = third_before[...]
        edge_ref[...] = third_edge[...]
        message_ref[...] = third_message[...]

    @pl.when(group == 3)
    def _():
        write(near_scan(block, lanes, got_ref, rate_ref, taps_ref, before_ref, edge_ref), message_ref)


def merge(block, lanes, across_ref, cross_ref, next_ref, rate_ref, taps_ref, ahead_ref):
    run = lax.axis_index("ctx") // NEAR
    states = rate_ref.shape[0]
    rates = rate_ref[...]
    across, cross, following = [r[: states + 4 * lanes].astype(F32) for r in (across_ref, cross_ref, next_ref)]
    start = jnp.where(run == 5, following, jnp.where(run == 6, across, cross))
    state, last = start[:states], pairs(start, states + 2 * lanes, lanes)
    for needed, message in ((run > 5, jnp.where(run == 6, cross, across)), (run > 6, following)):
        after, after_last = step_over(block * NEAR, lanes, rates, taps_ref, state, last, message)
        state, last = jnp.where(needed, after, state), [jnp.where(needed, a, b) for a, b in zip(after_last, last)]
    ahead_ref[...] = jnp.concatenate([state, start[states : states + 2 * lanes], *last], axis=0)


def add_mode(totals, term, rate):
    step = jnp.broadcast_to(jnp.exp(-SUB * rate), term.shape)
    out = []
    for total in totals:
        out.append(total + term)
        term = term * step
    return out


def inner_conv(rate_ref, residue_ref, product_ref, local_ref, filter_ref):
    count, chans = product_ref.shape
    modes = rate_ref.shape[0]
    blocks = count // SUB
    row = lax.broadcasted_iota(jnp.int32, (SUB, LANES), 0)
    lead = row.astype(F32)

    def one_lane(lane, carry):
        at = pl.ds(pl.multiple_of(lane * LANES, LANES), LANES)
        zero = jnp.zeros((SUB, LANES), F32)
        totals = [zero] * blocks
        for mode in range(modes):
            rate = rate_ref[pl.ds(mode, 1), at]
            term = residue_ref[pl.ds(mode, 1), at] * jnp.exp(-rate * lead)
            totals = add_mode(totals, term, rate)
        for i in range(blocks):
            filter_ref[pl.ds(i * SUB, SUB), :] = totals[i]

        shifted = [product_ref[pl.ds(i * SUB, SUB), at] for i in range(blocks)]
        totals = [zero] * blocks
        for b in range(SUB):
            for a in range(blocks):
                weight = filter_ref[pl.ds(a * SUB + b, 1), :]
                for j in range(blocks - a):
                    totals[j + a] = totals[j + a] + weight * shifted[j]
            if b < SUB - 1:
                rolled = [pltpu.roll(s, 1, 0) for s in shifted]
                shifted = [jnp.where(row == 0, before, now) for before, now in zip([zero] + rolled[:-1], rolled)]
        for i in range(blocks):
            local_ref[pl.ds(i * SUB, SUB), at] = totals[i]
        return carry

    lax.fori_loop(0, chans // LANES, one_lane, 0)


def finish(place, state, last, edge_ref, before_ref, rate_pack, residue_pack, taps_ref, rate_ref, query_ref, local_ref, mixed_ref, state_ref):
    count, chans = local_ref.shape
    lanes = chans // LANES
    modes = rate_ref.shape[0]
    states = lanes * modes
    blocks = count // SUB
    rates = rate_pack[...]
    state, own_last = step_into(count, lanes, place, rates, taps_ref, state, last, edge_ref, before_ref)
    own_head = pairs(edge_ref, 4 * lanes, lanes)
    own_query = [q.astype(BF16).astype(F32) for q in first_rows(taps_ref, 0, own_last, own_head)]
    first, second = first_products(taps_ref, own_last, own_head)
    ahead = jnp.exp(rates) * spread(second, modes)
    state = state * jnp.exp(-rates) + spread(first, modes) + ahead
    state = state * residue_pack[...]
    ahead = ahead * residue_pack[...]
    extra = [jnp.sum(ahead[l * modes : (l + 1) * modes], axis=0, keepdims=True) for l in range(lanes)]
    row = lax.broadcasted_iota(jnp.int32, (SUB, LANES), 0)
    lead = row.astype(F32)
    for l in range(lanes):
        state_ref[:modes, pl.ds(l * LANES, LANES)] = state[l * modes : (l + 1) * modes]
        take = jnp.where(row == 0, jnp.broadcast_to(extra[l], row.shape), 0.0)
        query = jnp.where(row == 0, own_query[0][l : l + 1], jnp.where(row == 1, own_query[1][l : l + 1], 0.0))
        state_ref[modes : modes + SUB, pl.ds(l * LANES, LANES)] = take
        state_ref[modes + SUB :, pl.ds(l * LANES, LANES)] = query
    rows = lax.broadcasted_iota(jnp.int32, (2 * SUB, LANES), 0)

    def one_lane(lane, carry):
        at = pl.ds(pl.multiple_of(lane * LANES, LANES), LANES)
        totals = [local_ref[pl.ds(i * SUB, SUB), at] for i in range(blocks)]
        for mode in range(modes):
            rate = rate_ref[pl.ds(mode, 1), at]
            term = state_ref[pl.ds(mode, 1), at] * jnp.exp(-rate * lead)
            totals = add_mode(totals, term, rate)
        totals[0] = totals[0] - state_ref[pl.ds(modes, SUB), at]
        for i in range(0, blocks, 2):
            where = pl.ds(i * SUB, 2 * SUB)
            conv = jnp.concatenate(totals[i : i + 2], axis=0).astype(BF16).astype(F32)
            query = query_ref[where, at].astype(F32)
            if i == 0:
                fixed = state_ref[pl.ds(modes + SUB, SUB), at]
                query = jnp.where(rows < 2, jnp.concatenate([fixed, fixed], axis=0), query)
            mixed_ref[where, at] = (query * conv).astype(BF16)
        return carry

    lax.fori_loop(0, lanes, one_lane, 0)


def output(first_before, first_edge, second_before, second_edge, upper_before, upper_edge, rate_pack, residue_pack, taps_ref, rate_ref, query_ref, local_ref, low_ref, third_ref, fourth_ref, ahead_ref, mixed_ref, state_ref):
    index = lax.axis_index("ctx")
    group, run = index // WIDE, index // NEAR
    states = rate_pack.shape[0]
    lanes = taps_ref.shape[0] // 9
    count = local_ref.shape[0]
    came = third_ref[...].astype(F32) + fourth_ref[: states + 4 * lanes].astype(F32)
    state, last = came[:states], (came[states : states + lanes], came[states + lanes : states + 2 * lanes])
    length = jnp.where(group == 1, WIDE, NEAR * jnp.maximum(run - 4, 1)) * count
    message = jnp.where(group == 1, low_ref[...].astype(F32), ahead_ref[...])
    needed = (group == 1) | (run > 4)
    after, after_last = step_over(length.astype(F32), lanes, rate_pack[...], taps_ref, state, last, message)
    state, last = jnp.where(needed, after, state), [jnp.where(needed, a, b) for a, b in zip(after_last, last)]
    place = jnp.where(group < 2, index % WIDE, index % NEAR)
    pick = lambda a, b, c: jnp.where(group == 0, a[...], jnp.where(group == 1, b[...], c[...]))
    before = pick(first_before, second_before, upper_before)
    edges = pick(first_edge, second_edge, upper_edge)
    finish(place, state, last, edges, before, rate_pack, residue_pack, taps_ref, rate_ref, query_ref, local_ref, mixed_ref, state_ref)


def gather(copies, axis, groups=None):
    return lax.all_to_all(copies, axis, 0, 0, tiled=True, axis_index_groups=groups)


def per_device(stream, norm_gain, short_filter, decay_rate, residue):
    count, chans = stream.shape
    modes = decay_rate.shape[1]
    lanes = chans // LANES
    states = lanes * modes
    peers = lax.axis_size("ch")
    ctx = lax.axis_size("ctx")
    groups = [[g + m for m in range(WIDE)] for g in range(0, ctx, WIDE)]
    runs = [[g + m for m in range(NEAR)] for g in range(0, ctx, NEAR)]
    index, stream = lax.optimization_barrier((lax.axis_index("ctx"), stream))
    held = [stream, norm_gain[None, :], short_filter, decay_rate.T, residue.T]
    held = [pltpu.with_memory_space_constraint(h, pltpu.HBM) for h in held]
    stream, gain, taps, rates, weights, sums, taps_pack, rate_pack, residue_pack = call(
        square_sums,
        [(h.shape, h.dtype) for h in held]
        + [((peers, 1, count), F32), ((9 * lanes, LANES), F32), ((states, LANES), F32), ((states, LANES), F32)],
        *held,
        scratch=[pltpu.SemaphoreType.DMA((len(held),))],
        space=pltpu.HBM,
    )
    sums = lax.cond(index < ctx, lambda c: gather(c, "ch"), lambda c: c, sums)
    query, product, wide, near = call(
        lambda *refs: block_states(chans * peers, *refs),
        [((count, chans), BF16), ((count, chans), F32), ((WIDE, states + 4 * lanes, LANES), BF16), ((NEAR, states + 4 * lanes, LANES), BF16)],
        sums, stream, gain, taps, rates,
        scratch=[pltpu.VMEM((SUB, chans), F32), pltpu.VMEM((modes, chans), F32), pltpu.VMEM((states + 4 * lanes, LANES), F32)],
    )
    index, wide, near = lax.optimization_barrier((index, wide, near))
    group = lax.shift_right_logical(index, WIDE.bit_length() - 1)
    small, large = ((states + 4 * lanes, LANES), BF16), ((states + 8 * lanes, LANES), BF16)
    kept = [((states, LANES), F32), ((6 * lanes, LANES), F32)]
    nothing = lambda *shapes: tuple(call(lambda *refs: None, shapes, out_hbm=range(len(shapes))))
    hops = lambda *ends: [pair for a, b in ends for pair in zip(a, b)]
    first, second, third, fourth = groups
    scan = lambda body, outs, *args: call(
        lambda *refs: body(count, lanes, *refs), [*kept, *outs], *args, rate_pack, taps_pack
    )

    def gather_in(number, copies, members):
        return lax.cond(
            group == number, lambda c: gather(c, "ctx", members), lambda c: nothing((c.shape, c.dtype))[0], copies
        )

    def inner():
        return call(
            inner_conv, [((count, chans), F32)], rates, weights, product, scratch=[pltpu.VMEM((count, LANES), F32)], flops=10**7
        )[0]

    *first_kept, message = scan(first_scan, [small], gather_in(0, wide, groups))
    low = lax.ppermute(message, "ctx", hops((first, second)))
    *second_kept, to_third, to_fourth = scan(second_scan, [small, large], gather_in(1, wide, groups), low)
    width = WIDE // 4
    turned = [fourth[WIDE - width * (i // width + 1) + i % width] for i in range(WIDE)]
    to_fourth = lax.ppermute(to_fourth, "ctx", hops((second, turned)))
    to_third = lax.ppermute(to_third, "ctx", hops((second, third)))

    def upper(copies):
        *own, message, first_message = scan(third_scan, [small, large], gather_in(2, copies, runs))
        across = lax.ppermute(first_message, "ctx", hops((runs[4], runs[6]), (runs[5], runs[7])))
        cross = lax.ppermute(first_message, "ctx", hops((runs[4], runs[7]), (runs[5], runs[6])))
        *own, message = scan(fourth_scan, [small], gather_in(3, copies, runs), *own, message)
        following = lax.ppermute(message, "ctx", hops((runs[4], runs[5]), (runs[6], runs[7])))
        (ahead,) = call(
            lambda *refs: merge(count, lanes, *refs), [(small[0], F32)], across, cross, following, rate_pack, taps_pack
        )
        return inner(), *own, ahead

    local, *upper_kept, ahead = lax.cond(
        group >= 2, upper, lambda c: (inner(), *nothing(*kept, (small[0], F32))), near
    )
    (mixed,) = call(
        output,
        [((count, chans), BF16)],
        *first_kept, *second_kept, *upper_kept, rate_pack, residue_pack, taps_pack, rates, query,
        local, low, to_third, to_fourth, ahead,
        scratch=[pltpu.VMEM((modes + 2 * SUB, chans), F32)],
    )
    return mixed


def solution(mesh):
    in_specs = (P("ctx", "ch"), P("ch"), P(None, None, "ch"), P("ch", None), P("ch", None))
    out_specs = P("ctx", "ch")
    return jax.shard_map(
        per_device, mesh=mesh, in_specs=in_specs, out_specs=out_specs, check_vma=False
    )
```

```python
import jax
import jax.numpy as jnp
from jax import lax
from jax.experimental import pallas as pl
from jax.experimental.pallas import tpu as pltpu
from jax.sharding import PartitionSpec as P

EXACT = lax.Precision.HIGHEST
EPSILON = 1e-05
SUB = 8
LANES = 128
WIDE = 16
NEAR = 8

F32 = jnp.float32
BF16 = jnp.bfloat16


def call(body, outs, *args, scratch=(), flops=0, space=pltpu.VMEM, in_hbm=(), out_hbm=(), out_any=(), aliases=None):
    shapes = [jax.ShapeDtypeStruct(s, d) for s, d in outs]
    spaces = [pltpu.HBM if i in in_hbm else space for i in range(len(args))]
    out_spaces = [pltpu.HBM if i in out_hbm else pl.ANY if i in out_any else pltpu.VMEM for i in range(len(outs))]
    moved = sum(a.size * a.dtype.itemsize for a in args)
    return pl.pallas_call(
        body,
        out_shape=shapes,
        in_specs=[pl.BlockSpec(memory_space=m) for m in spaces],
        out_specs=[pl.BlockSpec(memory_space=m) for m in out_spaces],
        scratch_shapes=list(scratch),
        input_output_aliases=aliases or {},
        compiler_params=pltpu.CompilerParams(vmem_limit_bytes=16 * 2**20),
        cost_estimate=pl.CostEstimate(flops=flops, bytes_accessed=moved, transcendentals=0),
    )(*args)


def pack(ref):
    return jnp.concatenate([ref[:, l * LANES : (l + 1) * LANES] for l in range(ref.shape[1] // LANES)], axis=0)


def square_sums(*refs):
    count = 5
    held, outs, refs = refs[:count], refs[count : 2 * count], refs[2 * count :]
    sums_ref, taps_pack, rate_pack, residue_pack, sem = refs
    copies = [pltpu.make_async_copy(source, target, sem.at[i]) for i, (source, target) in enumerate(zip(held, outs))]
    for copy in copies:
        copy.start()
    copies[0].wait()
    stream_ref, _, taps_ref, rate_ref, residue_ref = outs
    lanes = stream_ref.shape[1] // LANES
    total = 0.0
    for l in range(lanes):
        values = stream_ref[:, l * LANES : (l + 1) * LANES].astype(F32)
        total = total + values * values
    sums = jnp.sum(total.T, axis=0, keepdims=True)
    for peer in range(sums_ref.shape[0]):
        sums_ref[peer] = sums
    for copy in copies[1:]:
        copy.wait()
    rate_pack[...] = pack(rate_ref)
    residue_pack[...] = pack(residue_ref)
    for tap in range(3):
        for role in range(3):
            for l in range(lanes):
                taps_pack[pl.ds((tap * 3 + role) * lanes + l, 1), :] = taps_ref[tap, pl.ds(role, 1), pl.ds(l * LANES, LANES)]


def block_states(chan_total, sums_ref, stream_ref, gain_ref, taps_ref, rate_ref, query_ref, product_ref, wide_ref, near_ref, edge_ref, end_ref, whole_ref):
    count, chans = stream_ref.shape
    lanes = chans // LANES
    modes = rate_ref.shape[0]
    blocks = count // SUB
    sums = sums_ref[0]
    for peer in range(1, sums_ref.shape[0]):
        sums = sums + sums_ref[peer]
    rest = lax.rsqrt(sums / chan_total + EPSILON)
    rows = lax.broadcasted_iota(jnp.int32, (2 * SUB, count), 0)
    parts = jnp.zeros((2 * SUB, count), F32)
    for i in range(3):
        part = rest.astype(BF16).astype(F32)
        parts = jnp.where(rows == i, part, parts)
        rest = rest - part
    scale = lax.dot_general(
        parts.astype(BF16), jnp.ones((2 * SUB, LANES), BF16), (((0,), (0,)), ((), ())), preferred_element_type=F32
    )
    row = lax.broadcasted_iota(jnp.int32, (SUB, LANES), 0)
    lag = (SUB - 1 - row).astype(F32)

    def one_lane(lane, carry):
        at = pl.ds(pl.multiple_of(lane * LANES, LANES), LANES)
        gain = jnp.broadcast_to(gain_ref[:, at], (SUB, LANES))
        taps = [[jnp.broadcast_to(taps_ref[j, pl.ds(role, 1), at], (SUB, LANES)) for j in range(3)] for role in range(3)]
        before = [jnp.zeros((SUB, LANES), F32)] * 2
        products, queries = [], []
        for i in range(blocks):
            if i % 2 == 0:
                pair = stream_ref[pl.ds(i * SUB, 2 * SUB), at].astype(F32)
            normed = pair[i % 2 * SUB : (i % 2 + 1) * SUB] * scale[i * SUB : (i + 1) * SUB] * gain
            normed = normed.astype(BF16).astype(F32)
            if i == 0:
                edge_ref[:2, at] = normed[:2]
            if i == blocks - 1:
                edge_ref[2:4, at] = normed[SUB - 2 :]
            rolled = [pltpu.roll(normed, j, 0) for j in (1, 2)]
            shifted = [normed] + [jnp.where(row < j, b, r) for j, b, r in zip((1, 2), before, rolled)]
            before = rolled
            query, key, value = [sum(t * n for t, n in zip(taps[role], shifted)) for role in range(3)]
            product = (key * value).astype(BF16).astype(F32)
            if i == 0:
                product = jnp.where(row < 2, 0.0, product)
            product_ref[pl.ds(i * SUB, SUB), at] = product
            products.append(product)
            queries.append(query)
            if i % 2 == 1:
                query_ref[pl.ds((i - 1) * SUB, 2 * SUB), at] = jnp.concatenate(queries[-2:], axis=0).astype(BF16)
        for mode in range(modes):
            rate = rate_ref[pl.ds(mode, 1), at]
            step = jnp.broadcast_to(jnp.exp(-SUB * rate), (SUB, LANES))
            total = products[0]
            for product in products[1:]:
                total = total * step + product
            end_ref[pl.ds(mode, 1), at] = jnp.sum(total * jnp.exp(-rate * lag), axis=0, keepdims=True)
        return carry

    lax.fori_loop(0, lanes, one_lane, 0)
    whole_ref[: lanes * modes] = pack(end_ref)
    for e in range(4):
        for l in range(lanes):
            whole_ref[pl.ds(lanes * (modes + e) + l, 1), :] = edge_ref[pl.ds(e, 1), pl.ds(l * LANES, LANES)]
    message = whole_ref[...].astype(BF16)
    for ref in (wide_ref, near_ref):
        for peer in range(ref.shape[0]):
            ref[peer] = message


def first_rows(taps_ref, role, last, head):
    lanes = taps_ref.shape[0] // 9
    taps = [taps_ref[pl.ds((3 * j + role) * lanes, lanes)] for j in range(3)]
    first = taps[0] * head[0] + taps[1] * last[1] + taps[2] * last[0]
    second = taps[0] * head[1] + taps[1] * head[0] + taps[2] * last[1]
    return first, second


def first_products(taps_ref, last, head):
    keys, values = first_rows(taps_ref, 1, last, head), first_rows(taps_ref, 2, last, head)
    return [(k * v).astype(BF16).astype(F32) for k, v in zip(keys, values)]


def spread(rows, modes):
    return jnp.concatenate([jnp.broadcast_to(rows[l : l + 1], (modes, LANES)) for l in range(rows.shape[0])], axis=0)


def pairs(ref, start, lanes):
    return ref[start : start + lanes], ref[start + lanes : start + 2 * lanes]


def step_over(block, lanes, rates, taps_ref, state, last, run):
    states = rates.shape[0]
    modes = states // lanes
    first, second = first_products(taps_ref, last, pairs(run, states, lanes))
    end = run[:states] + state * jnp.exp(-block * rates)
    end = end + jnp.exp(-(block - 1) * rates) * spread(first, modes) + jnp.exp(-(block - 2) * rates) * spread(second, modes)
    return end, pairs(run, states + 2 * lanes, lanes)


def step_into(block, lanes, place, rates, taps_ref, state, last, edge_ref, before_ref):
    states = rates.shape[0]
    modes = states // lanes
    first, second = first_products(taps_ref, last, pairs(edge_ref, 0, lanes))
    lag = (block * place).astype(F32)
    held = jnp.exp(-rates * jnp.maximum(lag - 1.0, 0.0)) * spread(first, modes)
    held = held + jnp.exp(-rates * jnp.maximum(lag - 2.0, 0.0)) * spread(second, modes)
    state = before_ref[...] + state * jnp.exp(-rates * lag) + jnp.where(place > 0, held, 0.0)
    inside = pairs(edge_ref, 2 * lanes, lanes)
    return state, [jnp.where(place > 0, a, b) for a, b in zip(inside, last)]


def near_scan(block, lanes, got_ref, rate_ref, taps_ref, before_ref, edge_ref):
    size = got_ref.shape[0]
    place = lax.axis_index("ctx") % size
    states = rate_ref.shape[0]
    rates = rate_ref[...]
    run = got_ref[0].astype(F32)
    head = run[states : states + 2 * lanes]
    total, last = run[:states], pairs(run, states + 2 * lanes, lanes)
    before = jnp.where(place == 1, total, jnp.zeros_like(total))
    for j in range(1, size):
        total, last = step_over(block, lanes, rates, taps_ref, total, last, got_ref[j].astype(F32))
        if j < size - 1:
            before = jnp.where(place == j + 1, total, before)
    before_ref[...] = before
    edge_ref[: 2 * lanes] = head
    edge_ref[2 * lanes : 4 * lanes] = got_ref[jnp.maximum(place - 1, 0)].astype(F32)[states + 2 * lanes :]
    edge_ref[4 * lanes :] = got_ref[place].astype(F32)[states : states + 2 * lanes]
    return jnp.concatenate([total, head, *last], axis=0)


def write(message, *refs):
    for ref in refs:
        rest = ref.shape[0] - message.shape[0]
        whole = jnp.concatenate([message, jnp.zeros((rest, LANES), F32)], axis=0) if rest else message
        ref[...] = whole.astype(BF16)


def first_scan(block, lanes, got_ref, rate_ref, taps_ref, before_ref, edge_ref, message_ref):
    @pl.when(lax.axis_index("ctx") // WIDE == 0)
    def _():
        write(near_scan(block, lanes, got_ref, rate_ref, taps_ref, before_ref, edge_ref), message_ref)


def second_scan(block, lanes, got_ref, rate_ref, taps_ref, before_ref, edge_ref, message_ref):
    @pl.when(lax.axis_index("ctx") // WIDE == 1)
    def _():
        message_ref[...] = near_scan(block, lanes, got_ref, rate_ref, taps_ref, before_ref, edge_ref)


def relay(block, lanes, came_ref, own_ref, rate_ref, taps_ref, kept_ref, *message_refs):
    @pl.when(lax.axis_index("ctx") // WIDE == 1)
    def _():
        rates = rate_ref[...]
        state, last = jnp.zeros_like(rates), [jnp.zeros((lanes, LANES), F32)] * 2
        came = came_ref[...].astype(F32)
        kept_ref[...] = came
        for run in (came, own_ref[...]):
            state, last = step_over(block * WIDE, lanes, rates, taps_ref, state, last, run)
        write(jnp.concatenate([state, *last], axis=0), *message_refs)


def third_scan(block, lanes, got_ref, rate_ref, taps_ref, before_ref, edge_ref, *message_refs):
    @pl.when(lax.axis_index("ctx") // WIDE == 2)
    def _():
        write(near_scan(block, lanes, got_ref, rate_ref, taps_ref, before_ref, edge_ref), *message_refs)


def fourth_scan(block, lanes, got_ref, third_before, third_edge, third_message, rate_ref, taps_ref, before_ref, edge_ref, message_ref):
    group = lax.axis_index("ctx") // WIDE

    @pl.when(group == 2)
    def _():
        before_ref[...] = third_before[...]
        edge_ref[...] = third_edge[...]
        message_ref[...] = third_message[...]

    @pl.when(group == 3)
    def _():
        write(near_scan(block, lanes, got_ref, rate_ref, taps_ref, before_ref, edge_ref), message_ref)


def merge(block, lanes, across_ref, cross_ref, next_ref, rate_ref, taps_ref, ahead_ref):
    run = lax.axis_index("ctx") // NEAR
    states = rate_ref.shape[0]
    rates = rate_ref[...]
    across, cross, following = [r[: states + 4 * lanes].astype(F32) for r in (across_ref, cross_ref, next_ref)]
    start = jnp.where(run == 5, following, jnp.where(run == 6, across, cross))
    state, last = start[:states], pairs(start, states + 2 * lanes, lanes)
    for needed, message in ((run > 5, jnp.where(run == 6, cross, across)), (run > 6, following)):
        after, after_last = step_over(block * NEAR, lanes, rates, taps_ref, state, last, message)
        state, last = jnp.where(needed, after, state), [jnp.where(needed, a, b) for a, b in zip(after_last, last)]
    ahead_ref[...] = jnp.concatenate([state, start[states : states + 2 * lanes], *last], axis=0)


def add_mode(totals, term, rate):
    step = jnp.broadcast_to(jnp.exp(-SUB * rate), term.shape)
    out = []
    for total in totals:
        out.append(total + term)
        term = term * step
    return out


def inner_conv(rate_ref, residue_ref, product_ref, local_ref, filter_ref):
    count, chans = product_ref.shape
    modes = rate_ref.shape[0]
    blocks = count // SUB
    row = lax.broadcasted_iota(jnp.int32, (SUB, LANES), 0)
    lead = row.astype(F32)

    def one_lane(lane, carry):
        at = pl.ds(pl.multiple_of(lane * LANES, LANES), LANES)
        zero = jnp.zeros((SUB, LANES), F32)
        totals = [zero] * blocks
        for mode in range(modes):
            rate = rate_ref[pl.ds(mode, 1), at]
            term = residue_ref[pl.ds(mode, 1), at] * jnp.exp(-rate * lead)
            totals = add_mode(totals, term, rate)
        for i in range(blocks):
            filter_ref[pl.ds(i * SUB, SUB), :] = totals[i]

        shifted = [product_ref[pl.ds(i * SUB, SUB), at] for i in range(blocks)]
        totals = [zero] * blocks
        for b in range(SUB):
            for a in range(blocks):
                weight = filter_ref[pl.ds(a * SUB + b, 1), :]
                for j in range(blocks - a):
                    totals[j + a] = totals[j + a] + weight * shifted[j]
            if b < SUB - 1:
                rolled = [pltpu.roll(s, 1, 0) for s in shifted]
                shifted = [jnp.where(row == 0, before, now) for before, now in zip([zero] + rolled[:-1], rolled)]
        for i in range(blocks):
            local_ref[pl.ds(i * SUB, SUB), at] = totals[i]
        return carry

    lax.fori_loop(0, chans // LANES, one_lane, 0)


def finish(place, state, last, edge_ref, before_ref, rate_pack, residue_pack, taps_ref, rate_ref, query_ref, local_ref, mixed_ref, state_ref):
    count, chans = local_ref.shape
    lanes = chans // LANES
    modes = rate_ref.shape[0]
    states = lanes * modes
    blocks = count // SUB
    rates = rate_pack[...]
    state, own_last = step_into(count, lanes, place, rates, taps_ref, state, last, edge_ref, before_ref)
    own_head = pairs(edge_ref, 4 * lanes, lanes)
    own_query = [q.astype(BF16).astype(F32) for q in first_rows(taps_ref, 0, own_last, own_head)]
    first, second = first_products(taps_ref, own_last, own_head)
    ahead = jnp.exp(rates) * spread(second, modes)
    state = state * jnp.exp(-rates) + spread(first, modes) + ahead
    state = state * residue_pack[...]
    ahead = ahead * residue_pack[...]
    extra = [jnp.sum(ahead[l * modes : (l + 1) * modes], axis=0, keepdims=True) for l in range(lanes)]
    row = lax.broadcasted_iota(jnp.int32, (SUB, LANES), 0)
    lead = row.astype(F32)
    for l in range(lanes):
        state_ref[:modes, pl.ds(l * LANES, LANES)] = state[l * modes : (l + 1) * modes]
        take = jnp.where(row == 0, jnp.broadcast_to(extra[l], row.shape), 0.0)
        query = jnp.where(row == 0, own_query[0][l : l + 1], jnp.where(row == 1, own_query[1][l : l + 1], 0.0))
        state_ref[modes : modes + SUB, pl.ds(l * LANES, LANES)] = take
        state_ref[modes + SUB :, pl.ds(l * LANES, LANES)] = query
    rows = lax.broadcasted_iota(jnp.int32, (2 * SUB, LANES), 0)

    def one_lane(lane, carry):
        at = pl.ds(pl.multiple_of(lane * LANES, LANES), LANES)
        totals = [local_ref[pl.ds(i * SUB, SUB), at] for i in range(blocks)]
        for mode in range(modes):
            rate = rate_ref[pl.ds(mode, 1), at]
            term = state_ref[pl.ds(mode, 1), at] * jnp.exp(-rate * lead)
            totals = add_mode(totals, term, rate)
        totals[0] = totals[0] - state_ref[pl.ds(modes, SUB), at]
        for i in range(0, blocks, 2):
            where = pl.ds(i * SUB, 2 * SUB)
            conv = jnp.concatenate(totals[i : i + 2], axis=0).astype(BF16).astype(F32)
            query = query_ref[where, at].astype(F32)
            if i == 0:
                fixed = state_ref[pl.ds(modes + SUB, SUB), at]
                query = jnp.where(rows < 2, jnp.concatenate([fixed, fixed], axis=0), query)
            mixed_ref[where, at] = (query * conv).astype(BF16)
        return carry

    lax.fori_loop(0, lanes, one_lane, 0)


def leave(mixed_ref, out_ref, sem):
    copy = pltpu.make_async_copy(mixed_ref, out_ref, sem)
    copy.start()
    copy.wait()


def convolves_early():
    index = lax.axis_index("ctx")
    return index < WIDE + WIDE // 2


def early_inner(rate_ref, residue_ref, product_ref, after_ref, local_ref, filter_ref):
    @pl.when(convolves_early())
    def _():
        inner_conv(rate_ref, residue_ref, product_ref, local_ref, filter_ref)


def lower_output(first_before, first_edge, second_before, second_edge, rate_pack, residue_pack, taps_ref, rate_ref, query_ref, residue_ref, product_ref, held_ref, low_ref, out_ref, filter_ref, local_ref, state_ref, mixed_ref, sem):
    early = convolves_early()

    @pl.when(early)
    def _():
        local_ref[...] = held_ref[...]

    @pl.when(jnp.logical_not(early))
    def _():
        inner_conv(rate_ref, residue_ref, product_ref, local_ref, filter_ref)

    index = lax.axis_index("ctx")
    rates = rate_pack[...]
    second = index >= WIDE
    state, last = jnp.zeros_like(rates), [jnp.zeros((taps_ref.shape[0] // 9, LANES), F32)] * 2
    after, after_last = step_over(local_ref.shape[0] * WIDE, len(last[0]), rates, taps_ref, state, last, low_ref[...])
    state, last = jnp.where(second, after, state), [jnp.where(second, a, b) for a, b in zip(after_last, last)]
    before = jnp.where(second, second_before[...], first_before[...])
    edges = jnp.where(second, second_edge[...], first_edge[...])
    finish(index % WIDE, state, last, edges, before, rate_pack, residue_pack, taps_ref, rate_ref, query_ref, local_ref, mixed_ref, state_ref)
    leave(mixed_ref, out_ref, sem)


def upper_output(before_ref, edge_ref, rate_pack, residue_pack, taps_ref, rate_ref, query_ref, local_ref, third_ref, fourth_ref, ahead_ref, held_ref, out_ref, state_ref, mixed_ref, sem):
    index = lax.axis_index("ctx")
    run = index // NEAR
    states = rate_pack.shape[0]
    lanes = taps_ref.shape[0] // 9

    @pl.when(index >= 2 * WIDE)
    def _():
        came = third_ref[...].astype(F32) + fourth_ref[: states + 4 * lanes].astype(F32)
        state, last = came[:states], (came[states : states + lanes], came[states + lanes : states + 2 * lanes])
        length = (NEAR * jnp.maximum(run - 4, 1) * local_ref.shape[0]).astype(F32)
        after, after_last = step_over(length, lanes, rate_pack[...], taps_ref, state, last, ahead_ref[...])
        needed = run > 4
        state, last = jnp.where(needed, after, state), [jnp.where(needed, a, b) for a, b in zip(after_last, last)]
        finish(index % NEAR, state, last, edge_ref, before_ref, rate_pack, residue_pack, taps_ref, rate_ref, query_ref, local_ref, mixed_ref, state_ref)
        leave(mixed_ref, out_ref, sem)


def gather(copies, axis, groups=None):
    return lax.all_to_all(copies, axis, 0, 0, tiled=True, axis_index_groups=groups)


def per_device(stream, norm_gain, short_filter, decay_rate, residue):
    count, chans = stream.shape
    modes = decay_rate.shape[1]
    lanes = chans // LANES
    states = lanes * modes
    peers = lax.axis_size("ch")
    ctx = lax.axis_size("ctx")
    groups = [[g + m for m in range(WIDE)] for g in range(0, ctx, WIDE)]
    runs = [[g + m for m in range(NEAR)] for g in range(0, ctx, NEAR)]
    index, stream = lax.optimization_barrier((lax.axis_index("ctx"), stream))
    held = [stream, norm_gain[None, :], short_filter, decay_rate.T, residue.T]
    held = [pltpu.with_memory_space_constraint(h, pltpu.HBM) for h in held]
    stream, gain, taps, rates, weights, sums, taps_pack, rate_pack, residue_pack = call(
        square_sums,
        [(h.shape, h.dtype) for h in held]
        + [((peers, 1, count), F32), ((9 * lanes, LANES), F32), ((states, LANES), F32), ((states, LANES), F32)],
        *held,
        scratch=[pltpu.SemaphoreType.DMA((len(held),))],
        space=pltpu.HBM,
    )
    sums = lax.cond(index < ctx, lambda c: gather(c, "ch"), lambda c: c, sums)
    query, product, wide, near = call(
        lambda *refs: block_states(chans * peers, *refs),
        [((count, chans), BF16), ((count, chans), F32), ((WIDE, states + 4 * lanes, LANES), BF16), ((NEAR, states + 4 * lanes, LANES), BF16)],
        sums, stream, gain, taps, rates,
        scratch=[pltpu.VMEM((SUB, chans), F32), pltpu.VMEM((modes, chans), F32), pltpu.VMEM((states + 4 * lanes, LANES), F32)],
    )
    index, wide, near = lax.optimization_barrier((index, wide, near))
    group = lax.shift_right_logical(index, WIDE.bit_length() - 1)
    small, large = ((states + 4 * lanes, LANES), BF16), ((states + 8 * lanes, LANES), BF16)
    kept = [((states, LANES), F32), ((6 * lanes, LANES), F32)]
    nothing = lambda *shapes: tuple(call(lambda *refs: None, shapes, out_any=range(len(shapes))))
    hops = lambda *ends: [pair for a, b in ends for pair in zip(a, b)]
    first, second, third, fourth = groups
    scan = lambda body, outs, *args: call(
        lambda *refs: body(count, lanes, *refs), [*kept, *outs], *args, rate_pack, taps_pack
    )

    def gather_in(number, copies, members):
        return lax.cond(
            group == number, lambda c: gather(c, "ctx", members), lambda c: nothing((c.shape, c.dtype))[0], copies
        )

    def inner():
        return call(
            inner_conv, [((count, chans), F32)], rates, weights, product, scratch=[pltpu.VMEM((count, LANES), F32)], flops=10**7
        )[0]

    room = [pltpu.VMEM((count, LANES), F32)]
    work = [pltpu.VMEM((modes + 2 * SUB, chans), F32), pltpu.VMEM((count, chans), BF16), pltpu.SemaphoreType.DMA]
    whole = (small[0], F32)
    held, result = ((count, chans), F32), ((count, chans), BF16)

    def lower(copies):
        *first_kept, message = scan(first_scan, [small], gather_in(0, copies, groups))
        low = lax.ppermute(message, "ctx", hops((first, second)))
        (local,) = call(early_inner, [held], rates, weights, product, message, scratch=room, flops=10**7)
        copies, local = lax.optimization_barrier((copies, local))
        *second_kept, message = scan(second_scan, [whole], gather_in(1, copies, groups))
        onward = call(lambda *refs: relay(count, lanes, *refs), [whole, small, large], low, message, rate_pack, taps_pack)
        return *first_kept, *second_kept, local, *onward

    *lower_kept, to_third, to_fourth = lax.cond(
        group < 2, lower, lambda c: nothing(*kept, *kept, held, whole, small, large), wide
    )
    half = WIDE // 2
    to_fourth = lax.ppermute(to_fourth, "ctx", hops((second, fourth[half:] + fourth[:half])))
    to_third = lax.ppermute(to_third, "ctx", hops((second, third)))

    def upper(copies):
        *own, message, first_message = scan(third_scan, [small, large], gather_in(2, copies, runs))
        across = lax.ppermute(first_message, "ctx", hops((runs[4], runs[6]), (runs[5], runs[7])))
        cross = lax.ppermute(first_message, "ctx", hops((runs[4], runs[7]), (runs[5], runs[6])))
        *own, message = scan(fourth_scan, [small], gather_in(3, copies, runs), *own, message)
        following = lax.ppermute(message, "ctx", hops((runs[4], runs[5]), (runs[6], runs[7])))
        (ahead,) = call(
            lambda *refs: merge(count, lanes, *refs), [whole], across, cross, following, rate_pack, taps_pack
        )
        return *call(lambda *refs: None, [result], out_hbm=(0,)), *own, inner(), ahead

    def rest(copies):
        common = [rate_pack, residue_pack, taps_pack, rates, query, weights, product]
        (mixed,) = call(
            lower_output, [result], *lower_kept[:4], *common, *lower_kept[4:], scratch=room + [pltpu.VMEM(*held)] + work, out_hbm=(0,)
        )
        return mixed, *nothing(*kept, held, whole)

    mixed, *own, local, ahead = lax.cond(group >= 2, upper, rest, near)
    (mixed,) = call(
        upper_output,
        [result],
        *own, rate_pack, residue_pack, taps_pack, rates, query, local, to_third, to_fourth, ahead, mixed,
        scratch=work, in_hbm=(11,), out_hbm=(0,), aliases={11: 0},
    )
    return mixed


def solution(mesh):
    in_specs = (P("ctx", "ch"), P("ch"), P(None, None, "ch"), P("ch", None), P("ch", None))
    out_specs = P("ctx", "ch")
    return jax.shard_map(
        per_device, mesh=mesh, in_specs=in_specs, out_specs=out_specs, check_vma=False
    )
```

```python
import jax
import jax.numpy as jnp
from jax import lax
from jax.experimental import pallas as pl
from jax.experimental.pallas import tpu as pltpu
from jax.sharding import PartitionSpec as P

EXACT = lax.Precision.HIGHEST
EPSILON = 1e-05
SUB = 8
LANES = 128
WIDE = 16
NEAR = 8

F32 = jnp.float32
BF16 = jnp.bfloat16


def call(body, outs, *args, scratch=(), flops=0, space=pltpu.VMEM, in_hbm=(), out_hbm=(), out_any=(), aliases=None):
    shapes = [jax.ShapeDtypeStruct(s, d) for s, d in outs]
    spaces = [pltpu.HBM if i in in_hbm else space for i in range(len(args))]
    out_spaces = [pltpu.HBM if i in out_hbm else pl.ANY if i in out_any else pltpu.VMEM for i in range(len(outs))]
    moved = sum(a.size * a.dtype.itemsize for a in args)
    return pl.pallas_call(
        body,
        out_shape=shapes,
        in_specs=[pl.BlockSpec(memory_space=m) for m in spaces],
        out_specs=[pl.BlockSpec(memory_space=m) for m in out_spaces],
        scratch_shapes=list(scratch),
        input_output_aliases=aliases or {},
        compiler_params=pltpu.CompilerParams(vmem_limit_bytes=16 * 2**20),
        cost_estimate=pl.CostEstimate(flops=flops, bytes_accessed=moved, transcendentals=0),
    )(*args)


def pack(ref):
    return jnp.concatenate([ref[:, l * LANES : (l + 1) * LANES] for l in range(ref.shape[1] // LANES)], axis=0)


def square_sums(*refs):
    count = 5
    held, outs, refs = refs[:count], refs[count : 2 * count], refs[2 * count :]
    sums_ref, taps_pack, rate_pack, residue_pack, sem = refs
    stream_ref, _, taps_ref, rate_ref, residue_ref = outs
    lanes = stream_ref.shape[1] // LANES
    cuts = [pl.ds(l * LANES, LANES) for l in range(lanes)]
    copies = [pltpu.make_async_copy(held[0].at[:, at], stream_ref.at[:, at], sem.at[i]) for i, at in enumerate(cuts)]
    copies += [pltpu.make_async_copy(held[i], outs[i], sem.at[lanes + i - 1]) for i in range(1, count)]
    for copy in copies:
        copy.start()
    total = 0.0
    for copy, at in zip(copies, cuts):
        copy.wait()
        values = stream_ref[:, at].astype(F32)
        total = total + values * values
    sums = jnp.sum(total.T, axis=0, keepdims=True)
    for peer in range(sums_ref.shape[0]):
        sums_ref[peer] = sums
    for copy in copies[lanes:]:
        copy.wait()
    rate_pack[...] = pack(rate_ref)
    residue_pack[...] = pack(residue_ref)
    for tap in range(3):
        for role in range(3):
            for l in range(lanes):
                taps_pack[pl.ds((tap * 3 + role) * lanes + l, 1), :] = taps_ref[tap, pl.ds(role, 1), pl.ds(l * LANES, LANES)]


def block_states(chan_total, sums_ref, stream_ref, gain_ref, taps_ref, rate_ref, query_ref, product_ref, wide_ref, near_ref, edge_ref, end_ref, whole_ref):
    count, chans = stream_ref.shape
    lanes = chans // LANES
    modes = rate_ref.shape[0]
    blocks = count // SUB
    sums = sums_ref[0]
    for peer in range(1, sums_ref.shape[0]):
        sums = sums + sums_ref[peer]
    rest = lax.rsqrt(sums / chan_total + EPSILON)
    rows = lax.broadcasted_iota(jnp.int32, (2 * SUB, count), 0)
    parts = jnp.zeros((2 * SUB, count), F32)
    for i in range(3):
        part = rest.astype(BF16).astype(F32)
        parts = jnp.where(rows == i, part, parts)
        rest = rest - part
    scale = lax.dot_general(
        parts.astype(BF16), jnp.ones((2 * SUB, LANES), BF16), (((0,), (0,)), ((), ())), preferred_element_type=F32
    )
    row = lax.broadcasted_iota(jnp.int32, (SUB, LANES), 0)
    lag = (SUB - 1 - row).astype(F32)

    def one_lane(lane, carry):
        at = pl.ds(pl.multiple_of(lane * LANES, LANES), LANES)
        gain = jnp.broadcast_to(gain_ref[:, at], (SUB, LANES))
        taps = [[jnp.broadcast_to(taps_ref[j, pl.ds(role, 1), at], (SUB, LANES)) for j in range(3)] for role in range(3)]
        before = [jnp.zeros((SUB, LANES), F32)] * 2
        products, queries = [], []
        for i in range(blocks):
            if i % 2 == 0:
                pair = stream_ref[pl.ds(i * SUB, 2 * SUB), at].astype(F32)
            normed = pair[i % 2 * SUB : (i % 2 + 1) * SUB] * scale[i * SUB : (i + 1) * SUB] * gain
            normed = normed.astype(BF16).astype(F32)
            if i == 0:
                edge_ref[:2, at] = normed[:2]
            if i == blocks - 1:
                edge_ref[2:4, at] = normed[SUB - 2 :]
            rolled = [pltpu.roll(normed, j, 0) for j in (1, 2)]
            shifted = [normed] + [jnp.where(row < j, b, r) for j, b, r in zip((1, 2), before, rolled)]
            before = rolled
            query, key, value = [sum(t * n for t, n in zip(taps[role], shifted)) for role in range(3)]
            product = (key * value).astype(BF16).astype(F32)
            if i == 0:
                product = jnp.where(row < 2, 0.0, product)
            product_ref[pl.ds(i * SUB, SUB), at] = product
            products.append(product)
            queries.append(query)
            if i % 2 == 1:
                query_ref[pl.ds((i - 1) * SUB, 2 * SUB), at] = jnp.concatenate(queries[-2:], axis=0).astype(BF16)
        for mode in range(modes):
            rate = rate_ref[pl.ds(mode, 1), at]
            step = jnp.broadcast_to(jnp.exp(-SUB * rate), (SUB, LANES))
            total = products[0]
            for product in products[1:]:
                total = total * step + product
            end_ref[pl.ds(mode, 1), at] = jnp.sum(total * jnp.exp(-rate * lag), axis=0, keepdims=True)
        return carry

    lax.fori_loop(0, lanes, one_lane, 0, unroll=True)
    whole_ref[: lanes * modes] = pack(end_ref)
    for e in range(4):
        for l in range(lanes):
            whole_ref[pl.ds(lanes * (modes + e) + l, 1), :] = edge_ref[pl.ds(e, 1), pl.ds(l * LANES, LANES)]
    message = whole_ref[...].astype(BF16)
    for ref in (wide_ref, near_ref):
        for peer in range(ref.shape[0]):
            ref[peer] = message


def first_rows(taps_ref, role, last, head):
    lanes = taps_ref.shape[0] // 9
    taps = [taps_ref[pl.ds((3 * j + role) * lanes, lanes)] for j in range(3)]
    first = taps[0] * head[0] + taps[1] * last[1] + taps[2] * last[0]
    second = taps[0] * head[1] + taps[1] * head[0] + taps[2] * last[1]
    return first, second


def first_products(taps_ref, last, head):
    keys, values = first_rows(taps_ref, 1, last, head), first_rows(taps_ref, 2, last, head)
    return [(k * v).astype(BF16).astype(F32) for k, v in zip(keys, values)]


def spread(rows, modes):
    return jnp.concatenate([jnp.broadcast_to(rows[l : l + 1], (modes, LANES)) for l in range(rows.shape[0])], axis=0)


def pairs(ref, start, lanes):
    return ref[start : start + lanes], ref[start + lanes : start + 2 * lanes]


def step_over(block, lanes, rates, taps_ref, state, last, run):
    states = rates.shape[0]
    modes = states // lanes
    first, second = first_products(taps_ref, last, pairs(run, states, lanes))
    end = run[:states] + state * jnp.exp(-block * rates)
    end = end + jnp.exp(-(block - 1) * rates) * spread(first, modes) + jnp.exp(-(block - 2) * rates) * spread(second, modes)
    return end, pairs(run, states + 2 * lanes, lanes)


def step_into(block, lanes, place, rates, taps_ref, state, last, edge_ref, before_ref):
    states = rates.shape[0]
    modes = states // lanes
    first, second = first_products(taps_ref, last, pairs(edge_ref, 0, lanes))
    lag = (block * place).astype(F32)
    held = jnp.exp(-rates * jnp.maximum(lag - 1.0, 0.0)) * spread(first, modes)
    held = held + jnp.exp(-rates * jnp.maximum(lag - 2.0, 0.0)) * spread(second, modes)
    state = before_ref[...] + state * jnp.exp(-rates * lag) + jnp.where(place > 0, held, 0.0)
    inside = pairs(edge_ref, 2 * lanes, lanes)
    return state, [jnp.where(place > 0, a, b) for a, b in zip(inside, last)]


def slot(place, size):
    return size - 1 - place


def near_scan(block, lanes, got_ref, rate_ref, taps_ref, before_ref, edge_ref):
    size = got_ref.shape[0]
    place = lax.axis_index("ctx") % size
    states = rate_ref.shape[0]
    rates = rate_ref[...]
    run = got_ref[slot(0, size)].astype(F32)
    head = run[states : states + 2 * lanes]
    total, last = run[:states], pairs(run, states + 2 * lanes, lanes)
    before = jnp.where(place == 1, total, jnp.zeros_like(total))
    for j in range(1, size):
        total, last = step_over(block, lanes, rates, taps_ref, total, last, got_ref[slot(j, size)].astype(F32))
        if j < size - 1:
            before = jnp.where(place == j + 1, total, before)
    before_ref[...] = before
    edge_ref[: 2 * lanes] = head
    edge_ref[2 * lanes : 4 * lanes] = got_ref[slot(jnp.maximum(place - 1, 0), size)].astype(F32)[states + 2 * lanes :]
    edge_ref[4 * lanes :] = got_ref[slot(place, size)].astype(F32)[states : states + 2 * lanes]
    return jnp.concatenate([total, head, *last], axis=0)


def write(message, *refs):
    for ref in refs:
        rest = ref.shape[0] - message.shape[0]
        whole = jnp.concatenate([message, jnp.zeros((rest, LANES), F32)], axis=0) if rest else message
        ref[...] = whole.astype(BF16)


def first_scan(block, lanes, got_ref, rate_ref, taps_ref, before_ref, edge_ref, message_ref):
    @pl.when(lax.axis_index("ctx") // WIDE == 0)
    def _():
        write(near_scan(block, lanes, got_ref, rate_ref, taps_ref, before_ref, edge_ref), message_ref)


def second_scan(block, lanes, got_ref, rate_ref, taps_ref, before_ref, edge_ref, message_ref):
    @pl.when(lax.axis_index("ctx") // WIDE == 1)
    def _():
        message_ref[...] = near_scan(block, lanes, got_ref, rate_ref, taps_ref, before_ref, edge_ref)


def relay(block, lanes, came_ref, own_ref, rate_ref, taps_ref, kept_ref, *message_refs):
    @pl.when(lax.axis_index("ctx") // WIDE == 1)
    def _():
        rates = rate_ref[...]
        state, last = jnp.zeros_like(rates), [jnp.zeros((lanes, LANES), F32)] * 2
        came = came_ref[...].astype(F32)
        kept_ref[...] = came
        for run in (came, own_ref[...]):
            state, last = step_over(block * WIDE, lanes, rates, taps_ref, state, last, run)
        write(jnp.concatenate([state, *last], axis=0), *message_refs)


def third_scan(block, lanes, got_ref, rate_ref, taps_ref, before_ref, edge_ref, *message_refs):
    @pl.when(lax.axis_index("ctx") // WIDE == 2)
    def _():
        write(near_scan(block, lanes, got_ref, rate_ref, taps_ref, before_ref, edge_ref), *message_refs)


def fourth_scan(block, lanes, got_ref, third_before, third_edge, third_message, rate_ref, taps_ref, before_ref, edge_ref, message_ref):
    group = lax.axis_index("ctx") // WIDE

    @pl.when(group == 2)
    def _():
        before_ref[...] = third_before[...]
        edge_ref[...] = third_edge[...]
        message_ref[...] = third_message[...]

    @pl.when(group == 3)
    def _():
        write(near_scan(block, lanes, got_ref, rate_ref, taps_ref, before_ref, edge_ref), message_ref)


def prepare(block, lanes, across_ref, cross_ref, next_ref, before_ref, edge_ref, rate_ref, taps_ref, residue_ref, rates_ref, weights_ref, rest_ref, decay_ref, head_ref, lead_ref, step_ref, fixed_ref):
    index = lax.axis_index("ctx")
    run, place = index // NEAR, index % NEAR
    states = rate_ref.shape[0]
    modes = states // lanes
    rates = rate_ref[...]
    across, cross, following = [r[: states + 4 * lanes].astype(F32) for r in (across_ref, cross_ref, next_ref)]
    start = jnp.where(run == 5, following, jnp.where(run == 6, across, cross))
    state, last = start[:states], pairs(start, states + 2 * lanes, lanes)
    for needed, message in ((run > 5, jnp.where(run == 6, cross, across)), (run > 6, following)):
        after, after_last = step_over(block * NEAR, lanes, rates, taps_ref, state, last, message)
        state, last = jnp.where(needed, after, state), [jnp.where(needed, a, b) for a, b in zip(after_last, last)]
    into, own_last = step_into(block, lanes, place, rates, taps_ref, state, last, edge_ref, before_ref)
    state = jnp.where(run > 4, into, before_ref[...])
    length = (block * (NEAR * (run - 4) + place)).astype(F32)
    away = length > 0
    own_head = pairs(edge_ref, 4 * lanes, lanes)
    first, second = first_products(taps_ref, own_last, own_head)
    ahead = jnp.exp(rates) * spread(second, modes)
    rest_ref[...] = state * jnp.exp(-rates) + jnp.where(away, spread(first, modes) + ahead, 0.0)
    for i in range(3):
        decay_ref[pl.ds(i * states, states)] = jnp.exp(-rates * (length + (1.0 - i)))
    head_ref[...] = jnp.where(run > 4, start[states : states + 2 * lanes], edge_ref[: 2 * lanes])
    ahead = jnp.where(away, ahead * residue_ref[...], 0.0)
    query = [q.astype(BF16).astype(F32) for q in first_rows(taps_ref, 0, own_last, own_head)]
    fix_rows(lanes, ahead, query, fixed_ref, 0)
    row = lax.broadcasted_iota(jnp.int32, (SUB, weights_ref.shape[1]), 0).astype(F32)
    step_ref[...] = jnp.exp(-SUB * rates_ref[...])
    for mode in range(modes):
        at = pl.ds(mode, 1)
        lead_ref[pl.ds(mode * SUB, SUB)] = weights_ref[at] * jnp.exp(-rates_ref[at] * row)


def fix_rows(lanes, ahead, query, out_ref, start):
    modes = ahead.shape[0] // lanes
    row = lax.broadcasted_iota(jnp.int32, (SUB, LANES), 0)
    for l in range(lanes):
        extra = jnp.sum(ahead[l * modes : (l + 1) * modes], axis=0, keepdims=True)
        take = jnp.where(row == 0, jnp.broadcast_to(extra, row.shape), 0.0)
        fixed = jnp.where(row == 0, query[0][l : l + 1], jnp.where(row == 1, query[1][l : l + 1], 0.0))
        out_ref[start : start + SUB, pl.ds(l * LANES, LANES)] = take
        out_ref[start + SUB : start + 2 * SUB, pl.ds(l * LANES, LANES)] = fixed


def add_mode(totals, term, rate):
    step = jnp.broadcast_to(jnp.exp(-SUB * rate), term.shape)
    out = []
    for total in totals:
        out.append(total + term)
        term = term * step
    return out


def inner_conv(rate_ref, residue_ref, product_ref, local_ref, filter_ref):
    count, chans = product_ref.shape
    modes = rate_ref.shape[0]
    blocks = count // SUB
    row = lax.broadcasted_iota(jnp.int32, (SUB, LANES), 0)
    lead = row.astype(F32)

    def one_lane(lane, carry):
        at = pl.ds(pl.multiple_of(lane * LANES, LANES), LANES)
        zero = jnp.zeros((SUB, LANES), F32)
        totals = [zero] * blocks
        for mode in range(modes):
            rate = rate_ref[pl.ds(mode, 1), at]
            term = residue_ref[pl.ds(mode, 1), at] * jnp.exp(-rate * lead)
            totals = add_mode(totals, term, rate)
        for i in range(blocks):
            filter_ref[pl.ds(i * SUB, SUB), :] = totals[i]

        shifted = [product_ref[pl.ds(i * SUB, SUB), at] for i in range(blocks)]
        totals = [zero] * blocks
        for b in range(SUB):
            for a in range(blocks):
                weight = filter_ref[pl.ds(a * SUB + b, 1), :]
                for j in range(blocks - a):
                    totals[j + a] = totals[j + a] + weight * shifted[j]
            if b < SUB - 1:
                rolled = [pltpu.roll(s, 1, 0) for s in shifted]
                shifted = [jnp.where(row == 0, before, now) for before, now in zip([zero] + rolled[:-1], rolled)]
        for i in range(blocks):
            local_ref[pl.ds(i * SUB, SUB), at] = totals[i]
        return carry

    lax.fori_loop(0, chans // LANES, one_lane, 0)


def finish(place, state, last, edge_ref, before_ref, rate_pack, residue_pack, taps_ref, rate_ref, query_ref, local_ref, mixed_ref, state_ref):
    count, chans = local_ref.shape
    lanes = chans // LANES
    modes = rate_ref.shape[0]
    states = lanes * modes
    blocks = count // SUB
    rates = rate_pack[...]
    state, own_last = step_into(count, lanes, place, rates, taps_ref, state, last, edge_ref, before_ref)
    own_head = pairs(edge_ref, 4 * lanes, lanes)
    own_query = [q.astype(BF16).astype(F32) for q in first_rows(taps_ref, 0, own_last, own_head)]
    first, second = first_products(taps_ref, own_last, own_head)
    ahead = jnp.exp(rates) * spread(second, modes)
    state = state * jnp.exp(-rates) + spread(first, modes) + ahead
    state = state * residue_pack[...]
    ahead = ahead * residue_pack[...]
    fix_rows(lanes, ahead, own_query, state_ref, modes)
    lead = lax.broadcasted_iota(jnp.int32, (SUB, LANES), 0).astype(F32)
    for l in range(lanes):
        state_ref[:modes, pl.ds(l * LANES, LANES)] = state[l * modes : (l + 1) * modes]

    def one_lane(lane, carry):
        at = pl.ds(pl.multiple_of(lane * LANES, LANES), LANES)
        totals = [local_ref[pl.ds(i * SUB, SUB), at] for i in range(blocks)]
        for mode in range(modes):
            rate = rate_ref[pl.ds(mode, 1), at]
            term = state_ref[pl.ds(mode, 1), at] * jnp.exp(-rate * lead)
            totals = add_mode(totals, term, rate)
        gate(totals, at, state_ref, modes, query_ref, mixed_ref)
        return carry

    lax.fori_loop(0, lanes, one_lane, 0)


def gate(totals, at, fixed_ref, start, query_ref, mixed_ref):
    totals[0] = totals[0] - fixed_ref[pl.ds(start, SUB), at]
    rows = lax.broadcasted_iota(jnp.int32, (2 * SUB, LANES), 0)
    for i in range(0, len(totals), 2):
        where = pl.ds(i * SUB, 2 * SUB)
        conv = jnp.concatenate(totals[i : i + 2], axis=0).astype(BF16).astype(F32)
        query = query_ref[where, at].astype(F32)
        if i == 0:
            fixed = fixed_ref[pl.ds(start + SUB, SUB), at]
            query = jnp.where(rows < 2, jnp.concatenate([fixed, fixed], axis=0), query)
        mixed_ref[where, at] = (query * conv).astype(BF16)


def leave(mixed_ref, out_ref, sem):
    copy = pltpu.make_async_copy(mixed_ref, out_ref, sem)
    copy.start()
    copy.wait()


def convolves_early():
    index = lax.axis_index("ctx")
    return index < WIDE + WIDE // 2


def early_inner(rate_ref, residue_ref, product_ref, after_ref, local_ref, filter_ref):
    @pl.when(convolves_early())
    def _():
        inner_conv(rate_ref, residue_ref, product_ref, local_ref, filter_ref)


def lower_output(first_before, first_edge, second_before, second_edge, rate_pack, residue_pack, taps_ref, rate_ref, query_ref, residue_ref, product_ref, held_ref, low_ref, out_ref, filter_ref, local_ref, state_ref, mixed_ref, sem):
    early = convolves_early()

    @pl.when(early)
    def _():
        local_ref[...] = held_ref[...]

    @pl.when(jnp.logical_not(early))
    def _():
        inner_conv(rate_ref, residue_ref, product_ref, local_ref, filter_ref)

    index = lax.axis_index("ctx")
    rates = rate_pack[...]
    second = index >= WIDE
    state, last = jnp.zeros_like(rates), [jnp.zeros((taps_ref.shape[0] // 9, LANES), F32)] * 2
    after, after_last = step_over(local_ref.shape[0] * WIDE, len(last[0]), rates, taps_ref, state, last, low_ref[...])
    state, last = jnp.where(second, after, state), [jnp.where(second, a, b) for a, b in zip(after_last, last)]
    before = jnp.where(second, second_before[...], first_before[...])
    edges = jnp.where(second, second_edge[...], first_edge[...])
    finish(index % WIDE, state, last, edges, before, rate_pack, residue_pack, taps_ref, rate_ref, query_ref, local_ref, mixed_ref, state_ref)
    leave(mixed_ref, out_ref, sem)


def upper_output(rest_ref, decay_ref, head_ref, lead_ref, step_ref, fixed_ref, residue_ref, rate_ref, taps_ref, query_ref, local_ref, third_ref, fourth_ref, held_ref, out_ref, state_ref, mixed_ref, sem):
    index = lax.axis_index("ctx")
    states = rest_ref.shape[0]
    lanes = taps_ref.shape[0] // 9
    modes = states // lanes
    blocks = local_ref.shape[0] // SUB

    @pl.when(index >= 2 * WIDE)
    def _():
        came = third_ref[...].astype(F32) + fourth_ref[: states + 4 * lanes].astype(F32)
        last = pairs(came, states, lanes)
        head = pairs(head_ref, 0, lanes)
        first, second = first_products(taps_ref, last, head)
        ahead = spread(second, modes)
        state = rest_ref[...] + came[:states] * decay_ref[:states]
        state = state + spread(first, modes) * decay_ref[states : 2 * states] + ahead * decay_ref[2 * states :]
        for l in range(lanes):
            state_ref[:modes, pl.ds(l * LANES, LANES)] = state[l * modes : (l + 1) * modes]
        state_ref[modes:] = fixed_ref[...]

        @pl.when(index == 2 * WIDE)
        def _():
            query = [q.astype(BF16).astype(F32) for q in first_rows(taps_ref, 0, last, head)]
            fix_rows(lanes, jnp.exp(rate_ref[...]) * ahead * residue_ref[...], query, state_ref, modes)

        def one_lane(lane, carry):
            at = pl.ds(pl.multiple_of(lane * LANES, LANES), LANES)
            totals = [local_ref[pl.ds(i * SUB, SUB), at] for i in range(blocks)]
            for mode in range(modes):
                step = jnp.broadcast_to(step_ref[pl.ds(mode, 1), at], (SUB, LANES))
                term = state_ref[pl.ds(mode, 1), at] * lead_ref[pl.ds(mode * SUB, SUB), at]
                for i in range(blocks):
                    totals[i] = totals[i] + term
                    if i < blocks - 1:
                        term = term * step
            gate(totals, at, state_ref, modes, query_ref, mixed_ref)
            pltpu.make_async_copy(mixed_ref.at[:, at], out_ref.at[:, at], sem.at[lane]).start()
            return carry

        lax.fori_loop(0, lanes, one_lane, 0, unroll=True)
        for l in range(lanes):
            at = pl.ds(l * LANES, LANES)
            pltpu.make_async_copy(mixed_ref.at[:, at], out_ref.at[:, at], sem.at[l]).wait()


def gather(copies, axis, groups=None):
    return lax.all_to_all(copies, axis, 0, 0, tiled=True, axis_index_groups=groups)


def per_device(stream, norm_gain, short_filter, decay_rate, residue):
    count, chans = stream.shape
    modes = decay_rate.shape[1]
    lanes = chans // LANES
    states = lanes * modes
    peers = lax.axis_size("ch")
    ctx = lax.axis_size("ctx")
    groups = [[g + m for m in range(WIDE)] for g in range(0, ctx, WIDE)]
    runs = [[g + m for m in range(NEAR)] for g in range(0, ctx, NEAR)]
    index, stream = lax.optimization_barrier((lax.axis_index("ctx"), stream))
    held = [stream, norm_gain[None, :], short_filter, decay_rate.T, residue.T]
    held = [pltpu.with_memory_space_constraint(h, pltpu.HBM) for h in held]
    stream, gain, taps, rates, weights, sums, taps_pack, rate_pack, residue_pack = call(
        square_sums,
        [(h.shape, h.dtype) for h in held]
        + [((peers, 1, count), F32), ((9 * lanes, LANES), F32), ((states, LANES), F32), ((states, LANES), F32)],
        *held,
        scratch=[pltpu.SemaphoreType.DMA((lanes + len(held) - 1,))],
        space=pltpu.HBM,
    )
    sums = lax.cond(index < ctx, lambda c: gather(c, "ch"), lambda c: c, sums)
    query, product, wide, near = call(
        lambda *refs: block_states(chans * peers, *refs),
        [((count, chans), BF16), ((count, chans), F32), ((WIDE, states + 4 * lanes, LANES), BF16), ((NEAR, states + 4 * lanes, LANES), BF16)],
        sums, stream, gain, taps, rates,
        scratch=[pltpu.VMEM((SUB, chans), F32), pltpu.VMEM((modes, chans), F32), pltpu.VMEM((states + 4 * lanes, LANES), F32)],
    )
    index, wide, near = lax.optimization_barrier((index, wide, near))
    group = lax.shift_right_logical(index, WIDE.bit_length() - 1)
    small, large = ((states + 4 * lanes, LANES), BF16), ((states + 8 * lanes, LANES), BF16)
    kept = [((states, LANES), F32), ((6 * lanes, LANES), F32)]
    nothing = lambda *shapes: tuple(call(lambda *refs: None, shapes, out_any=range(len(shapes))))
    hops = lambda *ends: [pair for a, b in ends for pair in zip(a, b)]
    first, second, third, fourth = groups
    scan = lambda body, outs, *args: call(
        lambda *refs: body(count, lanes, *refs), [*kept, *outs], *args, rate_pack, taps_pack
    )

    def gather_in(number, copies, members):
        size = len(members[0])
        order = sorted(range(size), key=lambda j: slot(j, size))
        members = [[g[j] for j in order] for g in members]
        return lax.cond(
            group == number, lambda c: gather(c, "ctx", members), lambda c: nothing((c.shape, c.dtype))[0], copies
        )

    def inner():
        return call(
            inner_conv, [((count, chans), F32)], rates, weights, product, scratch=[pltpu.VMEM((count, LANES), F32)], flops=10**7
        )[0]

    room = [pltpu.VMEM((count, LANES), F32)]
    work = [pltpu.VMEM((modes + 2 * SUB, chans), F32), pltpu.VMEM((count, chans), BF16), pltpu.SemaphoreType.DMA]
    whole = (small[0], F32)
    held, result = ((count, chans), F32), ((count, chans), BF16)

    def lower(copies):
        *first_kept, message = scan(first_scan, [small], gather_in(0, copies, groups))
        low = lax.ppermute(message, "ctx", hops((first, second)))
        (local,) = call(early_inner, [held], rates, weights, product, message, scratch=room, flops=10**7)
        copies, local = lax.optimization_barrier((copies, local))
        *second_kept, message = scan(second_scan, [whole], gather_in(1, copies, groups))
        onward = call(lambda *refs: relay(count, lanes, *refs), [whole, small, large], low, message, rate_pack, taps_pack)
        return *first_kept, *second_kept, local, *onward

    *lower_kept, to_third, to_fourth = lax.cond(
        group < 2, lower, lambda c: nothing(*kept, *kept, held, whole, small, large), wide
    )
    half = WIDE // 2
    to_fourth = lax.ppermute(to_fourth, "ctx", hops((second, fourth[half:] + fourth[:half])))
    to_third = lax.ppermute(to_third, "ctx", hops((second, third)))

    prepared = [
        ((states, LANES), F32), ((3 * states, LANES), F32), ((2 * lanes, LANES), F32),
        ((modes * SUB, chans), F32), ((modes, chans), F32), ((2 * SUB, chans), F32),
    ]

    def upper(copies):
        *own, message, first_message = scan(third_scan, [small, large], gather_in(2, copies, runs))
        across = lax.ppermute(first_message, "ctx", hops((runs[4], runs[6]), (runs[5], runs[7])))
        cross = lax.ppermute(first_message, "ctx", hops((runs[4], runs[7]), (runs[5], runs[6])))
        *own, message = scan(fourth_scan, [small], gather_in(3, copies, runs), *own, message)
        following = lax.ppermute(message, "ctx", hops((runs[4], runs[5]), (runs[6], runs[7])))
        ready = call(
            lambda *refs: prepare(count, lanes, *refs),
            prepared,
            across, cross, following, *own, rate_pack, taps_pack, residue_pack, rates, weights,
        )
        return *call(lambda *refs: None, [result], out_hbm=(0,)), inner(), *ready

    def rest(copies):
        common = [rate_pack, residue_pack, taps_pack, rates, query, weights, product]
        (mixed,) = call(
            lower_output, [result], *lower_kept[:4], *common, *lower_kept[4:], scratch=room + [pltpu.VMEM(*held)] + work, out_hbm=(0,)
        )
        return mixed, *nothing(held, *prepared)

    mixed, local, *ready = lax.cond(group >= 2, upper, rest, near)
    (mixed,) = call(
        upper_output,
        [result],
        *ready, residue_pack, rate_pack, taps_pack, query, local, to_third, to_fourth, mixed,
        scratch=work[:2] + [pltpu.SemaphoreType.DMA((lanes,))], in_hbm=(13,), out_hbm=(0,), aliases={13: 0},
    )
    return mixed


def solution(mesh):
    in_specs = (P("ctx", "ch"), P("ch"), P(None, None, "ch"), P("ch", None), P("ch", None))
    out_specs = P("ctx", "ch")
    return jax.shard_map(
        per_device, mesh=mesh, in_specs=in_specs, out_specs=out_specs, check_vma=False
    )
```

```python
import jax
import jax.numpy as jnp
from jax import lax
from jax.experimental import pallas as pl
from jax.experimental.pallas import tpu as pltpu
from jax.sharding import PartitionSpec as P

EXACT = lax.Precision.HIGHEST
EPSILON = 1e-05
SUB = 8
LANES = 128
WIDE = 16
NEAR = 8

F32 = jnp.float32
BF16 = jnp.bfloat16


def call(body, outs, *args, scratch=(), flops=0, space=pltpu.VMEM, in_hbm=(), out_hbm=(), out_any=(), aliases=None):
    shapes = [jax.ShapeDtypeStruct(s, d) for s, d in outs]
    spaces = [pltpu.HBM if i in in_hbm else space for i in range(len(args))]
    out_spaces = [pltpu.HBM if i in out_hbm else pl.ANY if i in out_any else pltpu.VMEM for i in range(len(outs))]
    moved = sum(a.size * a.dtype.itemsize for a in args)
    return pl.pallas_call(
        body,
        out_shape=shapes,
        in_specs=[pl.BlockSpec(memory_space=m) for m in spaces],
        out_specs=[pl.BlockSpec(memory_space=m) for m in out_spaces],
        scratch_shapes=list(scratch),
        input_output_aliases=aliases or {},
        compiler_params=pltpu.CompilerParams(vmem_limit_bytes=16 * 2**20),
        cost_estimate=pl.CostEstimate(flops=flops, bytes_accessed=moved, transcendentals=0),
    )(*args)


def pack(ref):
    return jnp.concatenate([ref[:, l * LANES : (l + 1) * LANES] for l in range(ref.shape[1] // LANES)], axis=0)


def square_sums(*refs):
    count = 5
    held, outs, refs = refs[:count], refs[count : 2 * count], refs[2 * count :]
    sums_ref, taps_pack, rate_pack, residue_pack, sem = refs
    stream_ref, _, taps_ref, rate_ref, residue_ref = outs
    lanes = stream_ref.shape[1] // LANES
    cuts = [pl.ds(l * LANES, LANES) for l in range(lanes)]
    copies = [pltpu.make_async_copy(held[0].at[:, at], stream_ref.at[:, at], sem.at[i]) for i, at in enumerate(cuts)]
    copies += [pltpu.make_async_copy(held[i], outs[i], sem.at[lanes + i - 1]) for i in range(1, count)]
    for copy in copies:
        copy.start()
    total = 0.0
    for copy, at in zip(copies, cuts):
        copy.wait()
        values = stream_ref[:, at].astype(F32)
        total = total + values * values
    sums = jnp.sum(total.T, axis=0, keepdims=True)
    for peer in range(sums_ref.shape[0]):
        sums_ref[peer] = sums
    for copy in copies[lanes:]:
        copy.wait()
    rate_pack[...] = pack(rate_ref)
    residue_pack[...] = pack(residue_ref)
    for tap in range(3):
        for role in range(3):
            for l in range(lanes):
                taps_pack[pl.ds((tap * 3 + role) * lanes + l, 1), :] = taps_ref[tap, pl.ds(role, 1), pl.ds(l * LANES, LANES)]


def block_states(chan_total, sums_ref, stream_ref, gain_ref, taps_ref, rate_ref, query_ref, product_ref, wide_ref, near_ref, edge_ref, end_ref, whole_ref):
    count, chans = stream_ref.shape
    lanes = chans // LANES
    modes = rate_ref.shape[0]
    blocks = count // SUB
    sums = sums_ref[0]
    for peer in range(1, sums_ref.shape[0]):
        sums = sums + sums_ref[peer]
    rest = lax.rsqrt(sums / chan_total + EPSILON)
    rows = lax.broadcasted_iota(jnp.int32, (2 * SUB, count), 0)
    parts = jnp.zeros((2 * SUB, count), F32)
    for i in range(3):
        part = rest.astype(BF16).astype(F32)
        parts = jnp.where(rows == i, part, parts)
        rest = rest - part
    scale = lax.dot_general(
        parts.astype(BF16), jnp.ones((2 * SUB, LANES), BF16), (((0,), (0,)), ((), ())), preferred_element_type=F32
    )
    row = lax.broadcasted_iota(jnp.int32, (SUB, LANES), 0)
    lag = (SUB - 1 - row).astype(F32)

    def one_lane(lane, carry):
        at = pl.ds(pl.multiple_of(lane * LANES, LANES), LANES)
        gain = jnp.broadcast_to(gain_ref[:, at], (SUB, LANES))
        taps = [[jnp.broadcast_to(taps_ref[j, pl.ds(role, 1), at], (SUB, LANES)) for j in range(3)] for role in range(3)]
        before = [jnp.zeros((SUB, LANES), F32)] * 2
        products, queries = [], []
        for i in range(blocks):
            if i % 2 == 0:
                pair = stream_ref[pl.ds(i * SUB, 2 * SUB), at].astype(F32)
            normed = pair[i % 2 * SUB : (i % 2 + 1) * SUB] * scale[i * SUB : (i + 1) * SUB] * gain
            normed = normed.astype(BF16).astype(F32)
            if i == 0:
                edge_ref[:2, at] = normed[:2]
            if i == blocks - 1:
                edge_ref[2:4, at] = normed[SUB - 2 :]
            rolled = [pltpu.roll(normed, j, 0) for j in (1, 2)]
            shifted = [normed] + [jnp.where(row < j, b, r) for j, b, r in zip((1, 2), before, rolled)]
            before = rolled
            query, key, value = [sum(t * n for t, n in zip(taps[role], shifted)) for role in range(3)]
            product = (key * value).astype(BF16).astype(F32)
            if i == 0:
                product = jnp.where(row < 2, 0.0, product)
            product_ref[pl.ds(i * SUB, SUB), at] = product
            products.append(product)
            queries.append(query)
            if i % 2 == 1:
                query_ref[pl.ds((i - 1) * SUB, 2 * SUB), at] = jnp.concatenate(queries[-2:], axis=0).astype(BF16)
        for mode in range(modes):
            rate = rate_ref[pl.ds(mode, 1), at]
            step = jnp.broadcast_to(jnp.exp(-SUB * rate), (SUB, LANES))
            total = products[0]
            for product in products[1:]:
                total = total * step + product
            end_ref[pl.ds(mode, 1), at] = jnp.sum(total * jnp.exp(-rate * lag), axis=0, keepdims=True)
        return carry

    lax.fori_loop(0, lanes, one_lane, 0, unroll=True)
    whole_ref[: lanes * modes] = pack(end_ref)
    for e in range(4):
        for l in range(lanes):
            whole_ref[pl.ds(lanes * (modes + e) + l, 1), :] = edge_ref[pl.ds(e, 1), pl.ds(l * LANES, LANES)]
    message = whole_ref[...].astype(BF16)
    for ref in (wide_ref, near_ref):
        for peer in range(ref.shape[0]):
            ref[peer] = message


def first_rows(taps_ref, role, last, head):
    lanes = taps_ref.shape[0] // 9
    taps = [taps_ref[pl.ds((3 * j + role) * lanes, lanes)] for j in range(3)]
    first = taps[0] * head[0] + taps[1] * last[1] + taps[2] * last[0]
    second = taps[0] * head[1] + taps[1] * head[0] + taps[2] * last[1]
    return first, second


def first_products(taps_ref, last, head):
    keys, values = first_rows(taps_ref, 1, last, head), first_rows(taps_ref, 2, last, head)
    return [(k * v).astype(BF16).astype(F32) for k, v in zip(keys, values)]


def spread(rows, modes):
    return jnp.concatenate([jnp.broadcast_to(rows[l : l + 1], (modes, LANES)) for l in range(rows.shape[0])], axis=0)


def pairs(ref, start, lanes):
    return ref[start : start + lanes], ref[start + lanes : start + 2 * lanes]


def step_over(block, lanes, rates, taps_ref, state, last, run):
    states = rates.shape[0]
    modes = states // lanes
    first, second = first_products(taps_ref, last, pairs(run, states, lanes))
    end = run[:states] + state * jnp.exp(-block * rates)
    end = end + jnp.exp(-(block - 1) * rates) * spread(first, modes) + jnp.exp(-(block - 2) * rates) * spread(second, modes)
    return end, pairs(run, states + 2 * lanes, lanes)


def step_into(block, lanes, place, rates, taps_ref, state, last, edge_ref, before_ref):
    states = rates.shape[0]
    modes = states // lanes
    first, second = first_products(taps_ref, last, pairs(edge_ref, 0, lanes))
    lag = (block * place).astype(F32)
    held = jnp.exp(-rates * jnp.maximum(lag - 1.0, 0.0)) * spread(first, modes)
    held = held + jnp.exp(-rates * jnp.maximum(lag - 2.0, 0.0)) * spread(second, modes)
    state = before_ref[...] + state * jnp.exp(-rates * lag) + jnp.where(place > 0, held, 0.0)
    inside = pairs(edge_ref, 2 * lanes, lanes)
    return state, [jnp.where(place > 0, a, b) for a, b in zip(inside, last)]


def slot(place, size):
    return size - 1 - place


def near_scan(block, lanes, got_ref, rate_ref, taps_ref, before_ref, edge_ref):
    size = got_ref.shape[0]
    place = lax.axis_index("ctx") % size
    states = rate_ref.shape[0]
    rates = rate_ref[...]
    run = got_ref[slot(0, size)].astype(F32)
    head = run[states : states + 2 * lanes]
    total, last = run[:states], pairs(run, states + 2 * lanes, lanes)
    before = jnp.where(place == 1, total, jnp.zeros_like(total))
    for j in range(1, size):
        total, last = step_over(block, lanes, rates, taps_ref, total, last, got_ref[slot(j, size)].astype(F32))
        if j < size - 1:
            before = jnp.where(place == j + 1, total, before)
    before_ref[...] = before
    edge_ref[: 2 * lanes] = head
    edge_ref[2 * lanes : 4 * lanes] = got_ref[slot(jnp.maximum(place - 1, 0), size)].astype(F32)[states + 2 * lanes :]
    edge_ref[4 * lanes :] = got_ref[slot(place, size)].astype(F32)[states : states + 2 * lanes]
    return jnp.concatenate([total, head, *last], axis=0)


def write(message, *refs):
    for ref in refs:
        rest = ref.shape[0] - message.shape[0]
        whole = jnp.concatenate([message, jnp.zeros((rest, LANES), F32)], axis=0) if rest else message
        ref[...] = whole.astype(BF16)


def first_scan(block, lanes, got_ref, rate_ref, taps_ref, before_ref, edge_ref, message_ref):
    @pl.when(lax.axis_index("ctx") // WIDE == 0)
    def _():
        write(near_scan(block, lanes, got_ref, rate_ref, taps_ref, before_ref, edge_ref), message_ref)


def second_scan(block, lanes, got_ref, rate_ref, taps_ref, before_ref, edge_ref, message_ref):
    @pl.when(lax.axis_index("ctx") // WIDE == 1)
    def _():
        message_ref[...] = near_scan(block, lanes, got_ref, rate_ref, taps_ref, before_ref, edge_ref)


def relay(block, lanes, came_ref, own_ref, rate_ref, taps_ref, kept_ref, *message_refs):
    @pl.when(lax.axis_index("ctx") // WIDE == 1)
    def _():
        rates = rate_ref[...]
        state, last = jnp.zeros_like(rates), [jnp.zeros((lanes, LANES), F32)] * 2
        came = came_ref[...].astype(F32)
        kept_ref[...] = came
        for run in (came, own_ref[...]):
            state, last = step_over(block * WIDE, lanes, rates, taps_ref, state, last, run)
        write(jnp.concatenate([state, *last], axis=0), *message_refs)


def third_scan(block, lanes, got_ref, rate_ref, taps_ref, before_ref, edge_ref, *message_refs):
    @pl.when(lax.axis_index("ctx") // WIDE == 2)
    def _():
        write(near_scan(block, lanes, got_ref, rate_ref, taps_ref, before_ref, edge_ref), *message_refs)


def fourth_scan(block, lanes, got_ref, third_before, third_edge, third_message, rate_ref, taps_ref, before_ref, edge_ref, message_ref):
    group = lax.axis_index("ctx") // WIDE

    @pl.when(group == 2)
    def _():
        before_ref[...] = third_before[...]
        edge_ref[...] = third_edge[...]
        message_ref[...] = third_message[...]

    @pl.when(group == 3)
    def _():
        write(near_scan(block, lanes, got_ref, rate_ref, taps_ref, before_ref, edge_ref), message_ref)


def prepare(block, lanes, across_ref, cross_ref, next_ref, before_ref, edge_ref, rate_ref, taps_ref, residue_ref, rates_ref, weights_ref, rest_ref, decay_ref, head_ref, lead_ref, step_ref, fixed_ref):
    index = lax.axis_index("ctx")
    run, place = index // NEAR, index % NEAR
    states = rate_ref.shape[0]
    modes = states // lanes
    rates = rate_ref[...]
    across, cross, following = [r[: states + 4 * lanes].astype(F32) for r in (across_ref, cross_ref, next_ref)]
    start = jnp.where(run == 5, following, jnp.where(run == 6, across, cross))
    state, last = start[:states], pairs(start, states + 2 * lanes, lanes)
    for needed, message in ((run > 5, jnp.where(run == 6, cross, across)), (run > 6, following)):
        after, after_last = step_over(block * NEAR, lanes, rates, taps_ref, state, last, message)
        state, last = jnp.where(needed, after, state), [jnp.where(needed, a, b) for a, b in zip(after_last, last)]
    into, own_last = step_into(block, lanes, place, rates, taps_ref, state, last, edge_ref, before_ref)
    state = jnp.where(run > 4, into, before_ref[...])
    length = (block * (NEAR * (run - 4) + place)).astype(F32)
    away = length > 0
    own_head = pairs(edge_ref, 4 * lanes, lanes)
    first, second = first_products(taps_ref, own_last, own_head)
    ahead = jnp.exp(rates) * spread(second, modes)
    rest_ref[...] = state * jnp.exp(-rates) + jnp.where(away, spread(first, modes) + ahead, 0.0)
    for i in range(3):
        decay_ref[pl.ds(i * states, states)] = jnp.exp(-rates * (length + (1.0 - i)))
    head_ref[...] = jnp.where(run > 4, start[states : states + 2 * lanes], edge_ref[: 2 * lanes])
    ahead = jnp.where(away, ahead * residue_ref[...], 0.0)
    query = [q.astype(BF16).astype(F32) for q in first_rows(taps_ref, 0, own_last, own_head)]
    fix_rows(lanes, ahead, query, fixed_ref, 0)
    row = lax.broadcasted_iota(jnp.int32, (SUB, weights_ref.shape[1]), 0).astype(F32)
    step_ref[...] = jnp.exp(-SUB * rates_ref[...])
    for mode in range(modes):
        at = pl.ds(mode, 1)
        lead_ref[pl.ds(mode * SUB, SUB)] = weights_ref[at] * jnp.exp(-rates_ref[at] * row)


def fix_rows(lanes, ahead, query, out_ref, start):
    modes = ahead.shape[0] // lanes
    row = lax.broadcasted_iota(jnp.int32, (SUB, LANES), 0)
    for l in range(lanes):
        extra = jnp.sum(ahead[l * modes : (l + 1) * modes], axis=0, keepdims=True)
        take = jnp.where(row == 0, jnp.broadcast_to(extra, row.shape), 0.0)
        fixed = jnp.where(row == 0, query[0][l : l + 1], jnp.where(row == 1, query[1][l : l + 1], 0.0))
        out_ref[start : start + SUB, pl.ds(l * LANES, LANES)] = take
        out_ref[start + SUB : start + 2 * SUB, pl.ds(l * LANES, LANES)] = fixed


def add_mode(totals, term, rate):
    step = jnp.broadcast_to(jnp.exp(-SUB * rate), term.shape)
    out = []
    for total in totals:
        out.append(total + term)
        term = term * step
    return out


def inner_conv(rate_ref, residue_ref, product_ref, local_ref, filter_ref):
    count, chans = product_ref.shape
    modes = rate_ref.shape[0]
    blocks = count // SUB
    row = lax.broadcasted_iota(jnp.int32, (SUB, LANES), 0)
    lead = row.astype(F32)

    def one_lane(lane, carry):
        at = pl.ds(pl.multiple_of(lane * LANES, LANES), LANES)
        zero = jnp.zeros((SUB, LANES), F32)
        totals = [zero] * blocks
        for mode in range(modes):
            rate = rate_ref[pl.ds(mode, 1), at]
            term = residue_ref[pl.ds(mode, 1), at] * jnp.exp(-rate * lead)
            totals = add_mode(totals, term, rate)
        for i in range(blocks):
            filter_ref[pl.ds(i * SUB, SUB), :] = totals[i]

        shifted = [product_ref[pl.ds(i * SUB, SUB), at] for i in range(blocks)]
        totals = [zero] * blocks
        for b in range(SUB):
            for a in range(blocks):
                weight = filter_ref[pl.ds(a * SUB + b, 1), :]
                for j in range(blocks - a):
                    totals[j + a] = totals[j + a] + weight * shifted[j]
            if b < SUB - 1:
                rolled = [pltpu.roll(s, 1, 0) for s in shifted]
                shifted = [jnp.where(row == 0, before, now) for before, now in zip([zero] + rolled[:-1], rolled)]
        for i in range(blocks):
            local_ref[pl.ds(i * SUB, SUB), at] = totals[i]
        return carry

    lax.fori_loop(0, chans // LANES, one_lane, 0)


def finish(place, state, last, edge_ref, before_ref, rate_pack, residue_pack, taps_ref, rate_ref, query_ref, local_ref, mixed_ref, state_ref):
    count, chans = local_ref.shape
    lanes = chans // LANES
    modes = rate_ref.shape[0]
    states = lanes * modes
    blocks = count // SUB
    rates = rate_pack[...]
    state, own_last = step_into(count, lanes, place, rates, taps_ref, state, last, edge_ref, before_ref)
    own_head = pairs(edge_ref, 4 * lanes, lanes)
    own_query = [q.astype(BF16).astype(F32) for q in first_rows(taps_ref, 0, own_last, own_head)]
    first, second = first_products(taps_ref, own_last, own_head)
    ahead = jnp.exp(rates) * spread(second, modes)
    state = state * jnp.exp(-rates) + spread(first, modes) + ahead
    state = state * residue_pack[...]
    ahead = ahead * residue_pack[...]
    fix_rows(lanes, ahead, own_query, state_ref, modes)
    lead = lax.broadcasted_iota(jnp.int32, (SUB, LANES), 0).astype(F32)
    for l in range(lanes):
        state_ref[:modes, pl.ds(l * LANES, LANES)] = state[l * modes : (l + 1) * modes]

    def one_lane(lane, carry):
        at = pl.ds(pl.multiple_of(lane * LANES, LANES), LANES)
        totals = [local_ref[pl.ds(i * SUB, SUB), at] for i in range(blocks)]
        for mode in range(modes):
            rate = rate_ref[pl.ds(mode, 1), at]
            term = state_ref[pl.ds(mode, 1), at] * jnp.exp(-rate * lead)
            totals = add_mode(totals, term, rate)
        gate(totals, at, state_ref, modes, query_ref, mixed_ref)
        return carry

    lax.fori_loop(0, lanes, one_lane, 0)


def gate(totals, at, fixed_ref, start, query_ref, mixed_ref):
    totals[0] = totals[0] - fixed_ref[pl.ds(start, SUB), at]
    rows = lax.broadcasted_iota(jnp.int32, (2 * SUB, LANES), 0)
    for i in range(0, len(totals), 2):
        where = pl.ds(i * SUB, 2 * SUB)
        conv = jnp.concatenate(totals[i : i + 2], axis=0).astype(BF16).astype(F32)
        query = query_ref[where, at].astype(F32)
        if i == 0:
            fixed = fixed_ref[pl.ds(start + SUB, SUB), at]
            query = jnp.where(rows < 2, jnp.concatenate([fixed, fixed], axis=0), query)
        mixed_ref[where, at] = (query * conv).astype(BF16)


def leave(mixed_ref, out_ref, sem):
    copy = pltpu.make_async_copy(mixed_ref, out_ref, sem)
    copy.start()
    copy.wait()


def convolves_early():
    index = lax.axis_index("ctx")
    return index < WIDE + WIDE // 2


def early_inner(rate_ref, residue_ref, product_ref, after_ref, local_ref, filter_ref):
    @pl.when(convolves_early())
    def _():
        inner_conv(rate_ref, residue_ref, product_ref, local_ref, filter_ref)


def lower_output(first_before, first_edge, second_before, second_edge, rate_pack, residue_pack, taps_ref, rate_ref, query_ref, residue_ref, product_ref, held_ref, low_ref, out_ref, filter_ref, local_ref, state_ref, mixed_ref, sem):
    early = convolves_early()

    @pl.when(early)
    def _():
        local_ref[...] = held_ref[...]

    @pl.when(jnp.logical_not(early))
    def _():
        inner_conv(rate_ref, residue_ref, product_ref, local_ref, filter_ref)

    index = lax.axis_index("ctx")
    rates = rate_pack[...]
    second = index >= WIDE
    state, last = jnp.zeros_like(rates), [jnp.zeros((taps_ref.shape[0] // 9, LANES), F32)] * 2
    after, after_last = step_over(local_ref.shape[0] * WIDE, len(last[0]), rates, taps_ref, state, last, low_ref[...])
    state, last = jnp.where(second, after, state), [jnp.where(second, a, b) for a, b in zip(after_last, last)]
    before = jnp.where(second, second_before[...], first_before[...])
    edges = jnp.where(second, second_edge[...], first_edge[...])
    finish(index % WIDE, state, last, edges, before, rate_pack, residue_pack, taps_ref, rate_ref, query_ref, local_ref, mixed_ref, state_ref)
    leave(mixed_ref, out_ref, sem)


def upper_output(rest_ref, decay_ref, head_ref, lead_ref, step_ref, fixed_ref, residue_ref, rate_ref, taps_ref, query_ref, local_ref, third_ref, fourth_ref, held_ref, out_ref, state_ref, mixed_ref, sem):
    index = lax.axis_index("ctx")
    states = rest_ref.shape[0]
    lanes = taps_ref.shape[0] // 9
    modes = states // lanes
    blocks = local_ref.shape[0] // SUB

    @pl.when(index >= 2 * WIDE)
    def _():
        came = third_ref[...].astype(F32) + fourth_ref[: states + 4 * lanes].astype(F32)
        last = pairs(came, states, lanes)
        head = pairs(head_ref, 0, lanes)
        first, second = first_products(taps_ref, last, head)
        ahead = spread(second, modes)
        state = rest_ref[...] + came[:states] * decay_ref[:states]
        state = state + spread(first, modes) * decay_ref[states : 2 * states] + ahead * decay_ref[2 * states :]
        for l in range(lanes):
            state_ref[:modes, pl.ds(l * LANES, LANES)] = state[l * modes : (l + 1) * modes]
        state_ref[modes:] = fixed_ref[...]

        @pl.when(index == 2 * WIDE)
        def _():
            query = [q.astype(BF16).astype(F32) for q in first_rows(taps_ref, 0, last, head)]
            fix_rows(lanes, jnp.exp(rate_ref[...]) * ahead * residue_ref[...], query, state_ref, modes)

        def one_lane(lane, carry):
            at = pl.ds(pl.multiple_of(lane * LANES, LANES), LANES)
            totals = [local_ref[pl.ds(i * SUB, SUB), at] for i in range(blocks)]
            for mode in range(modes):
                step = jnp.broadcast_to(step_ref[pl.ds(mode, 1), at], (SUB, LANES))
                term = state_ref[pl.ds(mode, 1), at] * lead_ref[pl.ds(mode * SUB, SUB), at]
                for i in range(blocks):
                    totals[i] = totals[i] + term
                    if i < blocks - 1:
                        term = term * step
            gate(totals, at, state_ref, modes, query_ref, mixed_ref)
            pltpu.make_async_copy(mixed_ref.at[:, at], out_ref.at[:, at], sem.at[lane]).start()
            return carry

        lax.fori_loop(0, lanes, one_lane, 0, unroll=True)
        for l in range(lanes):
            at = pl.ds(l * LANES, LANES)
            pltpu.make_async_copy(mixed_ref.at[:, at], out_ref.at[:, at], sem.at[l]).wait()


def gather(copies, axis, groups=None):
    return lax.all_to_all(copies, axis, 0, 0, tiled=True, axis_index_groups=groups)


def per_device(stream, norm_gain, short_filter, decay_rate, residue):
    count, chans = stream.shape
    modes = decay_rate.shape[1]
    lanes = chans // LANES
    states = lanes * modes
    peers = lax.axis_size("ch")
    ctx = lax.axis_size("ctx")
    groups = [[g + m for m in range(WIDE)] for g in range(0, ctx, WIDE)]
    runs = [[g + m for m in range(NEAR)] for g in range(0, ctx, NEAR)]
    index, stream = lax.optimization_barrier((lax.axis_index("ctx"), stream))
    held = [stream, norm_gain[None, :], short_filter, decay_rate.T, residue.T]
    held = [pltpu.with_memory_space_constraint(h, pltpu.HBM) for h in held]
    stream, gain, taps, rates, weights, sums, taps_pack, rate_pack, residue_pack = call(
        square_sums,
        [(h.shape, h.dtype) for h in held]
        + [((peers, 1, count), F32), ((9 * lanes, LANES), F32), ((states, LANES), F32), ((states, LANES), F32)],
        *held,
        scratch=[pltpu.SemaphoreType.DMA((lanes + len(held) - 1,))],
        space=pltpu.HBM,
    )
    sums = lax.cond(index < ctx, lambda c: gather(c, "ch", [list(range(peers))[::-1]]), lambda c: c, sums)
    query, product, wide, near = call(
        lambda *refs: block_states(chans * peers, *refs),
        [((count, chans), BF16), ((count, chans), F32), ((WIDE, states + 4 * lanes, LANES), BF16), ((NEAR, states + 4 * lanes, LANES), BF16)],
        sums, stream, gain, taps, rates,
        scratch=[pltpu.VMEM((SUB, chans), F32), pltpu.VMEM((modes, chans), F32), pltpu.VMEM((states + 4 * lanes, LANES), F32)],
    )
    index, wide, near = lax.optimization_barrier((index, wide, near))
    group = lax.shift_right_logical(index, WIDE.bit_length() - 1)
    small, large = ((states + 4 * lanes, LANES), BF16), ((states + 8 * lanes, LANES), BF16)
    kept = [((states, LANES), F32), ((6 * lanes, LANES), F32)]
    nothing = lambda *shapes: tuple(call(lambda *refs: None, shapes, out_any=range(len(shapes))))
    hops = lambda *ends: [pair for a, b in ends for pair in zip(a, b)]
    first, second, third, fourth = groups
    scan = lambda body, outs, *args: call(
        lambda *refs: body(count, lanes, *refs), [*kept, *outs], *args, rate_pack, taps_pack
    )

    def gather_in(number, copies, members):
        size = len(members[0])
        order = sorted(range(size), key=lambda j: slot(j, size))
        members = [[g[j] for j in order] for g in members]
        return lax.cond(
            group == number, lambda c: gather(c, "ctx", members), lambda c: nothing((c.shape, c.dtype))[0], copies
        )

    def inner():
        return call(
            inner_conv, [((count, chans), F32)], rates, weights, product, scratch=[pltpu.VMEM((count, LANES), F32)], flops=10**7
        )[0]

    room = [pltpu.VMEM((count, LANES), F32)]
    work = [pltpu.VMEM((modes + 2 * SUB, chans), F32), pltpu.VMEM((count, chans), BF16), pltpu.SemaphoreType.DMA]
    whole = (small[0], F32)
    held, result = ((count, chans), F32), ((count, chans), BF16)

    def lower(copies):
        *first_kept, message = scan(first_scan, [small], gather_in(0, copies, groups))
        low = lax.ppermute(message, "ctx", hops((first, second)))
        (local,) = call(early_inner, [held], rates, weights, product, message, scratch=room, flops=10**7)
        copies, local = lax.optimization_barrier((copies, local))
        *second_kept, message = scan(second_scan, [whole], gather_in(1, copies, groups))
        onward = call(lambda *refs: relay(count, lanes, *refs), [whole, small, large], low, message, rate_pack, taps_pack)
        return *first_kept, *second_kept, local, *onward

    *lower_kept, to_third, to_fourth = lax.cond(
        group < 2, lower, lambda c: nothing(*kept, *kept, held, whole, small, large), wide
    )
    half = WIDE // 2
    to_fourth = lax.ppermute(to_fourth, "ctx", hops((second, fourth[half:] + fourth[:half])))
    to_third = lax.ppermute(to_third, "ctx", hops((second, third)))

    prepared = [
        ((states, LANES), F32), ((3 * states, LANES), F32), ((2 * lanes, LANES), F32),
        ((modes * SUB, chans), F32), ((modes, chans), F32), ((2 * SUB, chans), F32),
    ]

    def upper(copies):
        *own, message, first_message = scan(third_scan, [small, large], gather_in(2, copies, runs))
        across = lax.ppermute(first_message, "ctx", hops((runs[4], runs[6]), (runs[5], runs[7])))
        cross = lax.ppermute(first_message, "ctx", hops((runs[4], runs[7]), (runs[5], runs[6])))
        *own, message = scan(fourth_scan, [small], gather_in(3, copies, runs), *own, message)
        following = lax.ppermute(message, "ctx", hops((runs[4], runs[5]), (runs[6], runs[7])))
        ready = call(
            lambda *refs: prepare(count, lanes, *refs),
            prepared,
            across, cross, following, *own, rate_pack, taps_pack, residue_pack, rates, weights,
        )
        return *call(lambda *refs: None, [result], out_hbm=(0,)), inner(), *ready

    def rest(copies):
        common = [rate_pack, residue_pack, taps_pack, rates, query, weights, product]
        (mixed,) = call(
            lower_output, [result], *lower_kept[:4], *common, *lower_kept[4:], scratch=room + [pltpu.VMEM(*held)] + work, out_hbm=(0,)
        )
        return mixed, *nothing(held, *prepared)

    mixed, local, *ready = lax.cond(group >= 2, upper, rest, near)
    (mixed,) = call(
        upper_output,
        [result],
        *ready, residue_pack, rate_pack, taps_pack, query, local, to_third, to_fourth, mixed,
        scratch=work[:2] + [pltpu.SemaphoreType.DMA((lanes,))], in_hbm=(13,), out_hbm=(0,), aliases={13: 0},
    )
    return mixed


def solution(mesh):
    in_specs = (P("ctx", "ch"), P("ch"), P(None, None, "ch"), P("ch", None), P("ch", None))
    out_specs = P("ctx", "ch")
    return jax.shard_map(
        per_device, mesh=mesh, in_specs=in_specs, out_specs=out_specs, check_vma=False
    )
```

```python
import jax
import jax.numpy as jnp
from jax import lax
from jax.experimental import pallas as pl
from jax.experimental.pallas import tpu as pltpu
from jax.sharding import PartitionSpec as P

EXACT = lax.Precision.HIGHEST
EPSILON = 1e-05
SUB = 8
LANES = 128
WIDE = 16
NEAR = 8

F32 = jnp.float32
BF16 = jnp.bfloat16


def call(body, outs, *args, scratch=(), flops=0, space=pltpu.VMEM, in_hbm=(), out_hbm=(), out_any=(), aliases=None):
    shapes = [jax.ShapeDtypeStruct(s, d) for s, d in outs]
    spaces = [pltpu.HBM if i in in_hbm else space for i in range(len(args))]
    out_spaces = [pltpu.HBM if i in out_hbm else pl.ANY if i in out_any else pltpu.VMEM for i in range(len(outs))]
    moved = sum(a.size * a.dtype.itemsize for a in args)
    return pl.pallas_call(
        body,
        out_shape=shapes,
        in_specs=[pl.BlockSpec(memory_space=m) for m in spaces],
        out_specs=[pl.BlockSpec(memory_space=m) for m in out_spaces],
        scratch_shapes=list(scratch),
        input_output_aliases=aliases or {},
        compiler_params=pltpu.CompilerParams(vmem_limit_bytes=16 * 2**20),
        cost_estimate=pl.CostEstimate(flops=flops, bytes_accessed=moved, transcendentals=0),
    )(*args)


def pack(ref):
    return jnp.concatenate([ref[:, l * LANES : (l + 1) * LANES] for l in range(ref.shape[1] // LANES)], axis=0)


def square_sums(*refs):
    count = 5
    held, outs, refs = refs[:count], refs[count : 2 * count], refs[2 * count :]
    sums_ref, taps_pack, rate_pack, residue_pack, sem = refs
    stream_ref, _, taps_ref, rate_ref, residue_ref = outs
    lanes = stream_ref.shape[1] // LANES
    cuts = [pl.ds(l * LANES, LANES) for l in range(lanes)]
    copies = [pltpu.make_async_copy(held[0].at[:, at], stream_ref.at[:, at], sem.at[i]) for i, at in enumerate(cuts)]
    copies += [pltpu.make_async_copy(held[i], outs[i], sem.at[lanes + i - 1]) for i in range(1, count)]
    for copy in copies:
        copy.start()
    total = 0.0
    for copy, at in zip(copies, cuts):
        copy.wait()
        values = stream_ref[:, at].astype(F32)
        total = total + values * values
    sums = jnp.sum(total.T, axis=0, keepdims=True)
    for peer in range(sums_ref.shape[0]):
        sums_ref[peer] = sums
    for copy in copies[lanes:]:
        copy.wait()
    rate_pack[...] = pack(rate_ref)
    residue_pack[...] = pack(residue_ref)
    for tap in range(3):
        for role in range(3):
            for l in range(lanes):
                taps_pack[pl.ds((tap * 3 + role) * lanes + l, 1), :] = taps_ref[tap, pl.ds(role, 1), pl.ds(l * LANES, LANES)]


def block_states(chan_total, sums_ref, stream_ref, gain_ref, taps_ref, rate_ref, query_ref, product_ref, wide_ref, near_ref, edge_ref, end_ref, whole_ref):
    count, chans = stream_ref.shape
    lanes = chans // LANES
    modes = rate_ref.shape[0]
    blocks = count // SUB
    sums = sums_ref[0]
    for peer in range(1, sums_ref.shape[0]):
        sums = sums + sums_ref[peer]
    rest = lax.rsqrt(sums / chan_total + EPSILON)
    rows = lax.broadcasted_iota(jnp.int32, (2 * SUB, count), 0)
    parts = jnp.zeros((2 * SUB, count), F32)
    for i in range(3):
        part = rest.astype(BF16).astype(F32)
        parts = jnp.where(rows == i, part, parts)
        rest = rest - part
    scale = lax.dot_general(
        parts.astype(BF16), jnp.ones((2 * SUB, LANES), BF16), (((0,), (0,)), ((), ())), preferred_element_type=F32
    )
    row = lax.broadcasted_iota(jnp.int32, (SUB, LANES), 0)
    lag = (SUB - 1 - row).astype(F32)

    def one_lane(lane, carry):
        at = pl.ds(pl.multiple_of(lane * LANES, LANES), LANES)
        gain = jnp.broadcast_to(gain_ref[:, at], (SUB, LANES))
        taps = [[jnp.broadcast_to(taps_ref[j, pl.ds(role, 1), at], (SUB, LANES)) for j in range(3)] for role in range(3)]
        before = [jnp.zeros((SUB, LANES), F32)] * 2
        products, queries = [], []
        for i in range(blocks):
            if i % 2 == 0:
                pair = stream_ref[pl.ds(i * SUB, 2 * SUB), at].astype(F32)
            normed = pair[i % 2 * SUB : (i % 2 + 1) * SUB] * scale[i * SUB : (i + 1) * SUB] * gain
            normed = normed.astype(BF16).astype(F32)
            if i == 0:
                edge_ref[:2, at] = normed[:2]
            if i == blocks - 1:
                edge_ref[2:4, at] = normed[SUB - 2 :]
            rolled = [pltpu.roll(normed, j, 0) for j in (1, 2)]
            shifted = [normed] + [jnp.where(row < j, b, r) for j, b, r in zip((1, 2), before, rolled)]
            before = rolled
            query, key, value = [sum(t * n for t, n in zip(taps[role], shifted)) for role in range(3)]
            product = (key * value).astype(BF16).astype(F32)
            if i == 0:
                product = jnp.where(row < 2, 0.0, product)
            product_ref[pl.ds(i * SUB, SUB), at] = product
            products.append(product)
            queries.append(query)
            if i % 2 == 1:
                query_ref[pl.ds((i - 1) * SUB, 2 * SUB), at] = jnp.concatenate(queries[-2:], axis=0).astype(BF16)
        for mode in range(modes):
            rate = rate_ref[pl.ds(mode, 1), at]
            step = jnp.broadcast_to(jnp.exp(-SUB * rate), (SUB, LANES))
            total = products[0]
            for product in products[1:]:
                total = total * step + product
            end_ref[pl.ds(mode, 1), at] = jnp.sum(total * jnp.exp(-rate * lag), axis=0, keepdims=True)
        return carry

    lax.fori_loop(0, lanes, one_lane, 0, unroll=True)
    whole_ref[: lanes * modes] = pack(end_ref)
    for e in range(4):
        for l in range(lanes):
            whole_ref[pl.ds(lanes * (modes + e) + l, 1), :] = edge_ref[pl.ds(e, 1), pl.ds(l * LANES, LANES)]
    message = whole_ref[...].astype(BF16)
    for ref in (wide_ref, near_ref):
        for peer in range(ref.shape[0]):
            ref[peer] = message


def first_rows(taps_ref, role, last, head):
    lanes = taps_ref.shape[0] // 9
    taps = [taps_ref[pl.ds((3 * j + role) * lanes, lanes)] for j in range(3)]
    first = taps[0] * head[0] + taps[1] * last[1] + taps[2] * last[0]
    second = taps[0] * head[1] + taps[1] * head[0] + taps[2] * last[1]
    return first, second


def first_products(taps_ref, last, head):
    keys, values = first_rows(taps_ref, 1, last, head), first_rows(taps_ref, 2, last, head)
    return [(k * v).astype(BF16).astype(F32) for k, v in zip(keys, values)]


def spread(rows, modes):
    return jnp.concatenate([jnp.broadcast_to(rows[l : l + 1], (modes, LANES)) for l in range(rows.shape[0])], axis=0)


def pairs(ref, start, lanes):
    return ref[start : start + lanes], ref[start + lanes : start + 2 * lanes]


def step_over(block, lanes, rates, taps_ref, state, last, run):
    states = rates.shape[0]
    modes = states // lanes
    first, second = first_products(taps_ref, last, pairs(run, states, lanes))
    end = run[:states] + state * jnp.exp(-block * rates)
    end = end + jnp.exp(-(block - 1) * rates) * spread(first, modes) + jnp.exp(-(block - 2) * rates) * spread(second, modes)
    return end, pairs(run, states + 2 * lanes, lanes)


def step_into(block, lanes, place, rates, taps_ref, state, last, edge_ref, before_ref):
    states = rates.shape[0]
    modes = states // lanes
    first, second = first_products(taps_ref, last, pairs(edge_ref, 0, lanes))
    lag = (block * place).astype(F32)
    held = jnp.exp(-rates * jnp.maximum(lag - 1.0, 0.0)) * spread(first, modes)
    held = held + jnp.exp(-rates * jnp.maximum(lag - 2.0, 0.0)) * spread(second, modes)
    state = before_ref[...] + state * jnp.exp(-rates * lag) + jnp.where(place > 0, held, 0.0)
    inside = pairs(edge_ref, 2 * lanes, lanes)
    return state, [jnp.where(place > 0, a, b) for a, b in zip(inside, last)]


def slot(place, size):
    return size - 1 - place


def first_slot(place, size):
    return (3 - place // 4) * 4 + place % 4


def near_scan(block, lanes, got_ref, rate_ref, taps_ref, before_ref, edge_ref, slot=slot):
    size = got_ref.shape[0]
    place = lax.axis_index("ctx") % size
    states = rate_ref.shape[0]
    rates = rate_ref[...]
    run = got_ref[slot(0, size)].astype(F32)
    head = run[states : states + 2 * lanes]
    total, last = run[:states], pairs(run, states + 2 * lanes, lanes)
    before = jnp.where(place == 1, total, jnp.zeros_like(total))
    for j in range(1, size):
        total, last = step_over(block, lanes, rates, taps_ref, total, last, got_ref[slot(j, size)].astype(F32))
        if j < size - 1:
            before = jnp.where(place == j + 1, total, before)
    before_ref[...] = before
    edge_ref[: 2 * lanes] = head
    edge_ref[2 * lanes : 4 * lanes] = got_ref[slot(jnp.maximum(place - 1, 0), size)].astype(F32)[states + 2 * lanes :]
    edge_ref[4 * lanes :] = got_ref[slot(place, size)].astype(F32)[states : states + 2 * lanes]
    return jnp.concatenate([total, head, *last], axis=0)


def write(message, *refs):
    for ref in refs:
        rest = ref.shape[0] - message.shape[0]
        whole = jnp.concatenate([message, jnp.zeros((rest, LANES), F32)], axis=0) if rest else message
        ref[...] = whole.astype(BF16)


def first_scan(block, lanes, got_ref, rate_ref, taps_ref, before_ref, edge_ref, message_ref):
    @pl.when(lax.axis_index("ctx") // WIDE == 0)
    def _():
        write(near_scan(block, lanes, got_ref, rate_ref, taps_ref, before_ref, edge_ref, first_slot), message_ref)


def second_scan(block, lanes, got_ref, rate_ref, taps_ref, before_ref, edge_ref, message_ref):
    @pl.when(lax.axis_index("ctx") // WIDE == 1)
    def _():
        message_ref[...] = near_scan(block, lanes, got_ref, rate_ref, taps_ref, before_ref, edge_ref)


def relay(block, lanes, came_ref, own_ref, rate_ref, taps_ref, kept_ref, *message_refs):
    @pl.when(lax.axis_index("ctx") // WIDE == 1)
    def _():
        rates = rate_ref[...]
        state, last = jnp.zeros_like(rates), [jnp.zeros((lanes, LANES), F32)] * 2
        came = came_ref[...].astype(F32)
        kept_ref[...] = came
        for run in (came, own_ref[...]):
            state, last = step_over(block * WIDE, lanes, rates, taps_ref, state, last, run)
        write(jnp.concatenate([state, *last], axis=0), *message_refs)


def third_scan(block, lanes, got_ref, rate_ref, taps_ref, before_ref, edge_ref, *message_refs):
    @pl.when(lax.axis_index("ctx") // WIDE == 2)
    def _():
        write(near_scan(block, lanes, got_ref, rate_ref, taps_ref, before_ref, edge_ref), *message_refs)


def fourth_scan(block, lanes, got_ref, third_before, third_edge, third_message, rate_ref, taps_ref, before_ref, edge_ref, message_ref):
    group = lax.axis_index("ctx") // WIDE

    @pl.when(group == 2)
    def _():
        before_ref[...] = third_before[...]
        edge_ref[...] = third_edge[...]
        message_ref[...] = third_message[...]

    @pl.when(group == 3)
    def _():
        write(near_scan(block, lanes, got_ref, rate_ref, taps_ref, before_ref, edge_ref), message_ref)


def prepare(block, lanes, across_ref, cross_ref, next_ref, before_ref, edge_ref, rate_ref, taps_ref, residue_ref, rates_ref, weights_ref, rest_ref, decay_ref, head_ref, lead_ref, step_ref, fixed_ref):
    index = lax.axis_index("ctx")
    run, place = index // NEAR, index % NEAR
    states = rate_ref.shape[0]
    modes = states // lanes
    rates = rate_ref[...]
    across, cross, following = [r[: states + 4 * lanes].astype(F32) for r in (across_ref, cross_ref, next_ref)]
    start = jnp.where(run == 5, following, jnp.where(run == 6, across, cross))
    state, last = start[:states], pairs(start, states + 2 * lanes, lanes)
    for needed, message in ((run > 5, jnp.where(run == 6, cross, across)), (run > 6, following)):
        after, after_last = step_over(block * NEAR, lanes, rates, taps_ref, state, last, message)
        state, last = jnp.where(needed, after, state), [jnp.where(needed, a, b) for a, b in zip(after_last, last)]
    into, own_last = step_into(block, lanes, place, rates, taps_ref, state, last, edge_ref, before_ref)
    state = jnp.where(run > 4, into, before_ref[...])
    length = (block * (NEAR * (run - 4) + place)).astype(F32)
    away = length > 0
    own_head = pairs(edge_ref, 4 * lanes, lanes)
    first, second = first_products(taps_ref, own_last, own_head)
    ahead = jnp.exp(rates) * spread(second, modes)
    rest_ref[...] = state * jnp.exp(-rates) + jnp.where(away, spread(first, modes) + ahead, 0.0)
    for i in range(3):
        decay_ref[pl.ds(i * states, states)] = jnp.exp(-rates * (length + (1.0 - i)))
    head_ref[...] = jnp.where(run > 4, start[states : states + 2 * lanes], edge_ref[: 2 * lanes])
    ahead = jnp.where(away, ahead * residue_ref[...], 0.0)
    query = [q.astype(BF16).astype(F32) for q in first_rows(taps_ref, 0, own_last, own_head)]
    fix_rows(lanes, ahead, query, fixed_ref, 0)
    row = lax.broadcasted_iota(jnp.int32, (SUB, weights_ref.shape[1]), 0).astype(F32)
    step_ref[...] = jnp.exp(-SUB * rates_ref[...])
    for mode in range(modes):
        at = pl.ds(mode, 1)
        lead_ref[pl.ds(mode * SUB, SUB)] = weights_ref[at] * jnp.exp(-rates_ref[at] * row)


def fix_rows(lanes, ahead, query, out_ref, start):
    modes = ahead.shape[0] // lanes
    row = lax.broadcasted_iota(jnp.int32, (SUB, LANES), 0)
    for l in range(lanes):
        extra = jnp.sum(ahead[l * modes : (l + 1) * modes], axis=0, keepdims=True)
        take = jnp.where(row == 0, jnp.broadcast_to(extra, row.shape), 0.0)
        fixed = jnp.where(row == 0, query[0][l : l + 1], jnp.where(row == 1, query[1][l : l + 1], 0.0))
        out_ref[start : start + SUB, pl.ds(l * LANES, LANES)] = take
        out_ref[start + SUB : start + 2 * SUB, pl.ds(l * LANES, LANES)] = fixed


def add_mode(totals, term, rate):
    step = jnp.broadcast_to(jnp.exp(-SUB * rate), term.shape)
    out = []
    for total in totals:
        out.append(total + term)
        term = term * step
    return out


def inner_conv(rate_ref, residue_ref, product_ref, local_ref, filter_ref):
    count, chans = product_ref.shape
    modes = rate_ref.shape[0]
    blocks = count // SUB
    row = lax.broadcasted_iota(jnp.int32, (SUB, LANES), 0)
    lead = row.astype(F32)

    def one_lane(lane, carry):
        at = pl.ds(pl.multiple_of(lane * LANES, LANES), LANES)
        zero = jnp.zeros((SUB, LANES), F32)
        totals = [zero] * blocks
        for mode in range(modes):
            rate = rate_ref[pl.ds(mode, 1), at]
            term = residue_ref[pl.ds(mode, 1), at] * jnp.exp(-rate * lead)
            totals = add_mode(totals, term, rate)
        for i in range(blocks):
            filter_ref[pl.ds(i * SUB, SUB), :] = totals[i]

        shifted = [product_ref[pl.ds(i * SUB, SUB), at] for i in range(blocks)]
        totals = [zero] * blocks
        for b in range(SUB):
            for a in range(blocks):
                weight = filter_ref[pl.ds(a * SUB + b, 1), :]
                for j in range(blocks - a):
                    totals[j + a] = totals[j + a] + weight * shifted[j]
            if b < SUB - 1:
                rolled = [pltpu.roll(s, 1, 0) for s in shifted]
                shifted = [jnp.where(row == 0, before, now) for before, now in zip([zero] + rolled[:-1], rolled)]
        for i in range(blocks):
            local_ref[pl.ds(i * SUB, SUB), at] = totals[i]
        return carry

    lax.fori_loop(0, chans // LANES, one_lane, 0)


def finish(place, state, last, edge_ref, before_ref, rate_pack, residue_pack, taps_ref, rate_ref, query_ref, local_ref, mixed_ref, state_ref):
    count, chans = local_ref.shape
    lanes = chans // LANES
    modes = rate_ref.shape[0]
    states = lanes * modes
    blocks = count // SUB
    rates = rate_pack[...]
    state, own_last = step_into(count, lanes, place, rates, taps_ref, state, last, edge_ref, before_ref)
    own_head = pairs(edge_ref, 4 * lanes, lanes)
    own_query = [q.astype(BF16).astype(F32) for q in first_rows(taps_ref, 0, own_last, own_head)]
    first, second = first_products(taps_ref, own_last, own_head)
    ahead = jnp.exp(rates) * spread(second, modes)
    state = state * jnp.exp(-rates) + spread(first, modes) + ahead
    state = state * residue_pack[...]
    ahead = ahead * residue_pack[...]
    fix_rows(lanes, ahead, own_query, state_ref, modes)
    lead = lax.broadcasted_iota(jnp.int32, (SUB, LANES), 0).astype(F32)
    for l in range(lanes):
        state_ref[:modes, pl.ds(l * LANES, LANES)] = state[l * modes : (l + 1) * modes]

    def one_lane(lane, carry):
        at = pl.ds(pl.multiple_of(lane * LANES, LANES), LANES)
        totals = [local_ref[pl.ds(i * SUB, SUB), at] for i in range(blocks)]
        for mode in range(modes):
            rate = rate_ref[pl.ds(mode, 1), at]
            term = state_ref[pl.ds(mode, 1), at] * jnp.exp(-rate * lead)
            totals = add_mode(totals, term, rate)
        gate(totals, at, state_ref, modes, query_ref, mixed_ref)
        return carry

    lax.fori_loop(0, lanes, one_lane, 0)


def gate(totals, at, fixed_ref, start, query_ref, mixed_ref):
    totals[0] = totals[0] - fixed_ref[pl.ds(start, SUB), at]
    rows = lax.broadcasted_iota(jnp.int32, (2 * SUB, LANES), 0)
    for i in range(0, len(totals), 2):
        where = pl.ds(i * SUB, 2 * SUB)
        conv = jnp.concatenate(totals[i : i + 2], axis=0).astype(BF16).astype(F32)
        query = query_ref[where, at].astype(F32)
        if i == 0:
            fixed = fixed_ref[pl.ds(start + SUB, SUB), at]
            query = jnp.where(rows < 2, jnp.concatenate([fixed, fixed], axis=0), query)
        mixed_ref[where, at] = (query * conv).astype(BF16)


def leave(mixed_ref, out_ref, sem):
    copy = pltpu.make_async_copy(mixed_ref, out_ref, sem)
    copy.start()
    copy.wait()


def convolves_early():
    index = lax.axis_index("ctx")
    return index < WIDE + WIDE // 2


def early_inner(rate_ref, residue_ref, product_ref, after_ref, local_ref, filter_ref):
    @pl.when(convolves_early())
    def _():
        inner_conv(rate_ref, residue_ref, product_ref, local_ref, filter_ref)


def lower_output(first_before, first_edge, second_before, second_edge, rate_pack, residue_pack, taps_ref, rate_ref, query_ref, residue_ref, product_ref, held_ref, low_ref, out_ref, filter_ref, local_ref, state_ref, mixed_ref, sem):
    early = convolves_early()

    @pl.when(early)
    def _():
        local_ref[...] = held_ref[...]

    @pl.when(jnp.logical_not(early))
    def _():
        inner_conv(rate_ref, residue_ref, product_ref, local_ref, filter_ref)

    index = lax.axis_index("ctx")
    rates = rate_pack[...]
    second = index >= WIDE
    state, last = jnp.zeros_like(rates), [jnp.zeros((taps_ref.shape[0] // 9, LANES), F32)] * 2
    after, after_last = step_over(local_ref.shape[0] * WIDE, len(last[0]), rates, taps_ref, state, last, low_ref[...])
    state, last = jnp.where(second, after, state), [jnp.where(second, a, b) for a, b in zip(after_last, last)]
    before = jnp.where(second, second_before[...], first_before[...])
    edges = jnp.where(second, second_edge[...], first_edge[...])
    finish(index % WIDE, state, last, edges, before, rate_pack, residue_pack, taps_ref, rate_ref, query_ref, local_ref, mixed_ref, state_ref)
    leave(mixed_ref, out_ref, sem)


def upper_output(rest_ref, decay_ref, head_ref, lead_ref, step_ref, fixed_ref, residue_ref, rate_ref, taps_ref, query_ref, local_ref, third_ref, fourth_ref, held_ref, out_ref, state_ref, mixed_ref, sem):
    index = lax.axis_index("ctx")
    states = rest_ref.shape[0]
    lanes = taps_ref.shape[0] // 9
    modes = states // lanes
    blocks = local_ref.shape[0] // SUB

    @pl.when(index >= 2 * WIDE)
    def _():
        came = third_ref[...].astype(F32) + fourth_ref[: states + 4 * lanes].astype(F32)
        last = pairs(came, states, lanes)
        head = pairs(head_ref, 0, lanes)
        first, second = first_products(taps_ref, last, head)
        ahead = spread(second, modes)
        state = rest_ref[...] + came[:states] * decay_ref[:states]
        state = state + spread(first, modes) * decay_ref[states : 2 * states] + ahead * decay_ref[2 * states :]
        for l in range(lanes):
            state_ref[:modes, pl.ds(l * LANES, LANES)] = state[l * modes : (l + 1) * modes]
        state_ref[modes:] = fixed_ref[...]

        @pl.when(index == 2 * WIDE)
        def _():
            query = [q.astype(BF16).astype(F32) for q in first_rows(taps_ref, 0, last, head)]
            fix_rows(lanes, jnp.exp(rate_ref[...]) * ahead * residue_ref[...], query, state_ref, modes)

        def one_lane(lane, carry):
            at = pl.ds(pl.multiple_of(lane * LANES, LANES), LANES)
            totals = [local_ref[pl.ds(i * SUB, SUB), at] for i in range(blocks)]
            for mode in range(modes):
                step = jnp.broadcast_to(step_ref[pl.ds(mode, 1), at], (SUB, LANES))
                term = state_ref[pl.ds(mode, 1), at] * lead_ref[pl.ds(mode * SUB, SUB), at]
                for i in range(blocks):
                    totals[i] = totals[i] + term
                    if i < blocks - 1:
                        term = term * step
            gate(totals, at, state_ref, modes, query_ref, mixed_ref)
            pltpu.make_async_copy(mixed_ref.at[:, at], out_ref.at[:, at], sem.at[lane]).start()
            return carry

        lax.fori_loop(0, lanes, one_lane, 0, unroll=True)
        for l in range(lanes):
            at = pl.ds(l * LANES, LANES)
            pltpu.make_async_copy(mixed_ref.at[:, at], out_ref.at[:, at], sem.at[l]).wait()


def gather(copies, axis, groups=None):
    return lax.all_to_all(copies, axis, 0, 0, tiled=True, axis_index_groups=groups)


def per_device(stream, norm_gain, short_filter, decay_rate, residue):
    count, chans = stream.shape
    modes = decay_rate.shape[1]
    lanes = chans // LANES
    states = lanes * modes
    peers = lax.axis_size("ch")
    ctx = lax.axis_size("ctx")
    groups = [[g + m for m in range(WIDE)] for g in range(0, ctx, WIDE)]
    runs = [[g + m for m in range(NEAR)] for g in range(0, ctx, NEAR)]
    index, stream = lax.optimization_barrier((lax.axis_index("ctx"), stream))
    held = [stream, norm_gain[None, :], short_filter, decay_rate.T, residue.T]
    held = [pltpu.with_memory_space_constraint(h, pltpu.HBM) for h in held]
    stream, gain, taps, rates, weights, sums, taps_pack, rate_pack, residue_pack = call(
        square_sums,
        [(h.shape, h.dtype) for h in held]
        + [((peers, 1, count), F32), ((9 * lanes, LANES), F32), ((states, LANES), F32), ((states, LANES), F32)],
        *held,
        scratch=[pltpu.SemaphoreType.DMA((lanes + len(held) - 1,))],
        space=pltpu.HBM,
    )
    sums = lax.cond(index < ctx, lambda c: gather(c, "ch", [list(range(peers))[::-1]]), lambda c: c, sums)
    query, product, wide, near = call(
        lambda *refs: block_states(chans * peers, *refs),
        [((count, chans), BF16), ((count, chans), F32), ((WIDE, states + 4 * lanes, LANES), BF16), ((NEAR, states + 4 * lanes, LANES), BF16)],
        sums, stream, gain, taps, rates,
        scratch=[pltpu.VMEM((SUB, chans), F32), pltpu.VMEM((modes, chans), F32), pltpu.VMEM((states + 4 * lanes, LANES), F32)],
    )
    index, wide, near = lax.optimization_barrier((index, wide, near))
    group = lax.shift_right_logical(index, WIDE.bit_length() - 1)
    small, large = ((states + 4 * lanes, LANES), BF16), ((states + 8 * lanes, LANES), BF16)
    kept = [((states, LANES), F32), ((6 * lanes, LANES), F32)]
    nothing = lambda *shapes: tuple(call(lambda *refs: None, shapes, out_any=range(len(shapes))))
    hops = lambda *ends: [pair for a, b in ends for pair in zip(a, b)]
    first, second, third, fourth = groups
    scan = lambda body, outs, *args: call(
        lambda *refs: body(count, lanes, *refs), [*kept, *outs], *args, rate_pack, taps_pack
    )

    def gather_in(number, copies, members):
        size = len(members[0])
        put = slot if number else first_slot
        order = sorted(range(size), key=lambda j: put(j, size))
        members = [[g[j] for j in order] for g in members]
        return lax.cond(
            group == number, lambda c: gather(c, "ctx", members), lambda c: nothing((c.shape, c.dtype))[0], copies
        )

    def inner():
        return call(
            inner_conv, [((count, chans), F32)], rates, weights, product, scratch=[pltpu.VMEM((count, LANES), F32)], flops=10**7
        )[0]

    room = [pltpu.VMEM((count, LANES), F32)]
    work = [pltpu.VMEM((modes + 2 * SUB, chans), F32), pltpu.VMEM((count, chans), BF16), pltpu.SemaphoreType.DMA]
    whole = (small[0], F32)
    held, result = ((count, chans), F32), ((count, chans), BF16)

    def lower(copies):
        *first_kept, message = scan(first_scan, [small], gather_in(0, copies, groups))
        low = lax.ppermute(message, "ctx", hops((first, second)))
        (local,) = call(early_inner, [held], rates, weights, product, message, scratch=room, flops=10**7)
        copies, local = lax.optimization_barrier((copies, local))
        *second_kept, message = scan(second_scan, [whole], gather_in(1, copies, groups))
        onward = call(lambda *refs: relay(count, lanes, *refs), [whole, small, large], low, message, rate_pack, taps_pack)
        return *first_kept, *second_kept, local, *onward

    *lower_kept, to_third, to_fourth = lax.cond(
        group < 2, lower, lambda c: nothing(*kept, *kept, held, whole, small, large), wide
    )
    half = WIDE // 2
    quarter = WIDE // 4
    turned = fourth[half:] + fourth[quarter:half] + fourth[:quarter]
    to_fourth = lax.ppermute(to_fourth, "ctx", hops((second, turned)))
    to_third = lax.ppermute(to_third, "ctx", hops((second, third)))

    prepared = [
        ((states, LANES), F32), ((3 * states, LANES), F32), ((2 * lanes, LANES), F32),
        ((modes * SUB, chans), F32), ((modes, chans), F32), ((2 * SUB, chans), F32),
    ]

    def upper(copies):
        *own, message, first_message = scan(third_scan, [small, large], gather_in(2, copies, runs))
        across = lax.ppermute(first_message, "ctx", hops((runs[4], runs[6]), (runs[5], runs[7])))
        cross = lax.ppermute(first_message, "ctx", hops((runs[4], runs[7]), (runs[5], runs[6])))
        *own, message = scan(fourth_scan, [small], gather_in(3, copies, runs), *own, message)
        following = lax.ppermute(message, "ctx", hops((runs[4], runs[5]), (runs[6], runs[7])))
        ready = call(
            lambda *refs: prepare(count, lanes, *refs),
            prepared,
            across, cross, following, *own, rate_pack, taps_pack, residue_pack, rates, weights,
        )
        return *call(lambda *refs: None, [result], out_hbm=(0,)), inner(), *ready

    def rest(copies):
        common = [rate_pack, residue_pack, taps_pack, rates, query, weights, product]
        (mixed,) = call(
            lower_output, [result], *lower_kept[:4], *common, *lower_kept[4:], scratch=room + [pltpu.VMEM(*held)] + work, out_hbm=(0,)
        )
        return mixed, *nothing(held, *prepared)

    mixed, local, *ready = lax.cond(group >= 2, upper, rest, near)
    (mixed,) = call(
        upper_output,
        [result],
        *ready, residue_pack, rate_pack, taps_pack, query, local, to_third, to_fourth, mixed,
        scratch=work[:2] + [pltpu.SemaphoreType.DMA((lanes,))], in_hbm=(13,), out_hbm=(0,), aliases={13: 0},
    )
    return mixed


def solution(mesh):
    in_specs = (P("ctx", "ch"), P("ch"), P(None, None, "ch"), P("ch", None), P("ch", None))
    out_specs = P("ctx", "ch")
    return jax.shard_map(
        per_device, mesh=mesh, in_specs=in_specs, out_specs=out_specs, check_vma=False
    )
```

```python
import jax
import jax.numpy as jnp
from jax import lax
from jax.experimental import pallas as pl
from jax.experimental.pallas import tpu as pltpu
from jax.sharding import PartitionSpec as P

EXACT = lax.Precision.HIGHEST
EPSILON = 1e-05
SUB = 8
LANES = 128
WIDE = 16
NEAR = 8

F32 = jnp.float32
BF16 = jnp.bfloat16


def call(body, outs, *args, scratch=(), flops=0, space=pltpu.VMEM, in_hbm=(), out_hbm=(), out_any=(), aliases=None):
    shapes = [jax.ShapeDtypeStruct(s, d) for s, d in outs]
    spaces = [pltpu.HBM if i in in_hbm else space for i in range(len(args))]
    out_spaces = [pltpu.HBM if i in out_hbm else pl.ANY if i in out_any else pltpu.VMEM for i in range(len(outs))]
    moved = sum(a.size * a.dtype.itemsize for a in args)
    return pl.pallas_call(
        body,
        out_shape=shapes,
        in_specs=[pl.BlockSpec(memory_space=m) for m in spaces],
        out_specs=[pl.BlockSpec(memory_space=m) for m in out_spaces],
        scratch_shapes=list(scratch),
        input_output_aliases=aliases or {},
        compiler_params=pltpu.CompilerParams(vmem_limit_bytes=16 * 2**20),
        cost_estimate=pl.CostEstimate(flops=flops, bytes_accessed=moved, transcendentals=0),
    )(*args)


def pack(ref):
    return jnp.concatenate([ref[:, l * LANES : (l + 1) * LANES] for l in range(ref.shape[1] // LANES)], axis=0)


def square_sums(*refs):
    count = 5
    held, outs, refs = refs[:count], refs[count : 2 * count], refs[2 * count :]
    sums_ref, taps_pack, rate_pack, residue_pack, sem = refs
    stream_ref, _, taps_ref, rate_ref, residue_ref = outs
    lanes = stream_ref.shape[1] // LANES
    cuts = [pl.ds(l * LANES, LANES) for l in range(lanes)]
    copies = [pltpu.make_async_copy(held[0].at[:, at], stream_ref.at[:, at], sem.at[i]) for i, at in enumerate(cuts)]
    copies += [pltpu.make_async_copy(held[i], outs[i], sem.at[lanes + i - 1]) for i in range(1, count)]
    for copy in copies:
        copy.start()
    total = 0.0
    for copy, at in zip(copies, cuts):
        copy.wait()
        values = stream_ref[:, at].astype(F32)
        total = total + values * values
    sums = jnp.sum(total.T, axis=0, keepdims=True)
    for peer in range(sums_ref.shape[0]):
        sums_ref[peer] = sums
    for copy in copies[lanes:]:
        copy.wait()
    rate_pack[...] = pack(rate_ref)
    residue_pack[...] = pack(residue_ref)
    for tap in range(3):
        for role in range(3):
            for l in range(lanes):
                taps_pack[pl.ds((tap * 3 + role) * lanes + l, 1), :] = taps_ref[tap, pl.ds(role, 1), pl.ds(l * LANES, LANES)]


def block_states(chan_total, sums_ref, stream_ref, gain_ref, taps_ref, rate_ref, query_ref, product_ref, wide_ref, near_ref, edge_ref, end_ref, whole_ref):
    count, chans = stream_ref.shape
    lanes = chans // LANES
    modes = rate_ref.shape[0]
    blocks = count // SUB
    sums = sums_ref[0]
    for peer in range(1, sums_ref.shape[0]):
        sums = sums + sums_ref[peer]
    rest = lax.rsqrt(sums / chan_total + EPSILON)
    rows = lax.broadcasted_iota(jnp.int32, (2 * SUB, count), 0)
    parts = jnp.zeros((2 * SUB, count), F32)
    for i in range(3):
        part = rest.astype(BF16).astype(F32)
        parts = jnp.where(rows == i, part, parts)
        rest = rest - part
    scale = lax.dot_general(
        parts.astype(BF16), jnp.ones((2 * SUB, LANES), BF16), (((0,), (0,)), ((), ())), preferred_element_type=F32
    )
    row = lax.broadcasted_iota(jnp.int32, (SUB, LANES), 0)
    lag = (SUB - 1 - row).astype(F32)

    def one_lane(lane, carry):
        at = pl.ds(pl.multiple_of(lane * LANES, LANES), LANES)
        gain = jnp.broadcast_to(gain_ref[:, at], (SUB, LANES))
        taps = [[jnp.broadcast_to(taps_ref[j, pl.ds(role, 1), at], (SUB, LANES)) for j in range(3)] for role in range(3)]
        before = [jnp.zeros((SUB, LANES), F32)] * 2
        products, queries = [], []
        for i in range(blocks):
            if i % 2 == 0:
                pair = stream_ref[pl.ds(i * SUB, 2 * SUB), at].astype(F32)
            normed = pair[i % 2 * SUB : (i % 2 + 1) * SUB] * scale[i * SUB : (i + 1) * SUB] * gain
            normed = normed.astype(BF16).astype(F32)
            if i == 0:
                edge_ref[:2, at] = normed[:2]
            if i == blocks - 1:
                edge_ref[2:4, at] = normed[SUB - 2 :]
            rolled = [pltpu.roll(normed, j, 0) for j in (1, 2)]
            shifted = [normed] + [jnp.where(row < j, b, r) for j, b, r in zip((1, 2), before, rolled)]
            before = rolled
            query, key, value = [sum(t * n for t, n in zip(taps[role], shifted)) for role in range(3)]
            product = (key * value).astype(BF16).astype(F32)
            if i == 0:
                product = jnp.where(row < 2, 0.0, product)
            product_ref[pl.ds(i * SUB, SUB), at] = product
            products.append(product)
            queries.append(query)
            if i % 2 == 1:
                query_ref[pl.ds((i - 1) * SUB, 2 * SUB), at] = jnp.concatenate(queries[-2:], axis=0).astype(BF16)
        for mode in range(modes):
            rate = rate_ref[pl.ds(mode, 1), at]
            step = jnp.broadcast_to(jnp.exp(-SUB * rate), (SUB, LANES))
            total = products[0]
            for product in products[1:]:
                total = total * step + product
            end_ref[pl.ds(mode, 1), at] = jnp.sum(total * jnp.exp(-rate * lag), axis=0, keepdims=True)
        return carry

    lax.fori_loop(0, lanes, one_lane, 0, unroll=True)
    whole_ref[: lanes * modes] = pack(end_ref)
    for e in range(4):
        for l in range(lanes):
            whole_ref[pl.ds(lanes * (modes + e) + l, 1), :] = edge_ref[pl.ds(e, 1), pl.ds(l * LANES, LANES)]
    message = whole_ref[...].astype(BF16)
    for ref in (wide_ref, near_ref):
        for peer in range(ref.shape[0]):
            ref[peer] = message


def first_rows(taps_ref, role, last, head):
    lanes = taps_ref.shape[0] // 9
    taps = [taps_ref[pl.ds((3 * j + role) * lanes, lanes)] for j in range(3)]
    first = taps[0] * head[0] + taps[1] * last[1] + taps[2] * last[0]
    second = taps[0] * head[1] + taps[1] * head[0] + taps[2] * last[1]
    return first, second


def first_products(taps_ref, last, head):
    keys, values = first_rows(taps_ref, 1, last, head), first_rows(taps_ref, 2, last, head)
    return [(k * v).astype(BF16).astype(F32) for k, v in zip(keys, values)]


def spread(rows, modes):
    return jnp.concatenate([jnp.broadcast_to(rows[l : l + 1], (modes, LANES)) for l in range(rows.shape[0])], axis=0)


def pairs(ref, start, lanes):
    return ref[start : start + lanes], ref[start + lanes : start + 2 * lanes]


def step_over(block, lanes, rates, taps_ref, state, last, run):
    states = rates.shape[0]
    modes = states // lanes
    first, second = first_products(taps_ref, last, pairs(run, states, lanes))
    end = run[:states] + state * jnp.exp(-block * rates)
    end = end + jnp.exp(-(block - 1) * rates) * spread(first, modes) + jnp.exp(-(block - 2) * rates) * spread(second, modes)
    return end, pairs(run, states + 2 * lanes, lanes)


def step_into(block, lanes, place, rates, taps_ref, state, last, edge_ref, before_ref):
    states = rates.shape[0]
    modes = states // lanes
    first, second = first_products(taps_ref, last, pairs(edge_ref, 0, lanes))
    lag = (block * place).astype(F32)
    held = jnp.exp(-rates * jnp.maximum(lag - 1.0, 0.0)) * spread(first, modes)
    held = held + jnp.exp(-rates * jnp.maximum(lag - 2.0, 0.0)) * spread(second, modes)
    state = before_ref[...] + state * jnp.exp(-rates * lag) + jnp.where(place > 0, held, 0.0)
    inside = pairs(edge_ref, 2 * lanes, lanes)
    return state, [jnp.where(place > 0, a, b) for a, b in zip(inside, last)]


def slot(place, size):
    return size - 1 - place


def first_slot(place, size):
    return place % 4 * 4 + 3 - place // 4


def near_scan(block, lanes, got_ref, rate_ref, taps_ref, before_ref, edge_ref, slot=slot):
    size = got_ref.shape[0]
    place = lax.axis_index("ctx") % size
    states = rate_ref.shape[0]
    rates = rate_ref[...]
    run = got_ref[slot(0, size)].astype(F32)
    head = run[states : states + 2 * lanes]
    total, last = run[:states], pairs(run, states + 2 * lanes, lanes)
    before = jnp.where(place == 1, total, jnp.zeros_like(total))
    for j in range(1, size):
        total, last = step_over(block, lanes, rates, taps_ref, total, last, got_ref[slot(j, size)].astype(F32))
        if j < size - 1:
            before = jnp.where(place == j + 1, total, before)
    before_ref[...] = before
    edge_ref[: 2 * lanes] = head
    edge_ref[2 * lanes : 4 * lanes] = got_ref[slot(jnp.maximum(place - 1, 0), size)].astype(F32)[states + 2 * lanes :]
    edge_ref[4 * lanes :] = got_ref[slot(place, size)].astype(F32)[states : states + 2 * lanes]
    return jnp.concatenate([total, head, *last], axis=0)


def write(message, *refs):
    for ref in refs:
        rest = ref.shape[0] - message.shape[0]
        whole = jnp.concatenate([message, jnp.zeros((rest, LANES), F32)], axis=0) if rest else message
        ref[...] = whole.astype(BF16)


def first_scan(block, lanes, got_ref, rate_ref, taps_ref, before_ref, edge_ref, message_ref):
    @pl.when(lax.axis_index("ctx") // WIDE == 0)
    def _():
        write(near_scan(block, lanes, got_ref, rate_ref, taps_ref, before_ref, edge_ref, first_slot), message_ref)


def second_scan(block, lanes, got_ref, rate_ref, taps_ref, before_ref, edge_ref, message_ref):
    @pl.when(lax.axis_index("ctx") // WIDE == 1)
    def _():
        message_ref[...] = near_scan(block, lanes, got_ref, rate_ref, taps_ref, before_ref, edge_ref)


def relay(block, lanes, came_ref, own_ref, rate_ref, taps_ref, kept_ref, *message_refs):
    @pl.when(lax.axis_index("ctx") // WIDE == 1)
    def _():
        rates = rate_ref[...]
        state, last = jnp.zeros_like(rates), [jnp.zeros((lanes, LANES), F32)] * 2
        came = came_ref[...].astype(F32)
        kept_ref[...] = came
        for run in (came, own_ref[...]):
            state, last = step_over(block * WIDE, lanes, rates, taps_ref, state, last, run)
        write(jnp.concatenate([state, *last], axis=0), *message_refs)


def third_scan(block, lanes, got_ref, rate_ref, taps_ref, before_ref, edge_ref, *message_refs):
    @pl.when(lax.axis_index("ctx") // WIDE == 2)
    def _():
        write(near_scan(block, lanes, got_ref, rate_ref, taps_ref, before_ref, edge_ref), *message_refs)


def fourth_scan(block, lanes, got_ref, third_before, third_edge, third_message, rate_ref, taps_ref, before_ref, edge_ref, message_ref):
    group = lax.axis_index("ctx") // WIDE

    @pl.when(group == 2)
    def _():
        before_ref[...] = third_before[...]
        edge_ref[...] = third_edge[...]
        message_ref[...] = third_message[...]

    @pl.when(group == 3)
    def _():
        write(near_scan(block, lanes, got_ref, rate_ref, taps_ref, before_ref, edge_ref), message_ref)


def prepare(block, lanes, across_ref, cross_ref, next_ref, before_ref, edge_ref, rate_ref, taps_ref, residue_ref, rates_ref, weights_ref, rest_ref, decay_ref, head_ref, lead_ref, step_ref, fixed_ref):
    index = lax.axis_index("ctx")
    run, place = index // NEAR, index % NEAR
    states = rate_ref.shape[0]
    modes = states // lanes
    rates = rate_ref[...]
    across, cross, following = [r[: states + 4 * lanes].astype(F32) for r in (across_ref, cross_ref, next_ref)]
    start = jnp.where(run == 5, following, jnp.where(run == 6, across, cross))
    state, last = start[:states], pairs(start, states + 2 * lanes, lanes)
    for needed, message in ((run > 5, jnp.where(run == 6, cross, across)), (run > 6, following)):
        after, after_last = step_over(block * NEAR, lanes, rates, taps_ref, state, last, message)
        state, last = jnp.where(needed, after, state), [jnp.where(needed, a, b) for a, b in zip(after_last, last)]
    into, own_last = step_into(block, lanes, place, rates, taps_ref, state, last, edge_ref, before_ref)
    state = jnp.where(run > 4, into, before_ref[...])
    length = (block * (NEAR * (run - 4) + place)).astype(F32)
    away = length > 0
    own_head = pairs(edge_ref, 4 * lanes, lanes)
    first, second = first_products(taps_ref, own_last, own_head)
    ahead = jnp.exp(rates) * spread(second, modes)
    rest_ref[...] = state * jnp.exp(-rates) + jnp.where(away, spread(first, modes) + ahead, 0.0)
    for i in range(3):
        decay_ref[pl.ds(i * states, states)] = jnp.exp(-rates * (length + (1.0 - i)))
    head_ref[...] = jnp.where(run > 4, start[states : states + 2 * lanes], edge_ref[: 2 * lanes])
    ahead = jnp.where(away, ahead * residue_ref[...], 0.0)
    query = [q.astype(BF16).astype(F32) for q in first_rows(taps_ref, 0, own_last, own_head)]
    fix_rows(lanes, ahead, query, fixed_ref, 0)
    row = lax.broadcasted_iota(jnp.int32, (SUB, weights_ref.shape[1]), 0).astype(F32)
    step_ref[...] = jnp.exp(-SUB * rates_ref[...])
    for mode in range(modes):
        at = pl.ds(mode, 1)
        lead_ref[pl.ds(mode * SUB, SUB)] = weights_ref[at] * jnp.exp(-rates_ref[at] * row)


def fix_rows(lanes, ahead, query, out_ref, start):
    modes = ahead.shape[0] // lanes
    row = lax.broadcasted_iota(jnp.int32, (SUB, LANES), 0)
    for l in range(lanes):
        extra = jnp.sum(ahead[l * modes : (l + 1) * modes], axis=0, keepdims=True)
        take = jnp.where(row == 0, jnp.broadcast_to(extra, row.shape), 0.0)
        fixed = jnp.where(row == 0, query[0][l : l + 1], jnp.where(row == 1, query[1][l : l + 1], 0.0))
        out_ref[start : start + SUB, pl.ds(l * LANES, LANES)] = take
        out_ref[start + SUB : start + 2 * SUB, pl.ds(l * LANES, LANES)] = fixed


def add_mode(totals, term, rate):
    step = jnp.broadcast_to(jnp.exp(-SUB * rate), term.shape)
    out = []
    for total in totals:
        out.append(total + term)
        term = term * step
    return out


def inner_conv(rate_ref, residue_ref, product_ref, local_ref, filter_ref):
    count, chans = product_ref.shape
    modes = rate_ref.shape[0]
    blocks = count // SUB
    row = lax.broadcasted_iota(jnp.int32, (SUB, LANES), 0)
    lead = row.astype(F32)

    def one_lane(lane, carry):
        at = pl.ds(pl.multiple_of(lane * LANES, LANES), LANES)
        zero = jnp.zeros((SUB, LANES), F32)
        totals = [zero] * blocks
        for mode in range(modes):
            rate = rate_ref[pl.ds(mode, 1), at]
            term = residue_ref[pl.ds(mode, 1), at] * jnp.exp(-rate * lead)
            totals = add_mode(totals, term, rate)
        for i in range(blocks):
            filter_ref[pl.ds(i * SUB, SUB), :] = totals[i]

        shifted = [product_ref[pl.ds(i * SUB, SUB), at] for i in range(blocks)]
        totals = [zero] * blocks
        for b in range(SUB):
            for a in range(blocks):
                weight = filter_ref[pl.ds(a * SUB + b, 1), :]
                for j in range(blocks - a):
                    totals[j + a] = totals[j + a] + weight * shifted[j]
            if b < SUB - 1:
                rolled = [pltpu.roll(s, 1, 0) for s in shifted]
                shifted = [jnp.where(row == 0, before, now) for before, now in zip([zero] + rolled[:-1], rolled)]
        for i in range(blocks):
            local_ref[pl.ds(i * SUB, SUB), at] = totals[i]
        return carry

    lax.fori_loop(0, chans // LANES, one_lane, 0)


def finish(place, state, last, edge_ref, before_ref, rate_pack, residue_pack, taps_ref, rate_ref, query_ref, local_ref, mixed_ref, state_ref):
    count, chans = local_ref.shape
    lanes = chans // LANES
    modes = rate_ref.shape[0]
    states = lanes * modes
    blocks = count // SUB
    rates = rate_pack[...]
    state, own_last = step_into(count, lanes, place, rates, taps_ref, state, last, edge_ref, before_ref)
    own_head = pairs(edge_ref, 4 * lanes, lanes)
    own_query = [q.astype(BF16).astype(F32) for q in first_rows(taps_ref, 0, own_last, own_head)]
    first, second = first_products(taps_ref, own_last, own_head)
    ahead = jnp.exp(rates) * spread(second, modes)
    state = state * jnp.exp(-rates) + spread(first, modes) + ahead
    state = state * residue_pack[...]
    ahead = ahead * residue_pack[...]
    fix_rows(lanes, ahead, own_query, state_ref, modes)
    lead = lax.broadcasted_iota(jnp.int32, (SUB, LANES), 0).astype(F32)
    for l in range(lanes):
        state_ref[:modes, pl.ds(l * LANES, LANES)] = state[l * modes : (l + 1) * modes]

    def one_lane(lane, carry):
        at = pl.ds(pl.multiple_of(lane * LANES, LANES), LANES)
        totals = [local_ref[pl.ds(i * SUB, SUB), at] for i in range(blocks)]
        for mode in range(modes):
            rate = rate_ref[pl.ds(mode, 1), at]
            term = state_ref[pl.ds(mode, 1), at] * jnp.exp(-rate * lead)
            totals = add_mode(totals, term, rate)
        gate(totals, at, state_ref, modes, query_ref, mixed_ref)
        return carry

    lax.fori_loop(0, lanes, one_lane, 0)


def gate(totals, at, fixed_ref, start, query_ref, mixed_ref):
    totals[0] = totals[0] - fixed_ref[pl.ds(start, SUB), at]
    rows = lax.broadcasted_iota(jnp.int32, (2 * SUB, LANES), 0)
    for i in range(0, len(totals), 2):
        where = pl.ds(i * SUB, 2 * SUB)
        conv = jnp.concatenate(totals[i : i + 2], axis=0).astype(BF16).astype(F32)
        query = query_ref[where, at].astype(F32)
        if i == 0:
            fixed = fixed_ref[pl.ds(start + SUB, SUB), at]
            query = jnp.where(rows < 2, jnp.concatenate([fixed, fixed], axis=0), query)
        mixed_ref[where, at] = (query * conv).astype(BF16)


def leave(mixed_ref, out_ref, sem):
    copy = pltpu.make_async_copy(mixed_ref, out_ref, sem)
    copy.start()
    copy.wait()


def convolves_early():
    index = lax.axis_index("ctx")
    return index < WIDE + WIDE // 2


def early_inner(rate_ref, residue_ref, product_ref, after_ref, local_ref, filter_ref):
    @pl.when(convolves_early())
    def _():
        inner_conv(rate_ref, residue_ref, product_ref, local_ref, filter_ref)


def lower_output(first_before, first_edge, second_before, second_edge, rate_pack, residue_pack, taps_ref, rate_ref, query_ref, residue_ref, product_ref, held_ref, low_ref, out_ref, filter_ref, local_ref, state_ref, mixed_ref, sem):
    early = convolves_early()

    @pl.when(early)
    def _():
        local_ref[...] = held_ref[...]

    @pl.when(jnp.logical_not(early))
    def _():
        inner_conv(rate_ref, residue_ref, product_ref, local_ref, filter_ref)

    index = lax.axis_index("ctx")
    rates = rate_pack[...]
    second = index >= WIDE
    state, last = jnp.zeros_like(rates), [jnp.zeros((taps_ref.shape[0] // 9, LANES), F32)] * 2
    after, after_last = step_over(local_ref.shape[0] * WIDE, len(last[0]), rates, taps_ref, state, last, low_ref[...])
    state, last = jnp.where(second, after, state), [jnp.where(second, a, b) for a, b in zip(after_last, last)]
    before = jnp.where(second, second_before[...], first_before[...])
    edges = jnp.where(second, second_edge[...], first_edge[...])
    finish(index % WIDE, state, last, edges, before, rate_pack, residue_pack, taps_ref, rate_ref, query_ref, local_ref, mixed_ref, state_ref)
    leave(mixed_ref, out_ref, sem)


def upper_output(rest_ref, decay_ref, head_ref, lead_ref, step_ref, fixed_ref, residue_ref, rate_ref, taps_ref, query_ref, local_ref, third_ref, fourth_ref, held_ref, out_ref, state_ref, mixed_ref, sem):
    index = lax.axis_index("ctx")
    states = rest_ref.shape[0]
    lanes = taps_ref.shape[0] // 9
    modes = states // lanes
    blocks = local_ref.shape[0] // SUB

    @pl.when(index >= 2 * WIDE)
    def _():
        came = third_ref[...].astype(F32) + fourth_ref[: states + 4 * lanes].astype(F32)
        last = pairs(came, states, lanes)
        head = pairs(head_ref, 0, lanes)
        first, second = first_products(taps_ref, last, head)
        ahead = spread(second, modes)
        state = rest_ref[...] + came[:states] * decay_ref[:states]
        state = state + spread(first, modes) * decay_ref[states : 2 * states] + ahead * decay_ref[2 * states :]
        for l in range(lanes):
            state_ref[:modes, pl.ds(l * LANES, LANES)] = state[l * modes : (l + 1) * modes]
        state_ref[modes:] = fixed_ref[...]

        @pl.when(index == 2 * WIDE)
        def _():
            query = [q.astype(BF16).astype(F32) for q in first_rows(taps_ref, 0, last, head)]
            fix_rows(lanes, jnp.exp(rate_ref[...]) * ahead * residue_ref[...], query, state_ref, modes)

        def one_lane(lane, carry):
            at = pl.ds(pl.multiple_of(lane * LANES, LANES), LANES)
            totals = [local_ref[pl.ds(i * SUB, SUB), at] for i in range(blocks)]
            for mode in range(modes):
                step = jnp.broadcast_to(step_ref[pl.ds(mode, 1), at], (SUB, LANES))
                term = state_ref[pl.ds(mode, 1), at] * lead_ref[pl.ds(mode * SUB, SUB), at]
                for i in range(blocks):
                    totals[i] = totals[i] + term
                    if i < blocks - 1:
                        term = term * step
            gate(totals, at, state_ref, modes, query_ref, mixed_ref)
            pltpu.make_async_copy(mixed_ref.at[:, at], out_ref.at[:, at], sem.at[lane]).start()
            return carry

        lax.fori_loop(0, lanes, one_lane, 0, unroll=True)
        for l in range(lanes):
            at = pl.ds(l * LANES, LANES)
            pltpu.make_async_copy(mixed_ref.at[:, at], out_ref.at[:, at], sem.at[l]).wait()


def gather(copies, axis, groups=None):
    return lax.all_to_all(copies, axis, 0, 0, tiled=True, axis_index_groups=groups)


def per_device(stream, norm_gain, short_filter, decay_rate, residue):
    count, chans = stream.shape
    modes = decay_rate.shape[1]
    lanes = chans // LANES
    states = lanes * modes
    peers = lax.axis_size("ch")
    ctx = lax.axis_size("ctx")
    groups = [[g + m for m in range(WIDE)] for g in range(0, ctx, WIDE)]
    runs = [[g + m for m in range(NEAR)] for g in range(0, ctx, NEAR)]
    index, stream = lax.optimization_barrier((lax.axis_index("ctx"), stream))
    held = [stream, norm_gain[None, :], short_filter, decay_rate.T, residue.T]
    held = [pltpu.with_memory_space_constraint(h, pltpu.HBM) for h in held]
    stream, gain, taps, rates, weights, sums, taps_pack, rate_pack, residue_pack = call(
        square_sums,
        [(h.shape, h.dtype) for h in held]
        + [((peers, 1, count), F32), ((9 * lanes, LANES), F32), ((states, LANES), F32), ((states, LANES), F32)],
        *held,
        scratch=[pltpu.SemaphoreType.DMA((lanes + len(held) - 1,))],
        space=pltpu.HBM,
    )
    sums = lax.cond(index < ctx, lambda c: gather(c, "ch", [list(range(peers))[::-1]]), lambda c: c, sums)
    query, product, wide, near = call(
        lambda *refs: block_states(chans * peers, *refs),
        [((count, chans), BF16), ((count, chans), F32), ((WIDE, states + 4 * lanes, LANES), BF16), ((NEAR, states + 4 * lanes, LANES), BF16)],
        sums, stream, gain, taps, rates,
        scratch=[pltpu.VMEM((SUB, chans), F32), pltpu.VMEM((modes, chans), F32), pltpu.VMEM((states + 4 * lanes, LANES), F32)],
    )
    index, wide, near = lax.optimization_barrier((index, wide, near))
    group = lax.shift_right_logical(index, WIDE.bit_length() - 1)
    small, large = ((states + 4 * lanes, LANES), BF16), ((states + 8 * lanes, LANES), BF16)
    kept = [((states, LANES), F32), ((6 * lanes, LANES), F32)]
    nothing = lambda *shapes: tuple(call(lambda *refs: None, shapes, out_any=range(len(shapes))))
    hops = lambda *ends: [pair for a, b in ends for pair in zip(a, b)]
    first, second, third, fourth = groups
    scan = lambda body, outs, *args: call(
        lambda *refs: body(count, lanes, *refs), [*kept, *outs], *args, rate_pack, taps_pack
    )

    def gather_in(number, copies, members):
        size = len(members[0])
        put = slot if number else first_slot
        order = sorted(range(size), key=lambda j: put(j, size))
        members = [[g[j] for j in order] for g in members]
        return lax.cond(
            group == number, lambda c: gather(c, "ctx", members), lambda c: nothing((c.shape, c.dtype))[0], copies
        )

    def inner():
        return call(
            inner_conv, [((count, chans), F32)], rates, weights, product, scratch=[pltpu.VMEM((count, LANES), F32)], flops=10**7
        )[0]

    room = [pltpu.VMEM((count, LANES), F32)]
    work = [pltpu.VMEM((modes + 2 * SUB, chans), F32), pltpu.VMEM((count, chans), BF16), pltpu.SemaphoreType.DMA]
    whole = (small[0], F32)
    held, result = ((count, chans), F32), ((count, chans), BF16)

    def lower(copies):
        *first_kept, message = scan(first_scan, [small], gather_in(0, copies, groups))
        low = lax.ppermute(message, "ctx", hops((first, second)))
        (local,) = call(early_inner, [held], rates, weights, product, message, scratch=room, flops=10**7)
        copies, local = lax.optimization_barrier((copies, local))
        *second_kept, message = scan(second_scan, [whole], gather_in(1, copies, groups))
        onward = call(lambda *refs: relay(count, lanes, *refs), [whole, small, large], low, message, rate_pack, taps_pack)
        return *first_kept, *second_kept, local, *onward

    *lower_kept, to_third, to_fourth = lax.cond(
        group < 2, lower, lambda c: nothing(*kept, *kept, held, whole, small, large), wide
    )
    half = WIDE // 2
    quarter = WIDE // 4
    turned = fourth[half:] + fourth[quarter:half] + fourth[:quarter]
    to_fourth = lax.ppermute(to_fourth, "ctx", hops((second, turned)))
    to_third = lax.ppermute(to_third, "ctx", hops((second, third)))

    prepared = [
        ((states, LANES), F32), ((3 * states, LANES), F32), ((2 * lanes, LANES), F32),
        ((modes * SUB, chans), F32), ((modes, chans), F32), ((2 * SUB, chans), F32),
    ]

    def upper(copies):
        *own, message, first_message = scan(third_scan, [small, large], gather_in(2, copies, runs))
        across = lax.ppermute(first_message, "ctx", hops((runs[4], runs[6]), (runs[5], runs[7])))
        cross = lax.ppermute(first_message, "ctx", hops((runs[4], runs[7]), (runs[5], runs[6])))
        *own, message = scan(fourth_scan, [small], gather_in(3, copies, runs), *own, message)
        following = lax.ppermute(message, "ctx", hops((runs[4], runs[5]), (runs[6], runs[7])))
        ready = call(
            lambda *refs: prepare(count, lanes, *refs),
            prepared,
            across, cross, following, *own, rate_pack, taps_pack, residue_pack, rates, weights,
        )
        return *call(lambda *refs: None, [result], out_hbm=(0,)), inner(), *ready

    def rest(copies):
        common = [rate_pack, residue_pack, taps_pack, rates, query, weights, product]
        (mixed,) = call(
            lower_output, [result], *lower_kept[:4], *common, *lower_kept[4:], scratch=room + [pltpu.VMEM(*held)] + work, out_hbm=(0,)
        )
        return mixed, *nothing(held, *prepared)

    mixed, local, *ready = lax.cond(group >= 2, upper, rest, near)
    (mixed,) = call(
        upper_output,
        [result],
        *ready, residue_pack, rate_pack, taps_pack, query, local, to_third, to_fourth, mixed,
        scratch=work[:2] + [pltpu.SemaphoreType.DMA((lanes,))], in_hbm=(13,), out_hbm=(0,), aliases={13: 0},
    )
    return mixed


def solution(mesh):
    in_specs = (P("ctx", "ch"), P("ch"), P(None, None, "ch"), P("ch", None), P("ch", None))
    out_specs = P("ctx", "ch")
    return jax.shard_map(
        per_device, mesh=mesh, in_specs=in_specs, out_specs=out_specs, check_vma=False
    )
```

```python
import jax
import jax.numpy as jnp
from jax import lax
from jax.experimental import pallas as pl
from jax.experimental.pallas import tpu as pltpu
from jax.sharding import PartitionSpec as P

EXACT = lax.Precision.HIGHEST
EPSILON = 1e-05
SUB = 8
LANES = 128
WIDE = 16
NEAR = 8

F32 = jnp.float32
BF16 = jnp.bfloat16


def call(body, outs, *args, scratch=(), flops=0, space=pltpu.VMEM, in_hbm=(), out_hbm=(), out_any=(), aliases=None):
    shapes = [jax.ShapeDtypeStruct(s, d) for s, d in outs]
    spaces = [pltpu.HBM if i in in_hbm else space for i in range(len(args))]
    out_spaces = [pltpu.HBM if i in out_hbm else pl.ANY if i in out_any else pltpu.VMEM for i in range(len(outs))]
    moved = sum(a.size * a.dtype.itemsize for a in args)
    return pl.pallas_call(
        body,
        out_shape=shapes,
        in_specs=[pl.BlockSpec(memory_space=m) for m in spaces],
        out_specs=[pl.BlockSpec(memory_space=m) for m in out_spaces],
        scratch_shapes=list(scratch),
        input_output_aliases=aliases or {},
        compiler_params=pltpu.CompilerParams(vmem_limit_bytes=16 * 2**20),
        cost_estimate=pl.CostEstimate(flops=flops, bytes_accessed=moved, transcendentals=0),
    )(*args)


def pack(ref):
    return jnp.concatenate([ref[:, l * LANES : (l + 1) * LANES] for l in range(ref.shape[1] // LANES)], axis=0)


def square_sums(*refs):
    count = 5
    held, outs, refs = refs[:count], refs[count : 2 * count], refs[2 * count :]
    sums_ref, taps_pack, rate_pack, residue_pack, sem = refs
    stream_ref, _, taps_ref, rate_ref, residue_ref = outs
    lanes = stream_ref.shape[1] // LANES
    cuts = [pl.ds(l * LANES, LANES) for l in range(lanes)]
    copies = [pltpu.make_async_copy(held[0].at[:, at], stream_ref.at[:, at], sem.at[i]) for i, at in enumerate(cuts)]
    copies += [pltpu.make_async_copy(held[i], outs[i], sem.at[lanes + i - 1]) for i in range(1, count)]
    for copy in copies:
        copy.start()
    total = 0.0
    for copy, at in zip(copies, cuts):
        copy.wait()
        values = stream_ref[:, at].astype(F32)
        total = total + values * values
    sums = jnp.sum(total.T, axis=0, keepdims=True)
    for peer in range(sums_ref.shape[0]):
        sums_ref[peer] = sums
    for copy in copies[lanes:]:
        copy.wait()
    rate_pack[...] = pack(rate_ref)
    residue_pack[...] = pack(residue_ref)
    for tap in range(3):
        for role in range(3):
            for l in range(lanes):
                taps_pack[pl.ds((tap * 3 + role) * lanes + l, 1), :] = taps_ref[tap, pl.ds(role, 1), pl.ds(l * LANES, LANES)]


def block_states(chan_total, sums_ref, stream_ref, gain_ref, taps_ref, rate_ref, query_ref, product_ref, wide_ref, near_ref, edge_ref, end_ref, whole_ref):
    count, chans = stream_ref.shape
    lanes = chans // LANES
    modes = rate_ref.shape[0]
    blocks = count // SUB
    sums = sums_ref[0]
    for peer in range(1, sums_ref.shape[0]):
        sums = sums + sums_ref[peer]
    rest = lax.rsqrt(sums / chan_total + EPSILON)
    rows = lax.broadcasted_iota(jnp.int32, (2 * SUB, count), 0)
    parts = jnp.zeros((2 * SUB, count), F32)
    for i in range(3):
        part = rest.astype(BF16).astype(F32)
        parts = jnp.where(rows == i, part, parts)
        rest = rest - part
    scale = lax.dot_general(
        parts.astype(BF16), jnp.ones((2 * SUB, LANES), BF16), (((0,), (0,)), ((), ())), preferred_element_type=F32
    )
    row = lax.broadcasted_iota(jnp.int32, (SUB, LANES), 0)
    lag = (SUB - 1 - row).astype(F32)

    def one_lane(lane, carry):
        at = pl.ds(pl.multiple_of(lane * LANES, LANES), LANES)
        gain = jnp.broadcast_to(gain_ref[:, at], (SUB, LANES))
        taps = [[jnp.broadcast_to(taps_ref[j, pl.ds(role, 1), at], (SUB, LANES)) for j in range(3)] for role in range(3)]
        before = [jnp.zeros((SUB, LANES), F32)] * 2
        products, queries = [], []
        for i in range(blocks):
            if i % 2 == 0:
                pair = stream_ref[pl.ds(i * SUB, 2 * SUB), at].astype(F32)
            normed = pair[i % 2 * SUB : (i % 2 + 1) * SUB] * scale[i * SUB : (i + 1) * SUB] * gain
            normed = normed.astype(BF16).astype(F32)
            if i == 0:
                edge_ref[:2, at] = normed[:2]
            if i == blocks - 1:
                edge_ref[2:4, at] = normed[SUB - 2 :]
            rolled = [pltpu.roll(normed, j, 0) for j in (1, 2)]
            shifted = [normed] + [jnp.where(row < j, b, r) for j, b, r in zip((1, 2), before, rolled)]
            before = rolled
            query, key, value = [sum(t * n for t, n in zip(taps[role], shifted)) for role in range(3)]
            product = (key * value).astype(BF16).astype(F32)
            if i == 0:
                product = jnp.where(row < 2, 0.0, product)
            product_ref[pl.ds(i * SUB, SUB), at] = product
            products.append(product)
            queries.append(query)
            if i % 2 == 1:
                query_ref[pl.ds((i - 1) * SUB, 2 * SUB), at] = jnp.concatenate(queries[-2:], axis=0).astype(BF16)
        for mode in range(modes):
            rate = rate_ref[pl.ds(mode, 1), at]
            step = jnp.broadcast_to(jnp.exp(-SUB * rate), (SUB, LANES))
            total = products[0]
            for product in products[1:]:
                total = total * step + product
            end_ref[pl.ds(mode, 1), at] = jnp.sum(total * jnp.exp(-rate * lag), axis=0, keepdims=True)
        return carry

    lax.fori_loop(0, lanes, one_lane, 0, unroll=True)
    whole_ref[: lanes * modes] = pack(end_ref)
    for e in range(4):
        for l in range(lanes):
            whole_ref[pl.ds(lanes * (modes + e) + l, 1), :] = edge_ref[pl.ds(e, 1), pl.ds(l * LANES, LANES)]
    message = whole_ref[...].astype(BF16)
    for ref in (wide_ref, near_ref):
        for peer in range(ref.shape[0]):
            ref[peer] = message


def first_rows(taps_ref, role, last, head):
    lanes = taps_ref.shape[0] // 9
    taps = [taps_ref[pl.ds((3 * j + role) * lanes, lanes)] for j in range(3)]
    first = taps[0] * head[0] + taps[1] * last[1] + taps[2] * last[0]
    second = taps[0] * head[1] + taps[1] * head[0] + taps[2] * last[1]
    return first, second


def first_products(taps_ref, last, head):
    keys, values = first_rows(taps_ref, 1, last, head), first_rows(taps_ref, 2, last, head)
    return [(k * v).astype(BF16).astype(F32) for k, v in zip(keys, values)]


def spread(rows, modes):
    return jnp.concatenate([jnp.broadcast_to(rows[l : l + 1], (modes, LANES)) for l in range(rows.shape[0])], axis=0)


def pairs(ref, start, lanes):
    return ref[start : start + lanes], ref[start + lanes : start + 2 * lanes]


def step_over(block, lanes, rates, taps_ref, state, last, run):
    states = rates.shape[0]
    modes = states // lanes
    first, second = first_products(taps_ref, last, pairs(run, states, lanes))
    end = run[:states] + state * jnp.exp(-block * rates)
    end = end + jnp.exp(-(block - 1) * rates) * spread(first, modes) + jnp.exp(-(block - 2) * rates) * spread(second, modes)
    return end, pairs(run, states + 2 * lanes, lanes)


def step_into(block, lanes, place, rates, taps_ref, state, last, edge_ref, before_ref):
    states = rates.shape[0]
    modes = states // lanes
    first, second = first_products(taps_ref, last, pairs(edge_ref, 0, lanes))
    lag = (block * place).astype(F32)
    held = jnp.exp(-rates * jnp.maximum(lag - 1.0, 0.0)) * spread(first, modes)
    held = held + jnp.exp(-rates * jnp.maximum(lag - 2.0, 0.0)) * spread(second, modes)
    state = before_ref[...] + state * jnp.exp(-rates * lag) + jnp.where(place > 0, held, 0.0)
    inside = pairs(edge_ref, 2 * lanes, lanes)
    return state, [jnp.where(place > 0, a, b) for a, b in zip(inside, last)]


def slot(place, size):
    return place // 4 * 4 + 3 - place % 4 if size == WIDE else size - 1 - place


def first_slot(place, size):
    return (3 - place // 4) * 4 + place % 4


def near_scan(block, lanes, got_ref, rate_ref, taps_ref, before_ref, edge_ref, slot=slot):
    size = got_ref.shape[0]
    place = lax.axis_index("ctx") % size
    states = rate_ref.shape[0]
    rates = rate_ref[...]
    run = got_ref[slot(0, size)].astype(F32)
    head = run[states : states + 2 * lanes]
    total, last = run[:states], pairs(run, states + 2 * lanes, lanes)
    before = jnp.where(place == 1, total, jnp.zeros_like(total))
    for j in range(1, size):
        total, last = step_over(block, lanes, rates, taps_ref, total, last, got_ref[slot(j, size)].astype(F32))
        if j < size - 1:
            before = jnp.where(place == j + 1, total, before)
    before_ref[...] = before
    edge_ref[: 2 * lanes] = head
    edge_ref[2 * lanes : 4 * lanes] = got_ref[slot(jnp.maximum(place - 1, 0), size)].astype(F32)[states + 2 * lanes :]
    edge_ref[4 * lanes :] = got_ref[slot(place, size)].astype(F32)[states : states + 2 * lanes]
    return jnp.concatenate([total, head, *last], axis=0)


def write(message, *refs):
    for ref in refs:
        rest = ref.shape[0] - message.shape[0]
        whole = jnp.concatenate([message, jnp.zeros((rest, LANES), F32)], axis=0) if rest else message
        ref[...] = whole.astype(BF16)


def first_scan(block, lanes, got_ref, rate_ref, taps_ref, before_ref, edge_ref, message_ref):
    @pl.when(lax.axis_index("ctx") // WIDE == 0)
    def _():
        write(near_scan(block, lanes, got_ref, rate_ref, taps_ref, before_ref, edge_ref, first_slot), message_ref)


def second_scan(block, lanes, got_ref, rate_ref, taps_ref, before_ref, edge_ref, message_ref):
    @pl.when(lax.axis_index("ctx") // WIDE == 1)
    def _():
        message_ref[...] = near_scan(block, lanes, got_ref, rate_ref, taps_ref, before_ref, edge_ref)


def relay(block, lanes, came_ref, own_ref, rate_ref, taps_ref, kept_ref, *message_refs):
    @pl.when(lax.axis_index("ctx") // WIDE == 1)
    def _():
        rates = rate_ref[...]
        state, last = jnp.zeros_like(rates), [jnp.zeros((lanes, LANES), F32)] * 2
        came = came_ref[...].astype(F32)
        kept_ref[...] = came
        for run in (came, own_ref[...]):
            state, last = step_over(block * WIDE, lanes, rates, taps_ref, state, last, run)
        write(jnp.concatenate([state, *last], axis=0), *message_refs)


def third_scan(block, lanes, got_ref, rate_ref, taps_ref, before_ref, edge_ref, *message_refs):
    @pl.when(lax.axis_index("ctx") // WIDE == 2)
    def _():
        write(near_scan(block, lanes, got_ref, rate_ref, taps_ref, before_ref, edge_ref), *message_refs)


def fourth_scan(block, lanes, got_ref, third_before, third_edge, third_message, rate_ref, taps_ref, before_ref, edge_ref, message_ref):
    group = lax.axis_index("ctx") // WIDE

    @pl.when(group == 2)
    def _():
        before_ref[...] = third_before[...]
        edge_ref[...] = third_edge[...]
        message_ref[...] = third_message[...]

    @pl.when(group == 3)
    def _():
        write(near_scan(block, lanes, got_ref, rate_ref, taps_ref, before_ref, edge_ref), message_ref)


def prepare(block, lanes, across_ref, cross_ref, next_ref, before_ref, edge_ref, rate_ref, taps_ref, residue_ref, rates_ref, weights_ref, rest_ref, decay_ref, head_ref, lead_ref, step_ref, fixed_ref):
    index = lax.axis_index("ctx")
    run, place = index // NEAR, index % NEAR
    states = rate_ref.shape[0]
    modes = states // lanes
    rates = rate_ref[...]
    across, cross, following = [r[: states + 4 * lanes].astype(F32) for r in (across_ref, cross_ref, next_ref)]
    start = jnp.where(run == 5, following, jnp.where(run == 6, across, cross))
    state, last = start[:states], pairs(start, states + 2 * lanes, lanes)
    for needed, message in ((run > 5, jnp.where(run == 6, cross, across)), (run > 6, following)):
        after, after_last = step_over(block * NEAR, lanes, rates, taps_ref, state, last, message)
        state, last = jnp.where(needed, after, state), [jnp.where(needed, a, b) for a, b in zip(after_last, last)]
    into, own_last = step_into(block, lanes, place, rates, taps_ref, state, last, edge_ref, before_ref)
    state = jnp.where(run > 4, into, before_ref[...])
    length = (block * (NEAR * (run - 4) + place)).astype(F32)
    away = length > 0
    own_head = pairs(edge_ref, 4 * lanes, lanes)
    first, second = first_products(taps_ref, own_last, own_head)
    ahead = jnp.exp(rates) * spread(second, modes)
    rest_ref[...] = state * jnp.exp(-rates) + jnp.where(away, spread(first, modes) + ahead, 0.0)
    for i in range(3):
        decay_ref[pl.ds(i * states, states)] = jnp.exp(-rates * (length + (1.0 - i)))
    head_ref[...] = jnp.where(run > 4, start[states : states + 2 * lanes], edge_ref[: 2 * lanes])
    ahead = jnp.where(away, ahead * residue_ref[...], 0.0)
    query = [q.astype(BF16).astype(F32) for q in first_rows(taps_ref, 0, own_last, own_head)]
    fix_rows(lanes, ahead, query, fixed_ref, 0)
    row = lax.broadcasted_iota(jnp.int32, (SUB, weights_ref.shape[1]), 0).astype(F32)
    step_ref[...] = jnp.exp(-SUB * rates_ref[...])
    for mode in range(modes):
        at = pl.ds(mode, 1)
        lead_ref[pl.ds(mode * SUB, SUB)] = weights_ref[at] * jnp.exp(-rates_ref[at] * row)


def fix_rows(lanes, ahead, query, out_ref, start):
    modes = ahead.shape[0] // lanes
    row = lax.broadcasted_iota(jnp.int32, (SUB, LANES), 0)
    for l in range(lanes):
        extra = jnp.sum(ahead[l * modes : (l + 1) * modes], axis=0, keepdims=True)
        take = jnp.where(row == 0, jnp.broadcast_to(extra, row.shape), 0.0)
        fixed = jnp.where(row == 0, query[0][l : l + 1], jnp.where(row == 1, query[1][l : l + 1], 0.0))
        out_ref[start : start + SUB, pl.ds(l * LANES, LANES)] = take
        out_ref[start + SUB : start + 2 * SUB, pl.ds(l * LANES, LANES)] = fixed


def add_mode(totals, term, rate):
    step = jnp.broadcast_to(jnp.exp(-SUB * rate), term.shape)
    out = []
    for total in totals:
        out.append(total + term)
        term = term * step
    return out


def inner_conv(rate_ref, residue_ref, product_ref, local_ref, filter_ref):
    count, chans = product_ref.shape
    modes = rate_ref.shape[0]
    blocks = count // SUB
    row = lax.broadcasted_iota(jnp.int32, (SUB, LANES), 0)
    lead = row.astype(F32)

    def one_lane(lane, carry):
        at = pl.ds(pl.multiple_of(lane * LANES, LANES), LANES)
        zero = jnp.zeros((SUB, LANES), F32)
        totals = [zero] * blocks
        for mode in range(modes):
            rate = rate_ref[pl.ds(mode, 1), at]
            term = residue_ref[pl.ds(mode, 1), at] * jnp.exp(-rate * lead)
            totals = add_mode(totals, term, rate)
        for i in range(blocks):
            filter_ref[pl.ds(i * SUB, SUB), :] = totals[i]

        shifted = [product_ref[pl.ds(i * SUB, SUB), at] for i in range(blocks)]
        totals = [zero] * blocks
        for b in range(SUB):
            for a in range(blocks):
                weight = filter_ref[pl.ds(a * SUB + b, 1), :]
                for j in range(blocks - a):
                    totals[j + a] = totals[j + a] + weight * shifted[j]
            if b < SUB - 1:
                rolled = [pltpu.roll(s, 1, 0) for s in shifted]
                shifted = [jnp.where(row == 0, before, now) for before, now in zip([zero] + rolled[:-1], rolled)]
        for i in range(blocks):
            local_ref[pl.ds(i * SUB, SUB), at] = totals[i]
        return carry

    lax.fori_loop(0, chans // LANES, one_lane, 0)


def finish(place, state, last, edge_ref, before_ref, rate_pack, residue_pack, taps_ref, rate_ref, query_ref, local_ref, mixed_ref, state_ref):
    count, chans = local_ref.shape
    lanes = chans // LANES
    modes = rate_ref.shape[0]
    states = lanes * modes
    blocks = count // SUB
    rates = rate_pack[...]
    state, own_last = step_into(count, lanes, place, rates, taps_ref, state, last, edge_ref, before_ref)
    own_head = pairs(edge_ref, 4 * lanes, lanes)
    own_query = [q.astype(BF16).astype(F32) for q in first_rows(taps_ref, 0, own_last, own_head)]
    first, second = first_products(taps_ref, own_last, own_head)
    ahead = jnp.exp(rates) * spread(second, modes)
    state = state * jnp.exp(-rates) + spread(first, modes) + ahead
    state = state * residue_pack[...]
    ahead = ahead * residue_pack[...]
    fix_rows(lanes, ahead, own_query, state_ref, modes)
    lead = lax.broadcasted_iota(jnp.int32, (SUB, LANES), 0).astype(F32)
    for l in range(lanes):
        state_ref[:modes, pl.ds(l * LANES, LANES)] = state[l * modes : (l + 1) * modes]

    def one_lane(lane, carry):
        at = pl.ds(pl.multiple_of(lane * LANES, LANES), LANES)
        totals = [local_ref[pl.ds(i * SUB, SUB), at] for i in range(blocks)]
        for mode in range(modes):
            rate = rate_ref[pl.ds(mode, 1), at]
            term = state_ref[pl.ds(mode, 1), at] * jnp.exp(-rate * lead)
            totals = add_mode(totals, term, rate)
        gate(totals, at, state_ref, modes, query_ref, mixed_ref)
        return carry

    lax.fori_loop(0, lanes, one_lane, 0)


def gate(totals, at, fixed_ref, start, query_ref, mixed_ref):
    totals[0] = totals[0] - fixed_ref[pl.ds(start, SUB), at]
    rows = lax.broadcasted_iota(jnp.int32, (2 * SUB, LANES), 0)
    for i in range(0, len(totals), 2):
        where = pl.ds(i * SUB, 2 * SUB)
        conv = jnp.concatenate(totals[i : i + 2], axis=0).astype(BF16).astype(F32)
        query = query_ref[where, at].astype(F32)
        if i == 0:
            fixed = fixed_ref[pl.ds(start + SUB, SUB), at]
            query = jnp.where(rows < 2, jnp.concatenate([fixed, fixed], axis=0), query)
        mixed_ref[where, at] = (query * conv).astype(BF16)


def leave(mixed_ref, out_ref, sem):
    copy = pltpu.make_async_copy(mixed_ref, out_ref, sem)
    copy.start()
    copy.wait()


def convolves_early():
    index = lax.axis_index("ctx")
    return index < WIDE + WIDE // 2


def early_inner(rate_ref, residue_ref, product_ref, after_ref, local_ref, filter_ref):
    @pl.when(convolves_early())
    def _():
        inner_conv(rate_ref, residue_ref, product_ref, local_ref, filter_ref)


def lower_output(first_before, first_edge, second_before, second_edge, rate_pack, residue_pack, taps_ref, rate_ref, query_ref, residue_ref, product_ref, held_ref, low_ref, out_ref, filter_ref, local_ref, state_ref, mixed_ref, sem):
    early = convolves_early()

    @pl.when(early)
    def _():
        local_ref[...] = held_ref[...]

    @pl.when(jnp.logical_not(early))
    def _():
        inner_conv(rate_ref, residue_ref, product_ref, local_ref, filter_ref)

    index = lax.axis_index("ctx")
    rates = rate_pack[...]
    second = index >= WIDE
    state, last = jnp.zeros_like(rates), [jnp.zeros((taps_ref.shape[0] // 9, LANES), F32)] * 2
    after, after_last = step_over(local_ref.shape[0] * WIDE, len(last[0]), rates, taps_ref, state, last, low_ref[...])
    state, last = jnp.where(second, after, state), [jnp.where(second, a, b) for a, b in zip(after_last, last)]
    before = jnp.where(second, second_before[...], first_before[...])
    edges = jnp.where(second, second_edge[...], first_edge[...])
    finish(index % WIDE, state, last, edges, before, rate_pack, residue_pack, taps_ref, rate_ref, query_ref, local_ref, mixed_ref, state_ref)
    leave(mixed_ref, out_ref, sem)


def upper_output(rest_ref, decay_ref, head_ref, lead_ref, step_ref, fixed_ref, residue_ref, rate_ref, taps_ref, query_ref, local_ref, third_ref, fourth_ref, held_ref, out_ref, state_ref, mixed_ref, sem):
    index = lax.axis_index("ctx")
    states = rest_ref.shape[0]
    lanes = taps_ref.shape[0] // 9
    modes = states // lanes
    blocks = local_ref.shape[0] // SUB

    @pl.when(index >= 2 * WIDE)
    def _():
        came = third_ref[...].astype(F32) + fourth_ref[: states + 4 * lanes].astype(F32)
        last = pairs(came, states, lanes)
        head = pairs(head_ref, 0, lanes)
        first, second = first_products(taps_ref, last, head)
        ahead = spread(second, modes)
        state = rest_ref[...] + came[:states] * decay_ref[:states]
        state = state + spread(first, modes) * decay_ref[states : 2 * states] + ahead * decay_ref[2 * states :]
        for l in range(lanes):
            state_ref[:modes, pl.ds(l * LANES, LANES)] = state[l * modes : (l + 1) * modes]
        state_ref[modes:] = fixed_ref[...]

        @pl.when(index == 2 * WIDE)
        def _():
            query = [q.astype(BF16).astype(F32) for q in first_rows(taps_ref, 0, last, head)]
            fix_rows(lanes, jnp.exp(rate_ref[...]) * ahead * residue_ref[...], query, state_ref, modes)

        def one_lane(lane, carry):
            at = pl.ds(pl.multiple_of(lane * LANES, LANES), LANES)
            totals = [local_ref[pl.ds(i * SUB, SUB), at] for i in range(blocks)]
            for mode in range(modes):
                step = jnp.broadcast_to(step_ref[pl.ds(mode, 1), at], (SUB, LANES))
                term = state_ref[pl.ds(mode, 1), at] * lead_ref[pl.ds(mode * SUB, SUB), at]
                for i in range(blocks):
                    totals[i] = totals[i] + term
                    if i < blocks - 1:
                        term = term * step
            gate(totals, at, state_ref, modes, query_ref, mixed_ref)
            pltpu.make_async_copy(mixed_ref.at[:, at], out_ref.at[:, at], sem.at[lane]).start()
            return carry

        lax.fori_loop(0, lanes, one_lane, 0, unroll=True)
        for l in range(lanes):
            at = pl.ds(l * LANES, LANES)
            pltpu.make_async_copy(mixed_ref.at[:, at], out_ref.at[:, at], sem.at[l]).wait()


def gather(copies, axis, groups=None):
    return lax.all_to_all(copies, axis, 0, 0, tiled=True, axis_index_groups=groups)


def per_device(stream, norm_gain, short_filter, decay_rate, residue):
    count, chans = stream.shape
    modes = decay_rate.shape[1]
    lanes = chans // LANES
    states = lanes * modes
    peers = lax.axis_size("ch")
    ctx = lax.axis_size("ctx")
    groups = [[g + m for m in range(WIDE)] for g in range(0, ctx, WIDE)]
    runs = [[g + m for m in range(NEAR)] for g in range(0, ctx, NEAR)]
    index, stream = lax.optimization_barrier((lax.axis_index("ctx"), stream))
    held = [stream, norm_gain[None, :], short_filter, decay_rate.T, residue.T]
    held = [pltpu.with_memory_space_constraint(h, pltpu.HBM) for h in held]
    stream, gain, taps, rates, weights, sums, taps_pack, rate_pack, residue_pack = call(
        square_sums,
        [(h.shape, h.dtype) for h in held]
        + [((peers, 1, count), F32), ((9 * lanes, LANES), F32), ((states, LANES), F32), ((states, LANES), F32)],
        *held,
        scratch=[pltpu.SemaphoreType.DMA((lanes + len(held) - 1,))],
        space=pltpu.HBM,
    )
    sums = lax.cond(index < ctx, lambda c: gather(c, "ch", [list(range(peers))[::-1]]), lambda c: c, sums)
    query, product, wide, near = call(
        lambda *refs: block_states(chans * peers, *refs),
        [((count, chans), BF16), ((count, chans), F32), ((WIDE, states + 4 * lanes, LANES), BF16), ((NEAR, states + 4 * lanes, LANES), BF16)],
        sums, stream, gain, taps, rates,
        scratch=[pltpu.VMEM((SUB, chans), F32), pltpu.VMEM((modes, chans), F32), pltpu.VMEM((states + 4 * lanes, LANES), F32)],
    )
    index, wide, near = lax.optimization_barrier((index, wide, near))
    group = lax.shift_right_logical(index, WIDE.bit_length() - 1)
    small, large = ((states + 4 * lanes, LANES), BF16), ((states + 8 * lanes, LANES), BF16)
    kept = [((states, LANES), F32), ((6 * lanes, LANES), F32)]
    nothing = lambda *shapes: tuple(call(lambda *refs: None, shapes, out_any=range(len(shapes))))
    hops = lambda *ends: [pair for a, b in ends for pair in zip(a, b)]
    first, second, third, fourth = groups
    scan = lambda body, outs, *args: call(
        lambda *refs: body(count, lanes, *refs), [*kept, *outs], *args, rate_pack, taps_pack
    )

    def gather_in(number, copies, members):
        size = len(members[0])
        put = slot if number else first_slot
        order = sorted(range(size), key=lambda j: put(j, size))
        members = [[g[j] for j in order] for g in members]
        return lax.cond(
            group == number, lambda c: gather(c, "ctx", members), lambda c: nothing((c.shape, c.dtype))[0], copies
        )

    def inner():
        return call(
            inner_conv, [((count, chans), F32)], rates, weights, product, scratch=[pltpu.VMEM((count, LANES), F32)], flops=10**7
        )[0]

    room = [pltpu.VMEM((count, LANES), F32)]
    work = [pltpu.VMEM((modes + 2 * SUB, chans), F32), pltpu.VMEM((count, chans), BF16), pltpu.SemaphoreType.DMA]
    whole = (small[0], F32)
    held, result = ((count, chans), F32), ((count, chans), BF16)

    def lower(copies):
        *first_kept, message = scan(first_scan, [small], gather_in(0, copies, groups))
        low = lax.ppermute(message, "ctx", hops((first, second)))
        (local,) = call(early_inner, [held], rates, weights, product, message, scratch=room, flops=10**7)
        copies, local = lax.optimization_barrier((copies, local))
        *second_kept, message = scan(second_scan, [whole], gather_in(1, copies, groups))
        onward = call(lambda *refs: relay(count, lanes, *refs), [whole, small, large], low, message, rate_pack, taps_pack)
        return *first_kept, *second_kept, local, *onward

    *lower_kept, to_third, to_fourth = lax.cond(
        group < 2, lower, lambda c: nothing(*kept, *kept, held, whole, small, large), wide
    )
    half = WIDE // 2
    quarter = WIDE // 4
    turned = fourth[half:] + fourth[quarter:half] + fourth[:quarter]
    to_fourth = lax.ppermute(to_fourth, "ctx", hops((second, turned)))
    to_third = lax.ppermute(to_third, "ctx", hops((second, third)))

    prepared = [
        ((states, LANES), F32), ((3 * states, LANES), F32), ((2 * lanes, LANES), F32),
        ((modes * SUB, chans), F32), ((modes, chans), F32), ((2 * SUB, chans), F32),
    ]

    def upper(copies):
        *own, message, first_message = scan(third_scan, [small, large], gather_in(2, copies, runs))
        across = lax.ppermute(first_message, "ctx", hops((runs[4], runs[6]), (runs[5], runs[7])))
        cross = lax.ppermute(first_message, "ctx", hops((runs[4], runs[7]), (runs[5], runs[6])))
        *own, message = scan(fourth_scan, [small], gather_in(3, copies, runs), *own, message)
        following = lax.ppermute(message, "ctx", hops((runs[4], runs[5]), (runs[6], runs[7])))
        ready = call(
            lambda *refs: prepare(count, lanes, *refs),
            prepared,
            across, cross, following, *own, rate_pack, taps_pack, residue_pack, rates, weights,
        )
        return *call(lambda *refs: None, [result], out_hbm=(0,)), inner(), *ready

    def rest(copies):
        common = [rate_pack, residue_pack, taps_pack, rates, query, weights, product]
        (mixed,) = call(
            lower_output, [result], *lower_kept[:4], *common, *lower_kept[4:], scratch=room + [pltpu.VMEM(*held)] + work, out_hbm=(0,)
        )
        return mixed, *nothing(held, *prepared)

    mixed, local, *ready = lax.cond(group >= 2, upper, rest, near)
    (mixed,) = call(
        upper_output,
        [result],
        *ready, residue_pack, rate_pack, taps_pack, query, local, to_third, to_fourth, mixed,
        scratch=work[:2] + [pltpu.SemaphoreType.DMA((lanes,))], in_hbm=(13,), out_hbm=(0,), aliases={13: 0},
    )
    return mixed


def solution(mesh):
    in_specs = (P("ctx", "ch"), P("ch"), P(None, None, "ch"), P("ch", None), P("ch", None))
    out_specs = P("ctx", "ch")
    return jax.shard_map(
        per_device, mesh=mesh, in_specs=in_specs, out_specs=out_specs, check_vma=False
    )
```
